128 devices in a mesh: chan: 16 (over x, y_hi, core), band: 8 (over y_lo, z).
Axes of the slice: x: 4, y: 4 (y_hi: 2, y_lo: 2; y = y_hi * 2 + y_lo), z: 4, core: 2. Of those that a mesh axis runs over, the one named last changes fastest.
Arguments:
- strain: float32 [2048, 34816], P(('chan', 'band')), may hold values from -100 to 100
- source_block: int32 [1], replicated, may hold values from 0 to 15
- source_offset: int32 [1], replicated, may hold values from 0 to 127
- window_valid: int32 [16], replicated, may hold values 0 or 1
Outputs:
- correlation: bfloat16 [128, 256, 2048], P('band', None, 'chan')
The draws below stay inside these ranges and needn't reach their ends.
All inputs are finite; a program needn't handle non-finite values.
Results may differ from the reference program's by a relative error of at most 0.008.
Values may be sent and summed in bfloat16 or wider, within the bound.
A program may use at most 192 MiB of HBM per device.

```python
import math
import jax
import jax.numpy as jnp
from jax import lax

L = 4096
HOP = 2048
NF = 2048
W = 16
CH_DEV = 128
SRC_BLOCK = 128
NSB = 1
LAGS = 256
CH = 2048
FB = 256
S = 128
SAMPLES = 34816
NBLK = 16
N_BAND = 8


def draw_strain(key, part):
    key = jax.random.fold_in(key, 7)
    keys = jax.random.split(key, 3)
    gains = jnp.exp(jax.random.uniform(keys[0], (CH, 1), jnp.float32, 0.0, math.log(10.0)))
    pieces = (W + 1) * 4
    envelope = jnp.exp(jax.random.uniform(keys[1], (1, pieces), jnp.float32, math.log(0.5), math.log(2.0)))
    envelope = jnp.repeat(envelope, SAMPLES // pieces, axis=1)
    noise = jnp.clip(jax.random.normal(keys[2], (CH, SAMPLES), jnp.float32), -4.0, 4.0)
    values = noise * gains * envelope
    return values.astype(jnp.float32)


def with_ends(array, key, least, top_value):
    longest = array.shape.index(max(array.shape))
    spots = []
    for shift in (0, 1):
        where = [jax.random.randint(jax.random.fold_in(key, axis), (), 0, length) for axis, length in enumerate(array.shape)]
        where[longest] = (where[longest] + shift) % array.shape[longest]
        spots.append(tuple(where))
    return array.at[spots[0]].set(least).at[spots[1]].set(top_value)


def setup_inputs(seed: int = 0) -> dict:
    key_of = jax.random.split(jax.random.key(seed), 5)
    strain = draw_strain(jax.random.fold_in(key_of[4], 71), 0)
    source_block = jax.random.randint(key_of[1], (NSB,), 0, NBLK).astype(jnp.int32)
    source_offset = jax.random.randint(key_of[2], (NSB,), 0, SRC_BLOCK).astype(jnp.int32)
    window_valid = with_ends((jax.random.randint(key_of[3], (W,), 0, 4) < 3).astype(jnp.int32), jax.random.fold_in(key_of[3], 1), 0, 1)
    return dict(strain=strain, source_block=source_block, source_offset=source_offset, window_valid=window_valid)


def angle_table(points, bins):
    phase = points[:, None] * bins[None, :] % L
    angle = phase.astype(jnp.float32) * (2.0 * math.pi / L)
    return (jnp.cos(angle), -jnp.sin(angle))

def banded_table(points, first_bin, band_count, band_bins):
    bins = first_bin + jnp.arange(band_count * band_bins, dtype=jnp.int32)
    cosine, sine = angle_table(points, bins)
    shaped = (points.shape[0], band_count, 1, band_bins)
    stacked = jnp.concatenate([cosine.reshape(shaped), sine.reshape(shaped)], axis=2)
    return stacked.reshape(points.shape[0], 2 * band_count * band_bins).astype(jnp.bfloat16)

def taper(strain):
    channels = strain.shape[0]
    halves = strain.reshape(channels, W + 1, HOP)
    segments = jnp.concatenate([halves[:, :-1], halves[:, 1:]], axis=2)
    centred = segments - lax.optimization_barrier(jnp.mean(segments, axis=2, keepdims=True))
    points = jnp.arange(L, dtype=jnp.float32)
    hann = 0.5 - 0.5 * jnp.cos(points * (2.0 * math.pi / L))
    return (centred * hann).astype(jnp.bfloat16)

def whiten(spectra):
    band_bins = spectra.shape[-1]
    power = lax.optimization_barrier(jnp.sum(spectra * spectra, axis=(-2, -1), keepdims=True)) / band_bins
    return (spectra / jnp.sqrt(power + 1e-06)).astype(jnp.bfloat16)

def product(form, left, right):
    return jnp.einsum(form, left.astype(jnp.float32), right.astype(jnp.float32), precision=lax.Precision.HIGHEST)

def cross_lags(block_src, spectra, lag_table, factor):
    real_src = block_src[:, :, :, 0]
    imag_src = block_src[:, :, :, 1]
    real_rec = spectra[:, :, :, 0]
    imag_rec = spectra[:, :, :, 1]
    form = 'swbf,cwbf->bfsc'
    cross_real = product(form, real_src, real_rec) + product(form, imag_src, imag_rec)
    cross_imag = product(form, real_src, imag_rec) - product(form, imag_src, real_rec)
    cross = jnp.stack([cross_real, cross_imag], axis=1)
    cross = (cross.reshape(-1, block_src.shape[0], spectra.shape[0]) * factor).astype(jnp.bfloat16)
    return product('tq,qsc->stc', lag_table, cross)

def reference(strain, source_block, source_offset, window_valid):
    tapered = taper(strain)
    points = jnp.arange(L, dtype=jnp.int32)
    basis = banded_table(points, 0, N_BAND, FB)
    spectra = jnp.dot(tapered.reshape(CH * W, L), basis, preferred_element_type=jnp.float32)
    white = whiten(spectra.reshape(CH, W, N_BAND, 2, FB))
    offsets = jnp.arange(SRC_BLOCK, dtype=jnp.int32)
    chosen = ((source_block[:, None] * SRC_BLOCK + source_offset[:, None] + offsets[None, :]) % CH).reshape(-1)
    sources = jnp.take(white, chosen.astype(jnp.int32), axis=0)
    valid = window_valid.astype(jnp.bfloat16)
    masked = sources * valid[None, :, None, None, None]
    factor = jnp.float32(1.0 / (W * math.sqrt(NF)))
    lags = jnp.arange(LAGS, dtype=jnp.int32) - LAGS // 2
    lag_table = banded_table(lags, 0, N_BAND, FB)
    blocks = white.reshape(CH // CH_DEV, CH_DEV, W, N_BAND, 2, FB)

    def one_block(block):
        return cross_lags(masked, block, lag_table, factor).astype(jnp.bfloat16)
    result = lax.map(one_block, blocks)
    return jnp.transpose(result, (1, 2, 0, 3)).reshape(S, LAGS, CH)
```

```python
import functools
import math

import jax
import jax.numpy as jnp
import numpy as np
from jax import lax
from jax.experimental import pallas as pl
from jax.experimental.pallas import tpu as pltpu
from jax.sharding import PartitionSpec as P

L = 4096
HOP = 2048
NF = 2048
W = 16
SRC_BLOCK = 128
LAGS = 256
R1 = 32
R2 = 128
HALF = R2 // 2
BINS = 8
FACTOR = 1.0 / (W * math.sqrt(NF))


def window_table():
    points = np.arange(L, dtype=np.float32)
    angle = (points * np.float32(2.0 * math.pi / L)).astype(np.float32)
    return (np.float32(0.5) - np.float32(0.5) * np.cos(angle)).astype(np.float32).reshape(R1, R2)


def twiddle_tables():
    angle = 2.0 * np.pi * np.outer(np.arange(R1), np.arange(R2)) / L
    return np.cos(angle).astype(np.float32), (-np.sin(angle)).astype(np.float32)


def short_dft():
    angle = 2.0 * np.pi * (np.outer(np.arange(HALF), np.arange(R2)) % R2) / R2
    cosine, sine = np.cos(angle), np.sin(angle)
    top = np.concatenate([cosine, sine], axis=1)
    low = np.concatenate([-sine, cosine], axis=1)
    return np.concatenate([top, low], axis=0).astype(np.float32)


def lag_table():
    f1 = np.arange(R1)[:, None, None]
    m = np.arange(4)[None, :, None]
    i = np.arange(16)[None, None, :]
    bins = f1 + R1 * (16 * m + i)
    lags = np.arange(LAGS) - LAGS // 2
    angle = 2.0 * np.pi * ((lags[:, None, None, None] * bins[None]) % L) / L
    table = np.stack([np.cos(angle), -np.sin(angle)], axis=3)
    return table.reshape(LAGS, 2 * NF).astype(np.float32)


def real_dft(x):
    n = len(x)
    if n == 2:
        return [(x[0] + x[1], None), (x[0] - x[1], None)]
    even, odd = real_dft(x[0::2]), real_dft(x[1::2])
    out = [None] * (n // 2 + 1)
    for k in range(n // 4 + 1):
        er, ei = even[k]
        orr, oi = odd[k]
        if k == 0:
            out[0] = (er + orr, None)
            out[n // 2] = (er - orr, None)
            continue
        if 4 * k == n:
            out[k] = (er, -orr)
            continue
        c, s = math.cos(2 * math.pi * k / n), -math.sin(2 * math.pi * k / n)
        if oi is None:
            tr, ti = orr * c, orr * s
        else:
            tr, ti = orr * c - oi * s, orr * s + oi * c
        zi = ti if ei is None else ei + ti
        yi = -ti if ei is None else ei - ti
        out[k] = (er + tr, zi)
        out[n // 2 - k] = (er - tr, -yi)
    return out


def spectra_kernel(strain, hann, tw_cos, tw_sin, dft, mask, white, masked, rows, folded, spectra):
    channels = strain.shape[0]
    pieces = HOP // R2
    for h in range(W + 1):
        for k in range(pieces):
            piece = strain[:, h * HOP + k * R2:h * HOP + (k + 1) * R2]
            if h < W:
                rows[k, pl.ds(h, channels, stride=W), :] = piece
            if h > 0:
                rows[pieces + k, pl.ds(h - 1, channels, stride=W), :] = piece

    def fold(step, _):
        at = pl.ds(pl.multiple_of(step * 16, 16), 16)
        x = [rows[k, at, :] for k in range(R1)]
        total = x[0]
        for k in range(1, R1):
            total = total + x[k]
        mean = jnp.sum(total, axis=1, keepdims=True) * (1.0 / L)
        x = [((x[k] - mean) * hann[k:k + 1, :]).astype(jnp.bfloat16).astype(jnp.float32) for k in range(R1)]
        bins = real_dft(x)
        for f in range(R1):
            re, im = bins[f] if f <= R1 // 2 else bins[R1 - f]
            if im is None:
                gr, gi = re * tw_cos[f:f + 1, :], re * tw_sin[f:f + 1, :]
            else:
                im = im if f <= R1 // 2 else -im
                c, s = tw_cos[f:f + 1, :], tw_sin[f:f + 1, :]
                gr, gi = re * c - im * s, re * s + im * c
            folded[f, at, :] = jnp.concatenate([gr, gi], axis=1).astype(jnp.bfloat16)
        return 0

    lax.fori_loop(0, channels * W // 16, fold, 0)
    table = dft[...]

    def transform(f, power):
        y = lax.dot_general(table, folded[f], (((1,), (1,)), ((), ())), preferred_element_type=jnp.float32)
        spectra[f] = y
        return power + y * y

    power = lax.fori_loop(0, R1, transform, jnp.zeros((R2, channels * W), jnp.float32))
    scales = []
    for b in range(HALF // BINS):
        both = power[b * BINS:(b + 1) * BINS] + power[HALF + b * BINS:HALF + (b + 1) * BINS]
        total = jnp.sum(both, axis=0, keepdims=True) * (1.0 / 256.0)
        scales.append(jnp.broadcast_to(lax.rsqrt(total + 1e-06), both.shape))
    scale = jnp.concatenate(scales + scales, axis=0)
    keep = mask[...]

    def finish(f, _):
        value = (spectra[f] * scale).astype(jnp.bfloat16)
        white[f] = value
        masked[f] = (value.astype(jnp.float32) * keep).astype(jnp.bfloat16)
        return 0

    lax.fori_loop(0, R1, finish, 0)


def whiten(strain, mask):
    channels = strain.shape[0]
    lanes = channels * W
    tw_cos, tw_sin = twiddle_tables()
    shape = jax.ShapeDtypeStruct((R1, R2, lanes), jnp.bfloat16)
    return pl.pallas_call(
        spectra_kernel,
        out_shape=(shape, shape),
        scratch_shapes=[
            pltpu.VMEM((R1, lanes, R2), jnp.float32),
            pltpu.VMEM((R1, lanes, 2 * R2), jnp.bfloat16),
            pltpu.VMEM((R1, R2, lanes), jnp.float32),
        ],
        compiler_params=pltpu.CompilerParams(vmem_limit_bytes=48 * 2**20),
        cost_estimate=pl.CostEstimate(flops=2 * 32 * 128 * 256 * 256, bytes_accessed=8 * 2**20, transcendentals=0),
    )(strain, jnp.asarray(window_table()), jnp.asarray(tw_cos), jnp.asarray(tw_sin),
      jnp.asarray(short_dft(), dtype=jnp.bfloat16), mask)


CHUNK = 4


def lag_kernel(white, sources, table, out, total, cross):
    step = pl.program_id(0)
    row = lax.broadcasted_iota(jnp.int32, (BINS, R2), 0)
    lane = lax.broadcasted_iota(jnp.int32, (BINS, R2), 1)
    own = lane // W == row
    channels = white.shape[2] // W

    def slanted(x):
        return [pltpu.roll(x[:, k * R2:(k + 1) * R2], 0, 1, stride=W, stride_axis=0) for k in range(channels // 8)]

    def spread(x, c):
        part = x[c // 8]
        rolled = pltpu.roll(part, R2 - W * (c % 8), 1) if c % 8 else part
        return jnp.where(own, rolled, 0.0)

    def pair(index, _):
        f, m = index // 4, index % 4
        re = white[f, pl.ds(pl.multiple_of(m * 16, 16), 16), :].astype(jnp.float32)
        im = white[f, pl.ds(pl.multiple_of(HALF + m * 16, 16), 16), :].astype(jnp.float32)
        results = []
        for g in range(2):
            xr, xi = slanted(re[g * 8:(g + 1) * 8]), slanted(im[g * 8:(g + 1) * 8])
            left = jnp.concatenate(
                [jnp.concatenate([spread(xr, c), spread(xi, c)], axis=1) for c in range(channels)], axis=0
            ).astype(jnp.bfloat16)
            s = sources[index * 2 + g]
            sr, si = s[:R2], s[R2:]
            right = jnp.concatenate([s, jnp.concatenate([-si, sr], axis=0)], axis=1)
            results.append(jnp.dot(left, right, preferred_element_type=jnp.float32) * FACTOR)
        base = pl.multiple_of(index * 32, 32)
        for c in range(channels):
            both = jnp.concatenate([r[c * 8:(c + 1) * 8] for r in results], axis=0).astype(jnp.bfloat16)
            cross[pl.ds(base, 16), c * SRC_BLOCK:(c + 1) * SRC_BLOCK] = both[:, :SRC_BLOCK]
            cross[pl.ds(base + 16, 16), c * SRC_BLOCK:(c + 1) * SRC_BLOCK] = both[:, SRC_BLOCK:]
        return 0

    lax.fori_loop(0, CHUNK * 4, pair, 0)
    part = table[...]
    width = 256

    @pl.when(step == 0)
    def _():
        total[...] = jnp.zeros_like(total)

    def columns(n, _):
        at = pl.ds(pl.multiple_of(n * width, width), width)
        total[:, at] += jnp.dot(part, cross[:, at], preferred_element_type=jnp.float32)
        return 0

    lax.fori_loop(0, total.shape[1] // width, columns, 0)

    @pl.when(step == pl.num_programs(0) - 1)
    def _():
        out[...] = total[...].astype(out.dtype)


def correlate(white, sources):
    channels = white.shape[2] // W
    columns = channels * SRC_BLOCK
    depth = CHUNK * R2
    return pl.pallas_call(
        lag_kernel,
        grid=(R1 // CHUNK,),
        in_specs=[
            pl.BlockSpec((CHUNK, R2, channels * W), lambda i: (i, 0, 0)),
            pl.BlockSpec((CHUNK * 8, 2 * R2, SRC_BLOCK), lambda i: (i, 0, 0)),
            pl.BlockSpec((LAGS, depth), lambda i: (0, i)),
        ],
        out_specs=pl.BlockSpec((LAGS, columns), lambda i: (0, 0)),
        out_shape=jax.ShapeDtypeStruct((LAGS, columns), jnp.bfloat16),
        scratch_shapes=[
            pltpu.VMEM((LAGS, columns), jnp.float32),
            pltpu.VMEM((depth, columns), jnp.bfloat16),
        ],
        compiler_params=pltpu.CompilerParams(vmem_limit_bytes=48 * 2**20),
        cost_estimate=pl.CostEstimate(flops=2 * 256 * 4096 * 2048, bytes_accessed=20 * 2**20, transcendentals=0),
    )(white, sources, jnp.asarray(lag_table(), dtype=jnp.bfloat16))


def body(strain, source_block, source_offset, window_valid):
    own_rows = strain.shape[0]
    bands = lax.axis_size("band")
    chans = lax.axis_size("chan")
    block, offset = source_block[0], source_offset[0]
    row = lax.axis_index("band") * own_rows + jnp.arange(own_rows, dtype=jnp.int32)
    chan = lax.axis_index("chan")
    held = ((chan == block) & (row >= offset)) | ((chan == (block + 1) % chans) & (row < offset))
    mask = (held[:, None] & (window_valid != 0)[None, :]).astype(jnp.float32).reshape(1, own_rows * W)
    white, masked = whiten(strain, mask)

    per = R1 // chans
    parts = lax.all_to_all(masked, "chan", split_axis=0, concat_axis=0, tiled=True)
    piece = jnp.sum(parts.reshape(chans, per, R2, own_rows * W).astype(jnp.float32), axis=0).astype(jnp.bfloat16)
    piece = piece.reshape(per, 2, 4, 16, own_rows * W).transpose(0, 2, 1, 3, 4).reshape(bands, 2, 16, own_rows * W)
    piece = lax.all_to_all(piece, "band", split_axis=0, concat_axis=0, tiled=True)
    piece = piece.reshape(bands, 2, 2, BINS, own_rows, W).transpose(2, 1, 3, 5, 0, 4)
    piece = jnp.roll(piece.reshape(2, 2 * BINS * W, SRC_BLOCK), -offset, axis=2)
    sources = lax.all_gather(piece, ("chan", "band"), axis=0, tiled=True)

    total = correlate(white, sources)
    total = total.reshape(LAGS, own_rows, bands, SRC_BLOCK // bands).transpose(2, 3, 0, 1)
    total = lax.all_to_all(total, "band", split_axis=0, concat_axis=0, tiled=False)
    return total.transpose(1, 2, 0, 3).reshape(SRC_BLOCK // bands, LAGS, bands * own_rows)


def solution(mesh):
    in_specs = (P(("chan", "band"), None), P(), P(), P())
    out_specs = P("band", None, "chan")
    return jax.shard_map(body, mesh=mesh, in_specs=in_specs, out_specs=out_specs, check_vma=False)
```

```python
import functools
import math

import jax
import jax.numpy as jnp
import numpy as np
from jax import lax
from jax.experimental import pallas as pl
from jax.experimental.pallas import tpu as pltpu
from jax.sharding import PartitionSpec as P

L = 4096
HOP = 2048
NF = 2048
W = 16
SRC_BLOCK = 128
LAGS = 256
R1 = 32
R2 = 128
HALF = R2 // 2
BINS = 8
FACTOR = 1.0 / (W * math.sqrt(NF))


def window_table():
    points = np.arange(L, dtype=np.float32)
    angle = (points * np.float32(2.0 * math.pi / L)).astype(np.float32)
    return (np.float32(0.5) - np.float32(0.5) * np.cos(angle)).astype(np.float32).reshape(R1, R2)


def twiddle_tables():
    angle = 2.0 * np.pi * np.outer(np.arange(R1), np.arange(R2)) / L
    return np.cos(angle).astype(np.float32), (-np.sin(angle)).astype(np.float32)


def short_dft():
    angle = 2.0 * np.pi * (np.outer(np.arange(HALF), np.arange(R2)) % R2) / R2
    cosine, sine = np.cos(angle), np.sin(angle)
    top = np.concatenate([cosine, sine], axis=1)
    low = np.concatenate([-sine, cosine], axis=1)
    return np.concatenate([top, low], axis=0).astype(np.float32)


def lag_table():
    core, g, x, y_hi, y_lo, z_hi, z_lo, i = np.ix_(*[np.arange(n) for n in (2, 2, 4, 2, 2, 2, 2, 8)])
    bins = 8 * x + 4 * y_hi + 2 * core + y_lo + R1 * (16 * (2 * z_hi + z_lo) + 8 * g + i)
    lags = (np.arange(LAGS) - LAGS // 2).reshape((1, LAGS) + (1,) * 7)
    angle = 2.0 * np.pi * (lags * bins[:, None] % L) / L
    table = np.stack([np.cos(angle), -np.sin(angle)], axis=7)
    return table.reshape(2, LAGS, NF).astype(np.float32)


def real_dft(x):
    n = len(x)
    if n == 2:
        return [(x[0] + x[1], None), (x[0] - x[1], None)]
    even, odd = real_dft(x[0::2]), real_dft(x[1::2])
    out = [None] * (n // 2 + 1)
    for k in range(n // 4 + 1):
        er, ei = even[k]
        orr, oi = odd[k]
        if k == 0:
            out[0] = (er + orr, None)
            out[n // 2] = (er - orr, None)
            continue
        if 4 * k == n:
            out[k] = (er, -orr)
            continue
        c, s = math.cos(2 * math.pi * k / n), -math.sin(2 * math.pi * k / n)
        if oi is None:
            tr, ti = orr * c, orr * s
        else:
            tr, ti = orr * c - oi * s, orr * s + oi * c
        zi = ti if ei is None else ei + ti
        yi = -ti if ei is None else ei - ti
        out[k] = (er + tr, zi)
        out[n // 2 - k] = (er - tr, -yi)
    return out


def spectra_kernel(strain, hann, tw_cos, tw_sin, dft, mask, white, masked, rows, folded, spectra):
    channels = strain.shape[0]
    pieces = HOP // R2
    for h in range(W + 1):
        for k in range(pieces):
            piece = strain[:, h * HOP + k * R2:h * HOP + (k + 1) * R2]
            if h < W:
                rows[k, pl.ds(h, channels, stride=W), :] = piece
            if h > 0:
                rows[pieces + k, pl.ds(h - 1, channels, stride=W), :] = piece

    def fold(step, _):
        at = pl.ds(pl.multiple_of(step * 16, 16), 16)
        x = [rows[k, at, :] for k in range(R1)]
        total = x[0]
        for k in range(1, R1):
            total = total + x[k]
        mean = jnp.sum(total, axis=1, keepdims=True) * (1.0 / L)
        x = [((x[k] - mean) * hann[k:k + 1, :]).astype(jnp.bfloat16).astype(jnp.float32) for k in range(R1)]
        bins = real_dft(x)
        for f in range(R1):
            re, im = bins[f] if f <= R1 // 2 else bins[R1 - f]
            if im is None:
                gr, gi = re * tw_cos[f:f + 1, :], re * tw_sin[f:f + 1, :]
            else:
                im = im if f <= R1 // 2 else -im
                c, s = tw_cos[f:f + 1, :], tw_sin[f:f + 1, :]
                gr, gi = re * c - im * s, re * s + im * c
            folded[f, at, :] = jnp.concatenate([gr, gi], axis=1).astype(jnp.bfloat16)
        return 0

    lax.fori_loop(0, channels * W // 16, fold, 0)
    table = dft[...]

    def transform(f, power):
        y = lax.dot_general(table, folded[f], (((1,), (1,)), ((), ())), preferred_element_type=jnp.float32)
        spectra[f] = y
        return power + y * y

    power = lax.fori_loop(0, R1, transform, jnp.zeros((R2, channels * W), jnp.float32))
    scales = []
    for b in range(HALF // BINS):
        both = power[b * BINS:(b + 1) * BINS] + power[HALF + b * BINS:HALF + (b + 1) * BINS]
        total = jnp.sum(both, axis=0, keepdims=True) * (1.0 / 256.0)
        scales.append(jnp.broadcast_to(lax.rsqrt(total + 1e-06), both.shape))
    scale = jnp.concatenate(scales + scales, axis=0)
    keep = mask[...]

    def finish(f, _):
        value = (spectra[f] * scale).astype(jnp.bfloat16)
        white[f] = value
        masked[f] = (value.astype(jnp.float32) * keep).astype(jnp.bfloat16)
        return 0

    lax.fori_loop(0, R1, finish, 0)


def whiten(strain, mask):
    channels = strain.shape[0]
    lanes = channels * W
    tw_cos, tw_sin = twiddle_tables()
    shape = jax.ShapeDtypeStruct((R1, R2, lanes), jnp.bfloat16)
    return pl.pallas_call(
        spectra_kernel,
        out_shape=(shape, shape),
        scratch_shapes=[
            pltpu.VMEM((R1, lanes, R2), jnp.float32),
            pltpu.VMEM((R1, lanes, 2 * R2), jnp.bfloat16),
            pltpu.VMEM((R1, R2, lanes), jnp.float32),
        ],
        compiler_params=pltpu.CompilerParams(vmem_limit_bytes=48 * 2**20),
        cost_estimate=pl.CostEstimate(flops=2 * 32 * 128 * 256 * 256, bytes_accessed=8 * 2**20, transcendentals=0),
    )(strain, jnp.asarray(window_table()), jnp.asarray(tw_cos), jnp.asarray(tw_sin),
      jnp.asarray(short_dft(), dtype=jnp.bfloat16), mask)


SIDE = 4
SLOTS = SIDE ** 3
PIECE = 2 * 2 * BINS * W
PARTS = ((0, 48, 48, (0, 1, 2)), (96, 48, 32, (1, 2, 0)), (176, 32, 48, (2, 0, 1)))
ROUNDS = 2
MESH = pl.DeviceIdType.MESH


def position():
    chan, band = lax.axis_index("chan"), lax.axis_index("band")
    return (chan // 4, chan // 2 % 2 * 2 + band // 4, band % 4), chan % 2


def device_at(at, core):
    x, y, z = at
    return (x * 4 + y // 2 * 2 + core, y % 2 * 4 + z)


def neighbour(axis, step):
    at, core = position()
    moved = list(at)
    moved[axis] = lax.rem(at[axis] + step + SIDE, SIDE)
    return device_at(moved, core)


def slots(ref, at, full, first, count):
    whole = slice(None)
    x = whole if 0 in full else at[0]
    y_hi, y_lo = (whole, whole) if 1 in full else (at[1] // 2, at[1] % 2)
    z = whole if 2 in full else at[2]
    return ref.at[x, y_hi, y_lo, z, pl.ds(first, count), :]


def lag_kernel(white, piece, tables, out, spectra, held, left, cross, total, table, outgoing, incoming,
               local_sem, send_sem, recv_sem, side_send, side_recv):
    at, core = position()
    sibling = device_at(at, 1 - core)
    columns = out.shape[1]
    channels = columns // SRC_BLOCK

    own_piece = pltpu.make_async_copy(piece, spectra.at[at[0], at[1] // 2, at[1] % 2, at[2]], local_sem.at[0])
    own_white = pltpu.make_async_copy(white.at[:, core], held.at[0], local_sem.at[1])
    own_table = pltpu.make_async_copy(tables.at[core], table, local_sem.at[2])
    own_piece.start()
    own_white.start()
    own_table.start()

    barrier = pltpu.get_barrier_semaphore()
    for axis in range(3):
        for step in (1, -1):
            pl.semaphore_signal(barrier, inc=1, device_id=neighbour(axis, step), device_id_type=MESH)
    pl.semaphore_signal(barrier, inc=1, device_id=sibling, device_id_type=MESH)
    pl.semaphore_wait(barrier, 7)

    other_white = pltpu.make_async_remote_copy(
        src_ref=white.at[:, 1 - core], dst_ref=held.at[1], send_sem=side_send.at[0], recv_sem=side_recv.at[0],
        device_id=sibling, device_id_type=MESH)
    other_white.start()
    own_piece.wait()

    copies = {}

    def start(turn, stage, part, kind):
        first, low, high, order = PARTS[part]
        first += turn * (PIECE // ROUNDS)
        axis, full = order[stage], order[:stage]
        if kind < 2:
            ref = slots(spectra, at, full, first, low + high)
        else:
            moved = list(at)
            moved[axis] = lax.rem(at[axis] + (SIDE - 1 if kind == 2 else 1), SIDE)
            ref = slots(spectra, moved, full, first + (0 if kind == 2 else low), low if kind == 2 else high)
        slot = ((turn * 3 + stage) * 3 + part) * 4 + kind
        copy = pltpu.make_async_remote_copy(
            src_ref=ref, dst_ref=ref, send_sem=send_sem.at[slot], recv_sem=recv_sem.at[slot],
            device_id=neighbour(axis, 1 if kind % 2 == 0 else -1), device_id_type=MESH)
        copies[turn, stage, part, kind] = copy
        copy.start()

    def begin(turn, stage):
        for part in range(3):
            start(turn, stage, part, 0)
            start(turn, stage, part, 1)

    def forward(turn, stage):
        for part in range(3):
            copies[turn, stage, part, 0].wait_recv()
            start(turn, stage, part, 2)
            copies[turn, stage, part, 1].wait_recv()
            start(turn, stage, part, 3)

    def finish(turn, stage):
        for part in range(3):
            copies[turn, stage, part, 2].wait_recv()
            copies[turn, stage, part, 3].wait_recv()

    row = lax.broadcasted_iota(jnp.int32, (2 * BINS, R2), 0) % BINS
    lane = lax.broadcasted_iota(jnp.int32, (2 * BINS, R2), 1)
    own = lane // W == row

    def spread(core_index):
        def step(index, _):
            x, y_hi, y_lo, z = index // 16, index // 8 % 2, index // 4 % 2, index % 4
            for ri in range(2):
                rows = pl.ds(pl.multiple_of(ri * HALF + z * 16, 16), 16)
                for k in range(channels // 8):
                    value = held[core_index, x * 2 + y_hi, y_lo, rows, k * R2:(k + 1) * R2].astype(jnp.float32)
                    for g in range(2):
                        even = pltpu.roll(value[g * BINS:(g + 1) * BINS], 0, 1, stride=W, stride_axis=0)
                        both = jnp.concatenate([even, pltpu.roll(even, R2 - W, 1)], axis=0)
                        for t in range(4):
                            moved = pltpu.roll(both, R2 - 2 * W * t, 1) if t else both
                            first = ((core_index * channels // 8 + k) * 4 + t) * 2 * BINS
                            left[g, index, first:first + 2 * BINS, ri * R2:(ri + 1) * R2] = jnp.where(
                                own, moved, 0.0).astype(jnp.bfloat16)
            return 0

        return step

    def multiply(turn):
        def step(index, _):
            results = []
            for h in range(2):
                slot = index * 2 + h
                s = spectra[slot // 16, slot // 8 % 2, slot // 4 % 2, slot % 4, turn * 256:(turn + 1) * 256, :]
                right = jnp.concatenate([s, jnp.concatenate([-s[R2:], s[:R2]], axis=0)], axis=1)
                results.append(jnp.dot(left[turn, slot], right, preferred_element_type=jnp.float32))
            base = pl.multiple_of(index * 32, 32)
            for c in range(2 * channels):
                both = jnp.concatenate([r[c * BINS:(c + 1) * BINS] for r in results], axis=0).astype(jnp.bfloat16)
                cross[pl.ds(base, 16), c * SRC_BLOCK:(c + 1) * SRC_BLOCK] = both[:, :SRC_BLOCK]
                cross[pl.ds(base + 16, 16), c * SRC_BLOCK:(c + 1) * SRC_BLOCK] = both[:, SRC_BLOCK:]
            return 0

        return step

    width = 1024

    def sum_lags(turn, core_index, store):
        def step(n, _):
            to = pl.ds(pl.multiple_of(n * width, width), width)
            both = pl.ds(pl.multiple_of(core_index * columns + n * width, width), width)
            store(to, both, jnp.dot(table[:, turn * 1024:(turn + 1) * 1024], cross[:, both],
                                    preferred_element_type=jnp.float32))
            return 0

        lax.fori_loop(0, columns // width, step, 0)

    def keep(to, both, value):
        total[:, both] = value

    def hand_over(to, both, value):
        outgoing[:, to] = ((total[:, both] + value) * FACTOR).astype(jnp.bfloat16)

    def conclude(to, both, value):
        total[:, both] = total[:, both] + value

    pairs = SLOTS // 2
    begin(0, 0)
    own_white.wait()
    lax.fori_loop(0, 6, spread(0), 0)
    forward(0, 0)
    lax.fori_loop(6, 10, spread(0), 0)
    finish(0, 0)
    begin(0, 1)
    begin(1, 0)
    lax.fori_loop(10, 22, spread(0), 0)
    forward(0, 1)
    forward(1, 0)
    lax.fori_loop(22, 30, spread(0), 0)
    finish(0, 1)
    finish(1, 0)
    begin(0, 2)
    begin(1, 1)
    lax.fori_loop(30, SLOTS, spread(0), 0)
    other_white.wait_recv()
    lax.fori_loop(0, 16, spread(1), 0)
    forward(1, 1)
    forward(0, 2)
    finish(1, 1)
    lax.fori_loop(16, SLOTS, spread(1), 0)
    finish(0, 2)
    begin(1, 2)
    own_table.wait()
    lax.fori_loop(0, pairs, multiply(0), 0, unroll=2)
    forward(1, 2)
    sum_lags(0, 0, keep)
    sum_lags(0, 1, keep)
    finish(1, 2)
    lax.fori_loop(0, pairs, multiply(1), 0, unroll=2)
    sum_lags(1, 1, hand_over)
    exchange = pltpu.make_async_remote_copy(
        src_ref=outgoing, dst_ref=incoming, send_sem=side_send.at[1], recv_sem=side_recv.at[1],
        device_id=sibling, device_id_type=MESH)
    exchange.start()
    sum_lags(1, 0, conclude)
    exchange.wait()
    out[...] = (total[:, :columns] * FACTOR + incoming[...].astype(jnp.float32)).astype(out.dtype)
    other_white.wait_send()
    for copy in copies.values():
        copy.wait_send()


def correlate(white, piece):
    lanes = white.shape[2]
    columns = lanes // W * SRC_BLOCK
    grouped = white.reshape(SIDE * 2, 2, 2, R2, lanes)
    half = 2 * NF // 2
    copies = ROUNDS * 3 * 3 * 4
    anywhere = pl.BlockSpec(memory_space=pl.ANY)
    return pl.pallas_call(
        lag_kernel,
        in_specs=[anywhere] * 3,
        out_specs=pl.BlockSpec(memory_space=pltpu.VMEM),
        out_shape=jax.ShapeDtypeStruct((LAGS, columns), jnp.bfloat16),
        scratch_shapes=[
            pltpu.VMEM((SIDE, 2, 2, SIDE, PIECE, SRC_BLOCK), jnp.bfloat16),
            pltpu.VMEM((2, SIDE * 2, 2, R2, lanes), jnp.bfloat16),
            pltpu.VMEM((2, SLOTS, 256, 256), jnp.bfloat16),
            pltpu.VMEM((half // 2, 2 * columns), jnp.bfloat16),
            pltpu.VMEM((LAGS, 2 * columns), jnp.float32),
            pltpu.VMEM((LAGS, half), jnp.bfloat16),
            pltpu.VMEM((LAGS, columns), jnp.bfloat16),
            pltpu.VMEM((LAGS, columns), jnp.bfloat16),
            pltpu.SemaphoreType.DMA((3,)),
            pltpu.SemaphoreType.DMA((copies,)),
            pltpu.SemaphoreType.DMA((copies,)),
            pltpu.SemaphoreType.DMA((2,)),
            pltpu.SemaphoreType.DMA((2,)),
        ],
        compiler_params=pltpu.CompilerParams(
            vmem_limit_bytes=60 * 2**20, collective_id=1, has_side_effects=True),
        cost_estimate=pl.CostEstimate(flops=4 * 256 * 4096 * 2048, bytes_accessed=20 * 2**20, transcendentals=0),
    )(grouped, piece, jnp.asarray(lag_table(), dtype=jnp.bfloat16))


def body(strain, source_block, source_offset, window_valid):
    own_rows = strain.shape[0]
    bands = lax.axis_size("band")
    chans = lax.axis_size("chan")
    block, offset = source_block[0], source_offset[0]
    row = lax.axis_index("band") * own_rows + jnp.arange(own_rows, dtype=jnp.int32)
    chan = lax.axis_index("chan")
    held = ((chan == block) & (row >= offset)) | ((chan == (block + 1) % chans) & (row < offset))
    mask = (held[:, None] & (window_valid != 0)[None, :]).astype(jnp.float32).reshape(1, own_rows * W)
    white, masked = whiten(strain, mask)

    per = R1 // chans
    parts = lax.all_to_all(masked, "chan", split_axis=0, concat_axis=0, tiled=True)
    piece = jnp.sum(parts.reshape(chans, per, R2, own_rows * W).astype(jnp.float32), axis=0).astype(jnp.bfloat16)
    piece = piece.reshape(per, 2, 4, 16, own_rows * W).transpose(0, 2, 1, 3, 4).reshape(bands, 2, 16, own_rows * W)
    piece = lax.all_to_all(piece, "band", split_axis=0, concat_axis=0, tiled=True)
    piece = piece.reshape(bands, 2, 2, BINS, own_rows, W).transpose(2, 1, 3, 5, 0, 4)
    piece = jnp.roll(piece.reshape(2, 2 * BINS * W, SRC_BLOCK), -offset, axis=2)
    total = correlate(white, piece.reshape(PIECE, SRC_BLOCK))
    total = total.reshape(LAGS, own_rows, bands, SRC_BLOCK // bands).transpose(2, 3, 0, 1)
    total = lax.all_to_all(total, "band", split_axis=0, concat_axis=0, tiled=False)
    return total.transpose(1, 2, 0, 3).reshape(SRC_BLOCK // bands, LAGS, bands * own_rows)


def solution(mesh):
    in_specs = (P(("chan", "band"), None), P(), P(), P())
    out_specs = P("band", None, "chan")
    return jax.shard_map(body, mesh=mesh, in_specs=in_specs, out_specs=out_specs, check_vma=False)
```

```python
import functools
import math

import jax
import jax.numpy as jnp
import numpy as np
from jax import lax
from jax.experimental import pallas as pl
from jax.experimental.pallas import tpu as pltpu
from jax.sharding import PartitionSpec as P

L = 4096
HOP = 2048
NF = 2048
W = 16
SRC_BLOCK = 128
LAGS = 256
R1 = 32
R2 = 128
HALF = R2 // 2
BINS = 8
FACTOR = 1.0 / (W * math.sqrt(NF))


def window_table():
    points = np.arange(L, dtype=np.float32)
    angle = (points * np.float32(2.0 * math.pi / L)).astype(np.float32)
    return (np.float32(0.5) - np.float32(0.5) * np.cos(angle)).astype(np.float32).reshape(R1, R2)


def row_tables():
    angle = 2.0 * np.pi * np.outer(np.arange(R1), np.arange(R2)) / L
    return np.concatenate([window_table(), np.cos(angle), -np.sin(angle)], axis=0).astype(np.float32)


def short_dft():
    angle = 2.0 * np.pi * (np.outer(np.arange(HALF), np.arange(R2)) % R2) / R2
    cosine, sine = np.cos(angle), np.sin(angle)
    top = np.concatenate([cosine, sine], axis=1)
    low = np.concatenate([-sine, cosine], axis=1)
    return np.concatenate([top, low], axis=0).astype(np.float32)


def lag_table():
    core, g, x, y_hi, y_lo, z_hi, z_lo, i = np.ix_(*[np.arange(n) for n in (2, 2, 4, 2, 2, 2, 2, 8)])
    bins = 8 * x + 4 * y_hi + 2 * core + y_lo + R1 * (16 * (2 * z_hi + z_lo) + 8 * g + i)
    lags = (np.arange(LAGS) - LAGS // 2).reshape((1, LAGS) + (1,) * 7)
    angle = 2.0 * np.pi * (lags * bins[:, None] % L) / L
    table = np.stack([np.cos(angle), -np.sin(angle)], axis=7)
    return table.reshape(2, LAGS, NF).astype(np.float32)


def real_dft(x):
    n = len(x)
    if n == 2:
        return [(x[0] + x[1], None), (x[0] - x[1], None)]
    even, odd = real_dft(x[0::2]), real_dft(x[1::2])
    out = [None] * (n // 2 + 1)
    for k in range(n // 4 + 1):
        er, ei = even[k]
        orr, oi = odd[k]
        if k == 0:
            out[0] = (er + orr, None)
            out[n // 2] = (er - orr, None)
            continue
        if 4 * k == n:
            out[k] = (er, -orr)
            continue
        c, s = math.cos(2 * math.pi * k / n), -math.sin(2 * math.pi * k / n)
        if oi is None:
            tr, ti = orr * c, orr * s
        else:
            tr, ti = orr * c - oi * s, orr * s + oi * c
        zi = ti if ei is None else ei + ti
        yi = -ti if ei is None else ei - ti
        out[k] = (er + tr, zi)
        out[n // 2 - k] = (er - tr, -yi)
    return out


SIDE = 4
SLOTS = SIDE ** 3
PIECE = 2 * 2 * BINS * W
PARTS = ((0, 48, 48, (0, 1, 2)), (96, 48, 32, (1, 2, 0)), (176, 32, 48, (2, 0, 1)))
ROUNDS = 2
MESH = pl.DeviceIdType.MESH


def position():
    chan, band = lax.axis_index("chan"), lax.axis_index("band")
    return (chan // 4, chan // 2 % 2 * 2 + band // 4, band % 4), chan % 2


def device_at(at, core):
    x, y, z = at
    return (x * 4 + y // 2 * 2 + core, y % 2 * 4 + z)


def neighbour(axis, step):
    at, core = position()
    moved = list(at)
    moved[axis] = lax.rem(at[axis] + step + SIDE, SIDE)
    return device_at(moved, core)


def slots(ref, at, full, first, count):
    whole = slice(None)
    x = whole if 0 in full else at[0]
    y_hi, y_lo = (whole, whole) if 1 in full else (at[1] // 2, at[1] % 2)
    z = whole if 2 in full else at[2]
    return ref.at[x, y_hi, y_lo, z, pl.ds(first, count), :]


def partners(at, core):
    x, y, z = at
    side = lambda step: lax.rem(z + step, SIDE)
    along = [((lax.rem(x + dx, SIDE), y ^ (2 * dy), z), core) for dx in range(SIDE) for dy in range(2)][1:]
    across = [((x, y ^ dy, side(dz)), core) for dy in range(2) for dz in range(SIDE)][1:]
    return along, across, [((x, y ^ 3, z), core), (at, 1 - core)]


def kernel(strain_hbm, rows_hbm, dft_hbm, tables, block, offset, valid, out,
           strain, rows, dft, table, held, mixed, parts, share, bands, spectra, left, cross, total,
           outgoing, incoming, turned, shipped, landed,
           local_sem, send_sem, recv_sem, side_send, side_recv, chan_send, chan_recv, band_send, band_recv,
           ship_send, ship_recv):
    at, core = position()
    chan, band = lax.axis_index("chan"), lax.axis_index("band")
    sibling = device_at(at, 1 - core)
    lanes = held.shape[-1]
    channels = lanes // W
    columns = channels * SRC_BLOCK
    along, across, rest = partners(at, core)

    def fetch(src, dst, index):
        copy = pltpu.make_async_copy(src, dst, local_sem.at[index])
        copy.start()
        return copy

    fetched = [fetch(strain_hbm, strain, 0), fetch(rows_hbm, rows, 1), fetch(dft_hbm, dft, 2)]
    own_table = fetch(tables.at[core], table, 3)
    barrier = pltpu.get_barrier_semaphore()
    for place, which in along + across + rest:
        pl.semaphore_signal(barrier, inc=1, device_id=device_at(place, which), device_id_type=MESH)
    for copy in fetched:
        copy.wait()

    folded = left.at[0]

    def fold(c, _):
        first = c // BINS * (BINS * (W + 1) * W) + c % BINS
        x = [strain[pl.ds(first + BINS * k, W, stride=BINS * W), :] for k in range(R1)]
        whole = x[0]
        for k in range(1, R1):
            whole = whole + x[k]
        mean = jnp.sum(whole, axis=1, keepdims=True) * (1.0 / L)
        x = [((x[k] - mean) * rows[k:k + 1, :]).astype(jnp.bfloat16).astype(jnp.float32) for k in range(R1)]
        bins = real_dft(x)
        to = pl.ds(pl.multiple_of(c * W, W), W)
        for f in range(R1):
            re, im = bins[f] if f <= R1 // 2 else bins[R1 - f]
            cosine, sine = rows[R1 + f:R1 + f + 1, :], rows[2 * R1 + f:2 * R1 + f + 1, :]
            if im is None:
                gr, gi = re * cosine, re * sine
            else:
                im = im if f <= R1 // 2 else -im
                gr, gi = re * cosine - im * sine, re * sine + im * cosine
            folded[f, to, :R2] = gr.astype(jnp.bfloat16)
            folded[f, to, R2:] = gi.astype(jnp.bfloat16)
        return 0

    lax.fori_loop(0, channels, fold, 0, unroll=2)
    dft_table = dft[...]

    def transform(f, power):
        y = lax.dot_general(dft_table, folded[f], (((1,), (1,)), ((), ())), preferred_element_type=jnp.float32)
        total[f, :R2, :] = y[:, :R2]
        total[f, R2:, :] = y[:, R2:]
        square = y * y
        return power + (square[:HALF] + square[HALF:])

    power = lax.fori_loop(0, R1, transform, jnp.zeros((HALF, lanes), jnp.float32), unroll=8)
    scales = []
    for b in range(HALF // BINS):
        mean = jnp.sum(power[b * BINS:(b + 1) * BINS], axis=0, keepdims=True) * (1.0 / 256.0)
        scales.append(jnp.broadcast_to(lax.rsqrt(mean + 1e-06), (BINS, lanes)))
    scale = jnp.concatenate(scales + scales, axis=0)

    def finish_white(to, which):
        def step(index, _):
            f = index // 2 * 4 + which * 2 + index % 2
            y = jnp.concatenate([total[f, :R2, :], total[f, R2:, :]], axis=1)
            held[to, index // 2, index % 2] = (y * scale).astype(jnp.bfloat16)
            return 0

        lax.fori_loop(0, R1 // 2, step, 0, unroll=4)

    finish_white(2, 1 - core)
    pl.semaphore_wait(barrier, len(along) + len(across) + len(rest))
    swap = pltpu.make_async_remote_copy(
        src_ref=held.at[2], dst_ref=held.at[1], send_sem=side_send.at[0], recv_sem=side_recv.at[0],
        device_id=sibling, device_id_type=MESH)
    swap.start()
    finish_white(0, core)

    row = lax.broadcasted_iota(jnp.int32, (2 * BINS, R2), 0) % BINS
    lane = lax.broadcasted_iota(jnp.int32, (2 * BINS, R2), 1)
    own = lane // W == row

    def spread(core_index):
        def step(index, _):
            x, y_hi, y_lo, z = index // 16, index // 8 % 2, index // 4 % 2, index % 4
            for ri in range(2):
                picked = pl.ds(pl.multiple_of(ri * HALF + z * 16, 16), 16)
                for k in range(channels // 8):
                    value = held[core_index, x * 2 + y_hi, y_lo, picked, k * R2:(k + 1) * R2].astype(jnp.float32)
                    for g in range(2):
                        even = pltpu.roll(value[g * BINS:(g + 1) * BINS], 0, 1, stride=W, stride_axis=0)
                        both = jnp.concatenate([even, pltpu.roll(even, R2 - W, 1)], axis=0)
                        for t in range(4):
                            moved = pltpu.roll(both, R2 - 2 * W * t, 1) if t else both
                            first = ((core_index * channels // 8 + k) * 4 + t) * 2 * BINS
                            left[g, index, first:first + 2 * BINS, ri * R2:(ri + 1) * R2] = jnp.where(
                                own, moved, 0.0).astype(jnp.bfloat16)
            return 0

        return step

    lax.fori_loop(0, 16, spread(0), 0)

    spot = lax.broadcasted_iota(jnp.int32, (1, lanes), 1)
    source = band * channels + spot // W
    stacked = jnp.zeros((1, lanes), jnp.float32)
    for w in range(W):
        stacked = jnp.where(spot % W == w, jnp.where(valid[w] != 0, 1.0, 0.0), stacked)
    chans = R1 // 2

    def chosen(which):
        first = jnp.where(which == block[0], 1, 0)
        second = jnp.where(which == lax.rem(block[0] + 1, chans), 1, 0)
        taken = jnp.where(source >= offset[0], first, second)
        return jnp.where(taken == 1, stacked, 0.0)

    mine, theirs = chosen(chan), chosen(chan ^ 1)
    swap.wait_recv()

    def mix(index, _):
        a, b = held[0, index // 2, index % 2], held[1, index // 2, index % 2]
        value = a.astype(jnp.float32) * mine + b.astype(jnp.float32) * theirs
        mixed[index // 2, index % 2] = value.astype(jnp.bfloat16)
        return 0

    lax.fori_loop(0, R1 // 2, mix, 0, unroll=4)
    slot = chan // 2
    sums = []
    for r, (place, which) in enumerate(along):
        target = place[0] * 2 + place[1] // 2
        sums.append(pltpu.make_async_remote_copy(
            src_ref=mixed.at[target], dst_ref=parts.at[slot], send_sem=chan_send.at[r], recv_sem=chan_recv.at[r],
            device_id=device_at(place, which), device_id_type=MESH))
    for copy in sums:
        copy.start()
    lax.fori_loop(16, SLOTS, spread(0), 0)
    lax.fori_loop(0, 24, spread(1), 0)
    for copy in sums:
        copy.wait_recv()
    parts[slot] = mixed[slot]
    for lo in range(2):
        value = parts[0, lo].astype(jnp.float32)
        for k in range(1, SIDE * 2):
            value = value + parts[k, lo].astype(jnp.float32)
        share[lo] = value.astype(jnp.bfloat16).reshape(2, SIDE, 16, lanes)

    moves = []
    for r, (place, which) in enumerate(across):
        moves.append(pltpu.make_async_remote_copy(
            src_ref=share.at[place[1] % 2, :, place[2]], dst_ref=bands.at[band],
            send_sem=band_send.at[r], recv_sem=band_recv.at[r],
            device_id=device_at(place, which), device_id_type=MESH))
    for copy in moves:
        copy.start()
    bands[band] = share[at[1] % 2, :, at[2]]
    lax.fori_loop(24, 40, spread(1), 0)
    for copy in moves:
        copy.wait_recv()

    wide = (BINS * W, lanes)
    same = lax.broadcasted_iota(jnp.int32, wide, 1) % W == lax.broadcasted_iota(jnp.int32, wide, 0) % W
    tall = (lanes, SRC_BLOCK)
    channel = lax.broadcasted_iota(jnp.int32, tall, 0) // W
    column = lax.broadcasted_iota(jnp.int32, tall, 1)
    value = None
    for b in range(2 * SIDE):
        goal = (channel + (b * channels + SRC_BLOCK) - offset[0]) % SRC_BLOCK
        pick = jnp.where(goal == column, 1.0, 0.0).astype(jnp.bfloat16)
        blocks = []
        for g in range(2):
            for ri in range(2):
                part = bands[b, ri].astype(jnp.float32)[g * BINS:(g + 1) * BINS]
                part = jnp.broadcast_to(part[:, None, :], (BINS, W, lanes)).reshape(wide)
                blocks.append(jnp.where(same, part, 0.0).astype(jnp.bfloat16))
        term = jnp.dot(jnp.concatenate(blocks, axis=0), pick, preferred_element_type=jnp.float32)
        value = term if value is None else value + term
    spectra[at[0], at[1] // 2, at[1] % 2, at[2]] = value.astype(jnp.bfloat16)

    copies = {}

    def start(turn, stage, part, kind):
        first, low, high, order = PARTS[part]
        first += turn * (PIECE // ROUNDS)
        axis, full = order[stage], order[:stage]
        if kind < 2:
            ref = slots(spectra, at, full, first, low + high)
        else:
            moved = list(at)
            moved[axis] = lax.rem(at[axis] + (SIDE - 1 if kind == 2 else 1), SIDE)
            ref = slots(spectra, moved, full, first + (0 if kind == 2 else low), low if kind == 2 else high)
        index = ((turn * 3 + stage) * 3 + part) * 4 + kind
        copy = pltpu.make_async_remote_copy(
            src_ref=ref, dst_ref=ref, send_sem=send_sem.at[index], recv_sem=recv_sem.at[index],
            device_id=neighbour(axis, 1 if kind % 2 == 0 else -1), device_id_type=MESH)
        copies[turn, stage, part, kind] = copy
        copy.start()

    def begin(turn, stage):
        for part in range(3):
            start(turn, stage, part, 0)
            start(turn, stage, part, 1)

    def forward(turn, stage):
        for part in range(3):
            copies[turn, stage, part, 0].wait_recv()
            start(turn, stage, part, 2)
            copies[turn, stage, part, 1].wait_recv()
            start(turn, stage, part, 3)

    def finish(turn, stage):
        for part in range(3):
            copies[turn, stage, part, 2].wait_recv()
            copies[turn, stage, part, 3].wait_recv()

    def multiply(turn):
        def step(index, _):
            results = []
            for h in range(2):
                k = index * 2 + h
                s = spectra[k // 16, k // 8 % 2, k // 4 % 2, k % 4, turn * 256:(turn + 1) * 256, :]
                right = jnp.concatenate([s, jnp.concatenate([-s[R2:], s[:R2]], axis=0)], axis=1)
                results.append(jnp.dot(left[turn, k], right, preferred_element_type=jnp.float32))
            base = pl.multiple_of(index * 32, 32)
            for c in range(2 * channels):
                both = jnp.concatenate([r[c * BINS:(c + 1) * BINS] for r in results], axis=0).astype(jnp.bfloat16)
                cross[pl.ds(base, 16), c * SRC_BLOCK:(c + 1) * SRC_BLOCK] = both[:, :SRC_BLOCK]
                cross[pl.ds(base + 16, 16), c * SRC_BLOCK:(c + 1) * SRC_BLOCK] = both[:, SRC_BLOCK:]
            return 0

        return step

    group = 8
    width = group * SRC_BLOCK

    def sum_lags(turn, core_index, store):
        def step(n, _):
            both = pl.ds(pl.multiple_of(core_index * columns + n * width, width), width)
            value = jnp.dot(table[:, turn * 1024:(turn + 1) * 1024], cross[:, both],
                            preferred_element_type=jnp.float32)
            for i in range(group):
                store(n * group + i, core_index * channels + n * group + i,
                      value[:, i * SRC_BLOCK:(i + 1) * SRC_BLOCK])
            return 0

        lax.fori_loop(0, channels // group, step, 0)

    def keep(c, held_c, value):
        total[held_c] = value

    def hand_over(c, held_c, value):
        outgoing[c] = ((total[held_c] + value) * FACTOR).astype(jnp.bfloat16)

    def conclude(c, held_c, value):
        total[held_c] = total[held_c] + value

    pairs = SLOTS // 2
    begin(0, 0)
    lax.fori_loop(40, 48, spread(1), 0)
    forward(0, 0)
    finish(0, 0)
    begin(0, 1)
    begin(1, 0)
    lax.fori_loop(48, 56, spread(1), 0)
    forward(0, 1)
    forward(1, 0)
    lax.fori_loop(56, 60, spread(1), 0)
    finish(0, 1)
    finish(1, 0)
    begin(0, 2)
    begin(1, 1)
    lax.fori_loop(60, SLOTS, spread(1), 0)
    forward(1, 1)
    forward(0, 2)
    finish(1, 1)
    finish(0, 2)
    begin(1, 2)
    own_table.wait()
    lax.fori_loop(0, pairs, multiply(0), 0, unroll=2)
    forward(1, 2)
    sum_lags(0, 0, keep)
    sum_lags(0, 1, keep)
    finish(1, 2)
    lax.fori_loop(0, pairs, multiply(1), 0, unroll=2)
    sum_lags(1, 1, hand_over)
    exchange = pltpu.make_async_remote_copy(
        src_ref=outgoing, dst_ref=incoming, send_sem=side_send.at[1], recv_sem=side_recv.at[1],
        device_id=sibling, device_id_type=MESH)
    exchange.start()
    sum_lags(1, 0, conclude)
    exchange.wait_recv()

    diagonal = (lax.broadcasted_iota(jnp.int32, (LAGS, LAGS), 0) == lax.broadcasted_iota(jnp.int32, (LAGS, LAGS), 1))
    unit = jnp.where(diagonal, 1.0, 0.0).astype(jnp.bfloat16)
    last = (((1,), (1,)), ((), ()))
    for c in range(channels):
        value = (total[c] * FACTOR + incoming[c].astype(jnp.float32)).astype(jnp.bfloat16)
        value = lax.dot_general(unit[:SRC_BLOCK, :SRC_BLOCK], value, last, preferred_element_type=jnp.float32)
        for half in range(2):
            turned[half, pl.ds(c, SRC_BLOCK, stride=channels), :] = value[:, half * R2:(half + 1) * R2]

    def pack(index):
        picked = pl.ds(pl.multiple_of(index * 256, 256), 256)
        return jnp.concatenate([turned[0, picked, :], turned[1, picked, :]], axis=1).astype(jnp.bfloat16)

    ships = []
    for r, (place, which) in enumerate(across):
        index = place[1] % 2 * SIDE + place[2]
        shipped[index] = pack(index)
        ship = pltpu.make_async_remote_copy(
            src_ref=shipped.at[index], dst_ref=landed.at[band], send_sem=ship_send.at[r], recv_sem=ship_recv.at[r],
            device_id=device_at(place, which), device_id_type=MESH)
        ship.start()
        ships.append(ship)
    landed[band] = pack(band)
    for ship in ships:
        ship.wait_recv()
    for s in range(SRC_BLOCK // (2 * SIDE)):
        value = landed[:, s * channels:(s + 1) * channels, :].reshape(2 * SIDE * channels, LAGS)
        out[s] = lax.dot_general(unit, value, last, preferred_element_type=jnp.float32).astype(out.dtype)

    for copy in [swap, exchange] + sums + moves + ships + list(copies.values()):
        copy.wait_send()


def body(strain, source_block, source_offset, window_valid):
    channels = strain.shape[0]
    lanes = channels * W
    columns = channels * SRC_BLOCK
    tiles = strain.reshape(channels // BINS, BINS, -1, R2).transpose(0, 2, 1, 3).reshape(-1, R2)
    copies = ROUNDS * 3 * 3 * 4
    anywhere = pl.BlockSpec(memory_space=pl.ANY)
    scalars = pl.BlockSpec(memory_space=pltpu.SMEM)
    dma = pltpu.SemaphoreType.DMA
    bf16, f32 = jnp.bfloat16, jnp.float32
    return pl.pallas_call(
        kernel,
        in_specs=[anywhere] * 4 + [scalars] * 3,
        out_specs=pl.BlockSpec(memory_space=pltpu.VMEM),
        out_shape=jax.ShapeDtypeStruct((SRC_BLOCK // (2 * SIDE), LAGS, 2 * SIDE * channels), bf16),
        scratch_shapes=[
            pltpu.VMEM(tiles.shape, f32),
            pltpu.VMEM((3 * R1, R2), f32),
            pltpu.VMEM((R2, 2 * R2), bf16),
            pltpu.VMEM((LAGS, NF), bf16),
            pltpu.VMEM((3, SIDE * 2, 2, R2, lanes), bf16),
            pltpu.VMEM((SIDE * 2, 2, R2, lanes), bf16),
            pltpu.VMEM((SIDE * 2, 2, R2, lanes), bf16),
            pltpu.VMEM((2, 2, SIDE, 16, lanes), bf16),
            pltpu.VMEM((2 * SIDE, 2, 16, lanes), bf16),
            pltpu.VMEM((SIDE, 2, 2, SIDE, PIECE, SRC_BLOCK), bf16),
            pltpu.VMEM((2, SLOTS, 256, 256), bf16),
            pltpu.VMEM((NF // 2, 2 * columns), bf16),
            pltpu.VMEM((2 * channels, LAGS, SRC_BLOCK), f32),
            pltpu.VMEM((channels, LAGS, SRC_BLOCK), bf16),
            pltpu.VMEM((channels, LAGS, SRC_BLOCK), bf16),
            pltpu.VMEM((2, columns, R2), f32),
            pltpu.VMEM((2 * SIDE, 256, LAGS), bf16),
            pltpu.VMEM((2 * SIDE, 256, LAGS), bf16),
            dma((4,)), dma((copies,)), dma((copies,)), dma((2,)), dma((2,)),
            dma((7,)), dma((7,)), dma((7,)), dma((7,)), dma((7,)), dma((7,)),
        ],
        compiler_params=pltpu.CompilerParams(
            vmem_limit_bytes=62 * 2**20, collective_id=1, has_side_effects=True),
        cost_estimate=pl.CostEstimate(flops=4 * 256 * 4096 * 2048, bytes_accessed=20 * 2**20, transcendentals=0),
    )(tiles, jnp.asarray(row_tables()), jnp.asarray(short_dft(), dtype=bf16),
      jnp.asarray(lag_table(), dtype=bf16), source_block, source_offset, window_valid)


def solution(mesh):
    in_specs = (P(("chan", "band"), None), P(), P(), P())
    out_specs = P("band", None, "chan")
    return jax.shard_map(body, mesh=mesh, in_specs=in_specs, out_specs=out_specs, check_vma=False)
```

```python
import functools
import math

import jax
import jax.numpy as jnp
import numpy as np
from jax import lax
from jax.experimental import pallas as pl
from jax.experimental.pallas import tpu as pltpu
from jax.sharding import PartitionSpec as P

L = 4096
HOP = 2048
NF = 2048
W = 16
SRC_BLOCK = 128
LAGS = 256
R1 = 32
R2 = 128
HALF = R2 // 2
BINS = 8
FACTOR = 1.0 / (W * math.sqrt(NF))


def window_table():
    points = np.arange(L, dtype=np.float32)
    angle = (points * np.float32(2.0 * math.pi / L)).astype(np.float32)
    return (np.float32(0.5) - np.float32(0.5) * np.cos(angle)).astype(np.float32).reshape(R1, R2)


def row_tables():
    angle = 2.0 * np.pi * np.outer(np.arange(R1), np.arange(R2)) / L
    return np.concatenate([window_table(), np.cos(angle), -np.sin(angle)], axis=0).astype(np.float32)


def short_dft():
    angle = 2.0 * np.pi * (np.outer(np.arange(HALF), np.arange(R2)) % R2) / R2
    cosine, sine = np.cos(angle), np.sin(angle)
    top = np.concatenate([cosine, sine], axis=1)
    low = np.concatenate([-sine, cosine], axis=1)
    both = np.stack([top.reshape(-1, BINS, 2 * R2), low.reshape(-1, BINS, 2 * R2)], axis=1)
    return both.reshape(R2, 2 * R2).astype(np.float32)


def lag_table():
    core, g, x, y_hi, y_lo, z_hi, z_lo, i = np.ix_(*[np.arange(n) for n in (2, 2, 4, 2, 2, 2, 2, 8)])
    bins = 8 * x + 4 * y_hi + 2 * core + g + R1 * (32 * y_lo + 8 * (2 * z_hi + z_lo) + i)
    lags = (np.arange(LAGS) - LAGS // 2).reshape((1, LAGS) + (1,) * 7)
    angle = 2.0 * np.pi * (lags * bins[:, None] % L) / L
    table = np.stack([np.cos(angle), -np.sin(angle)], axis=7)
    return table.reshape(2, LAGS, NF).astype(np.float32)


def real_dft(x):
    n = len(x)
    if n == 2:
        return [(x[0] + x[1], None), (x[0] - x[1], None)]
    even, odd = real_dft(x[0::2]), real_dft(x[1::2])
    out = [None] * (n // 2 + 1)
    for k in range(n // 4 + 1):
        er, ei = even[k]
        orr, oi = odd[k]
        if k == 0:
            out[0] = (er + orr, None)
            out[n // 2] = (er - orr, None)
            continue
        if 4 * k == n:
            out[k] = (er, -orr)
            continue
        c, s = math.cos(2 * math.pi * k / n), -math.sin(2 * math.pi * k / n)
        if oi is None:
            tr, ti = orr * c, orr * s
        else:
            tr, ti = orr * c - oi * s, orr * s + oi * c
        zi = ti if ei is None else ei + ti
        yi = -ti if ei is None else ei - ti
        out[k] = (er + tr, zi)
        out[n // 2 - k] = (er - tr, -yi)
    return out


SIDE = 4
SLOTS = SIDE ** 3
PIECE = 2 * 2 * BINS * W
PARTS = ((0, 48, 48, (0, 1, 2)), (96, 48, 32, (1, 2, 0)), (176, 32, 48, (2, 0, 1)))
ROUNDS = 2
MESH = pl.DeviceIdType.MESH


def position():
    chan, band = lax.axis_index("chan"), lax.axis_index("band")
    return (chan // 4, chan // 2 % 2 * 2 + band // 4, band % 4), chan % 2


def device_at(at, core):
    x, y, z = at
    return (x * 4 + y // 2 * 2 + core, y % 2 * 4 + z)


def neighbour(axis, step):
    at, core = position()
    moved = list(at)
    moved[axis] = lax.rem(at[axis] + step + SIDE, SIDE)
    return device_at(moved, core)


def slots(ref, at, full, first, count):
    whole = slice(None)
    x = whole if 0 in full else at[0]
    y_hi, y_lo = (whole, whole) if 1 in full else (at[1] // 2, at[1] % 2)
    z = whole if 2 in full else at[2]
    return ref.at[x, y_hi, y_lo, z, pl.ds(first, count), :]


def partners(at, core):
    x, y, z = at
    side = lambda step: lax.rem(z + step, SIDE)
    along = [((lax.rem(x + dx, SIDE), y ^ (2 * dy), z), core) for dx in (2, 1, 3, 0) for dy in (1, 0)][:-1]
    across = [((x, y ^ dy, side(dz)), core) for dz in (2, 1, 3, 0) for dy in (1, 0)][:-1]
    return along, across, [((x, y ^ 3, z), core), (at, 1 - core)]


def kernel(strain_hbm, rows_hbm, dft_hbm, tables, block, offset, valid, out,
           strain, rows, dft, table, held, mixed, parts, share, bands, spectra, left, cross, total,
           outgoing, incoming, turned, shipped, landed,
           local_sem, send_sem, recv_sem, side_send, side_recv, chan_send, chan_recv, band_send, band_recv,
           ship_send, ship_recv):
    at, core = position()
    chan, band = lax.axis_index("chan"), lax.axis_index("band")
    sibling = device_at(at, 1 - core)
    lanes = held.shape[-1]
    channels = lanes // W
    columns = channels * SRC_BLOCK
    along, across, rest = partners(at, core)

    def fetch(src, dst, index):
        copy = pltpu.make_async_copy(src, dst, local_sem.at[index])
        copy.start()
        return copy

    fetched = [fetch(strain_hbm, strain, 0), fetch(rows_hbm, rows, 1), fetch(dft_hbm, dft, 2)]
    own_table = fetch(tables.at[core], table, 3)
    barrier = pltpu.get_barrier_semaphore()
    for place, which in along + across + rest:
        pl.semaphore_signal(barrier, inc=1, device_id=device_at(place, which), device_id_type=MESH)
    for copy in fetched:
        copy.wait()

    folded = left.at[0]

    def fold(c, _):
        first = c // BINS * (BINS * (W + 1) * W) + c % BINS
        x = [strain[pl.ds(first + BINS * k, W, stride=BINS * W), :] for k in range(R1)]
        whole = x[0]
        for k in range(1, R1):
            whole = whole + x[k]
        mean = jnp.sum(whole, axis=1, keepdims=True) * (1.0 / L)
        x = [((x[k] - mean) * rows[k:k + 1, :]).astype(jnp.bfloat16).astype(jnp.float32) for k in range(R1)]
        bins = real_dft(x)
        to = pl.ds(pl.multiple_of(c * W, W), W)
        for f in range(R1):
            re, im = bins[f] if f <= R1 // 2 else bins[R1 - f]
            cosine, sine = rows[R1 + f:R1 + f + 1, :], rows[2 * R1 + f:2 * R1 + f + 1, :]
            if im is None:
                gr, gi = re * cosine, re * sine
            else:
                im = im if f <= R1 // 2 else -im
                gr, gi = re * cosine - im * sine, re * sine + im * cosine
            folded[f, to, :R2] = gr.astype(jnp.bfloat16)
            folded[f, to, R2:] = gi.astype(jnp.bfloat16)
        return 0

    lax.fori_loop(0, channels, fold, 0, unroll=2)
    dft_table = dft[...]

    def transform(f, power):
        y = lax.dot_general(dft_table, folded[f], (((1,), (1,)), ((), ())), preferred_element_type=jnp.float32)
        total[f, :R2, :] = y[:, :R2]
        total[f, R2:, :] = y[:, R2:]
        square = (y * y).reshape(HALF // BINS, 2, BINS, lanes)
        return power + (square[:, 0] + square[:, 1]).reshape(HALF, lanes)

    power = lax.fori_loop(0, R1, transform, jnp.zeros((HALF, lanes), jnp.float32), unroll=8)
    scales = []
    for b in range(HALF // BINS):
        mean = jnp.sum(power[b * BINS:(b + 1) * BINS], axis=0, keepdims=True) * (1.0 / 256.0)
        scales.append(jnp.broadcast_to(lax.rsqrt(mean + 1e-06), (2 * BINS, lanes)))
    scale = jnp.concatenate(scales, axis=0)

    def finish_white(to, which, g):
        def step(index, _):
            f = index * 4 + which * 2 + g
            y = jnp.concatenate([total[f, :R2, :], total[f, R2:, :]], axis=1)
            held[to, g, index] = (y * scale).astype(jnp.bfloat16)
            return 0

        lax.fori_loop(0, SIDE * 2, step, 0, unroll=4)

    for g in range(2):
        finish_white(2, 1 - core, g)
    pl.semaphore_wait(barrier, len(along) + len(across) + len(rest))
    swaps = []
    for g in range(2):
        swap = pltpu.make_async_remote_copy(
            src_ref=held.at[2, g], dst_ref=held.at[1, g], send_sem=side_send.at[g], recv_sem=side_recv.at[g],
            device_id=sibling, device_id_type=MESH)
        swap.start()
        swaps.append(swap)
    for g in range(2):
        finish_white(0, core, g)

    row = lax.broadcasted_iota(jnp.int32, (2 * BINS, R2), 0) % BINS
    lane = lax.broadcasted_iota(jnp.int32, (2 * BINS, R2), 1)
    own = lane // W == row

    def spread(core_index):
        def step(index, _):
            x, y_hi, y_lo, z = index // 16, index // 8 % 2, index // 4 % 2, index % 4
            picked = pl.ds(pl.multiple_of((y_lo * SIDE + z) * 16, 16), 16)
            for g in range(2):
                for k in range(channels // 8):
                    value = held[core_index, g, x * 2 + y_hi, picked, k * R2:(k + 1) * R2].astype(jnp.float32)
                    for ri in range(2):
                        even = pltpu.roll(value[ri * BINS:(ri + 1) * BINS], 0, 1, stride=W, stride_axis=0)
                        both = jnp.concatenate([even, pltpu.roll(even, R2 - W, 1)], axis=0)
                        for t in range(4):
                            moved = pltpu.roll(both, R2 - 2 * W * t, 1) if t else both
                            first = ((core_index * channels // 8 + k) * 4 + t) * 2 * BINS
                            left[g, index, first:first + 2 * BINS, ri * R2:(ri + 1) * R2] = jnp.where(
                                own, moved, 0.0).astype(jnp.bfloat16)
            return 0

        return step

    lax.fori_loop(0, 8, spread(0), 0)

    spot = lax.broadcasted_iota(jnp.int32, (1, lanes), 1)
    source = band * channels + spot // W
    stacked = jnp.zeros((1, lanes), jnp.float32)
    for w in range(W):
        stacked = jnp.where(spot % W == w, jnp.where(valid[w] != 0, 1.0, 0.0), stacked)
    chans = R1 // 2

    def chosen(which):
        first = jnp.where(which == block[0], 1, 0)
        second = jnp.where(which == lax.rem(block[0] + 1, chans), 1, 0)
        taken = jnp.where(source >= offset[0], first, second)
        return jnp.where(taken == 1, stacked, 0.0)

    mine, theirs = chosen(chan), chosen(chan ^ 1)
    slot = chan // 2

    def mix(g):
        def step(index, _):
            a, b = held[0, g, index], held[1, g, index]
            value = a.astype(jnp.float32) * mine + b.astype(jnp.float32) * theirs
            mixed[g, index] = value.astype(jnp.bfloat16)
            return 0

        return step

    sums, moves = {}, {}
    for g in range(2):
        swaps[g].wait_recv()
        lax.fori_loop(0, SIDE * 2, mix(g), 0, unroll=4)
        sums[g] = []
        for r, (place, which) in enumerate(along):
            target = place[0] * 2 + place[1] // 2
            sums[g].append(pltpu.make_async_remote_copy(
                src_ref=mixed.at[g, target], dst_ref=parts.at[g, slot],
                send_sem=chan_send.at[g * 7 + r], recv_sem=chan_recv.at[g * 7 + r],
                device_id=device_at(place, which), device_id_type=MESH))
        for copy in sums[g]:
            copy.start()

    def to_bands(g):
        for copy in sums[g]:
            copy.wait_recv()
        parts[g, slot] = mixed[g, slot]
        value = parts[g, 0].astype(jnp.float32)
        for k in range(1, SIDE * 2):
            value = value + parts[g, k].astype(jnp.float32)
        share[g] = value.astype(jnp.bfloat16).reshape(2 * SIDE, 2 * BINS, lanes)
        moves[g] = []
        for r, (place, which) in enumerate(across):
            moves[g].append(pltpu.make_async_remote_copy(
                src_ref=share.at[g, place[1] % 2 * SIDE + place[2]], dst_ref=bands.at[g, band],
                send_sem=band_send.at[g * 7 + r], recv_sem=band_recv.at[g * 7 + r],
                device_id=device_at(place, which), device_id_type=MESH))
        for copy in moves[g]:
            copy.start()
        bands[g, band] = share[g, band]

    def arrange(g):
        for copy in moves[g]:
            copy.wait_recv()
        wide = (2 * BINS * W, lanes)
        same = lax.broadcasted_iota(jnp.int32, wide, 1) % W == lax.broadcasted_iota(jnp.int32, wide, 0) % W
        tall = (lanes, SRC_BLOCK)
        channel = lax.broadcasted_iota(jnp.int32, tall, 0) // W
        column = lax.broadcasted_iota(jnp.int32, tall, 1)
        value = None
        for b in range(2 * SIDE):
            goal = (channel + (b * channels + SRC_BLOCK) - offset[0]) % SRC_BLOCK
            pick = jnp.where(goal == column, 1.0, 0.0).astype(jnp.bfloat16)
            part = bands[g, b].astype(jnp.float32)
            part = jnp.broadcast_to(part[:, None, :], (2 * BINS, W, lanes)).reshape(wide)
            part = jnp.where(same, part, 0.0).astype(jnp.bfloat16)
            term = jnp.dot(part, pick, preferred_element_type=jnp.float32)
            value = term if value is None else value + term
        spectra[at[0], at[1] // 2, at[1] % 2, at[2], g * wide[0]:(g + 1) * wide[0], :] = value.astype(jnp.bfloat16)

    copies = {}

    def start(turn, stage, part, kind):
        first, low, high, order = PARTS[part]
        first += turn * (PIECE // ROUNDS)
        axis, full = order[stage], order[:stage]
        if kind < 2 or stage < 2:
            ref = slots(spectra, at, full, first, low + high)
        else:
            moved = list(at)
            moved[axis] = lax.rem(at[axis] + (SIDE - 1 if kind == 2 else 1), SIDE)
            ref = slots(spectra, moved, full, first + (0 if kind == 2 else low), low if kind == 2 else high)
        index = ((turn * 3 + stage) * 3 + part) * 4 + kind
        copy = pltpu.make_async_remote_copy(
            src_ref=ref, dst_ref=ref, send_sem=send_sem.at[index], recv_sem=recv_sem.at[index],
            device_id=neighbour(axis, 2 if kind == 2 and stage < 2 else 1 if kind % 2 == 0 else -1),
            device_id_type=MESH)
        copies[turn, stage, part, kind] = copy
        copy.start()

    def begin(turn, stage):
        for part in range(3):
            start(turn, stage, part, 0)
            start(turn, stage, part, 1)
            if stage < 2:
                start(turn, stage, part, 2)

    def forward(turn, stage):
        for part in range(3):
            copies[turn, stage, part, 0].wait_recv()
            start(turn, stage, part, 2)
            copies[turn, stage, part, 1].wait_recv()
            start(turn, stage, part, 3)

    def finish(turn, stage):
        for part in range(3):
            for kind in (2, 3) if stage == 2 else (0, 1, 2):
                copies[turn, stage, part, kind].wait_recv()

    def multiply(turn):
        def step(index, _):
            results = []
            for h in range(2):
                k = index * 2 + h
                s = spectra[k // 16, k // 8 % 2, k // 4 % 2, k % 4, turn * 256:(turn + 1) * 256, :]
                right = jnp.concatenate([s, jnp.concatenate([-s[R2:], s[:R2]], axis=0)], axis=1)
                results.append(jnp.dot(left[turn, k], right, preferred_element_type=jnp.float32))
            base = pl.multiple_of(index * 32, 32)
            for c in range(2 * channels):
                both = jnp.concatenate([r[c * BINS:(c + 1) * BINS] for r in results], axis=0).astype(jnp.bfloat16)
                cross[pl.ds(base, 16), c * SRC_BLOCK:(c + 1) * SRC_BLOCK] = both[:, :SRC_BLOCK]
                cross[pl.ds(base + 16, 16), c * SRC_BLOCK:(c + 1) * SRC_BLOCK] = both[:, SRC_BLOCK:]
            return 0

        return step

    group = 8
    width = group * SRC_BLOCK

    def sum_lags(turn, core_index, store):
        def step(n, _):
            both = pl.ds(pl.multiple_of(core_index * columns + n * width, width), width)
            value = jnp.dot(table[:, turn * 1024:(turn + 1) * 1024], cross[:, both],
                            preferred_element_type=jnp.float32)
            for i in range(group):
                store(n * group + i, core_index * channels + n * group + i,
                      value[:, i * SRC_BLOCK:(i + 1) * SRC_BLOCK])
            return 0

        lax.fori_loop(0, channels // group, step, 0)

    def keep(c, held_c, value):
        total[held_c] = value

    def hand_over(c, held_c, value):
        outgoing[c] = ((total[held_c] + value) * FACTOR).astype(jnp.bfloat16)

    def conclude(c, held_c, value):
        total[held_c] = total[held_c] + value

    pairs = SLOTS // 2
    lax.fori_loop(8, SLOTS, spread(0), 0)
    to_bands(0)
    lax.fori_loop(0, 24, spread(1), 0)
    arrange(0)
    begin(0, 0)
    to_bands(1)
    lax.fori_loop(24, 36, spread(1), 0)
    finish(0, 0)
    begin(0, 1)
    arrange(1)
    begin(1, 0)
    lax.fori_loop(36, 56, spread(1), 0)
    finish(0, 1)
    begin(0, 2)
    finish(1, 0)
    begin(1, 1)
    lax.fori_loop(56, SLOTS, spread(1), 0)
    forward(0, 2)
    finish(1, 1)
    begin(1, 2)
    finish(0, 2)
    own_table.wait()
    lax.fori_loop(0, pairs, multiply(0), 0, unroll=2)
    forward(1, 2)
    sum_lags(0, 0, keep)
    sum_lags(0, 1, keep)
    finish(1, 2)
    lax.fori_loop(0, pairs, multiply(1), 0, unroll=2)
    sum_lags(1, 1, hand_over)
    exchange = pltpu.make_async_remote_copy(
        src_ref=outgoing, dst_ref=incoming, send_sem=side_send.at[2], recv_sem=side_recv.at[2],
        device_id=sibling, device_id_type=MESH)
    exchange.start()
    sum_lags(1, 0, conclude)
    exchange.wait_recv()

    diagonal = (lax.broadcasted_iota(jnp.int32, (LAGS, LAGS), 0) == lax.broadcasted_iota(jnp.int32, (LAGS, LAGS), 1))
    unit = jnp.where(diagonal, 1.0, 0.0).astype(jnp.bfloat16)
    last = (((1,), (1,)), ((), ()))
    for c in range(channels):
        value = (total[c] * FACTOR + incoming[c].astype(jnp.float32)).astype(jnp.bfloat16)
        value = lax.dot_general(unit[:SRC_BLOCK, :SRC_BLOCK], value, last, preferred_element_type=jnp.float32)
        for half in range(2):
            turned[half, pl.ds(c, SRC_BLOCK, stride=channels), :] = value[:, half * R2:(half + 1) * R2]

    def pack(index):
        picked = pl.ds(pl.multiple_of(index * 256, 256), 256)
        return jnp.concatenate([turned[0, picked, :], turned[1, picked, :]], axis=1).astype(jnp.bfloat16)

    ships = []
    for r, (place, which) in enumerate(across):
        index = place[1] % 2 * SIDE + place[2]
        shipped[index] = pack(index)
        ship = pltpu.make_async_remote_copy(
            src_ref=shipped.at[index], dst_ref=landed.at[band], send_sem=ship_send.at[r], recv_sem=ship_recv.at[r],
            device_id=device_at(place, which), device_id_type=MESH)
        ship.start()
        ships.append(ship)
    landed[band] = pack(band)
    for ship in ships:
        ship.wait_recv()
    for s in range(SRC_BLOCK // (2 * SIDE)):
        value = landed[:, s * channels:(s + 1) * channels, :].reshape(2 * SIDE * channels, LAGS)
        out[s] = lax.dot_general(unit, value, last, preferred_element_type=jnp.float32).astype(out.dtype)

    for copy in swaps + [exchange] + sums[0] + sums[1] + moves[0] + moves[1] + ships + list(copies.values()):
        copy.wait_send()


def body(strain, source_block, source_offset, window_valid):
    channels = strain.shape[0]
    lanes = channels * W
    columns = channels * SRC_BLOCK
    tiles = strain.reshape(channels // BINS, BINS, -1, R2).transpose(0, 2, 1, 3).reshape(-1, R2)
    copies = ROUNDS * 3 * 3 * 4
    anywhere = pl.BlockSpec(memory_space=pl.ANY)
    scalars = pl.BlockSpec(memory_space=pltpu.SMEM)
    dma = pltpu.SemaphoreType.DMA
    bf16, f32 = jnp.bfloat16, jnp.float32
    return pl.pallas_call(
        kernel,
        in_specs=[anywhere] * 4 + [scalars] * 3,
        out_specs=pl.BlockSpec(memory_space=pltpu.VMEM),
        out_shape=jax.ShapeDtypeStruct((SRC_BLOCK // (2 * SIDE), LAGS, 2 * SIDE * channels), bf16),
        scratch_shapes=[
            pltpu.VMEM(tiles.shape, f32),
            pltpu.VMEM((3 * R1, R2), f32),
            pltpu.VMEM((R2, 2 * R2), bf16),
            pltpu.VMEM((LAGS, NF), bf16),
            pltpu.VMEM((3, 2, SIDE * 2, R2, lanes), bf16),
            pltpu.VMEM((2, SIDE * 2, R2, lanes), bf16),
            pltpu.VMEM((2, SIDE * 2, R2, lanes), bf16),
            pltpu.VMEM((2, SIDE * 2, 2 * BINS, lanes), bf16),
            pltpu.VMEM((2, SIDE * 2, 2 * BINS, lanes), bf16),
            pltpu.VMEM((SIDE, 2, 2, SIDE, PIECE, SRC_BLOCK), bf16),
            pltpu.VMEM((2, SLOTS, 256, 256), bf16),
            pltpu.VMEM((NF // 2, 2 * columns), bf16),
            pltpu.VMEM((2 * channels, LAGS, SRC_BLOCK), f32),
            pltpu.VMEM((channels, LAGS, SRC_BLOCK), bf16),
            pltpu.VMEM((channels, LAGS, SRC_BLOCK), bf16),
            pltpu.VMEM((2, columns, R2), f32),
            pltpu.VMEM((2 * SIDE, 256, LAGS), bf16),
            pltpu.VMEM((2 * SIDE, 256, LAGS), bf16),
            dma((4,)), dma((copies,)), dma((copies,)), dma((3,)), dma((3,)),
            dma((14,)), dma((14,)), dma((14,)), dma((14,)), dma((7,)), dma((7,)),
        ],
        compiler_params=pltpu.CompilerParams(
            vmem_limit_bytes=62 * 2**20, collective_id=1, has_side_effects=True),
        cost_estimate=pl.CostEstimate(flops=4 * 256 * 4096 * 2048, bytes_accessed=20 * 2**20, transcendentals=0),
    )(tiles, jnp.asarray(row_tables()), jnp.asarray(short_dft(), dtype=bf16),
      jnp.asarray(lag_table(), dtype=bf16), source_block, source_offset, window_valid)


def solution(mesh):
    in_specs = (P(("chan", "band"), None), P(), P(), P())
    out_specs = P("band", None, "chan")
    return jax.shard_map(body, mesh=mesh, in_specs=in_specs, out_specs=out_specs, check_vma=False)
```

```python
import functools
import math

import jax
import jax.numpy as jnp
import numpy as np
from jax import lax
from jax.experimental import pallas as pl
from jax.experimental.pallas import tpu as pltpu
from jax.sharding import PartitionSpec as P

L = 4096
HOP = 2048
NF = 2048
W = 16
SRC_BLOCK = 128
LAGS = 256
R1 = 32
R2 = 128
HALF = R2 // 2
BINS = 8
FACTOR = 1.0 / (W * math.sqrt(NF))


def window_table():
    points = np.arange(L, dtype=np.float32)
    angle = (points * np.float32(2.0 * math.pi / L)).astype(np.float32)
    return (np.float32(0.5) - np.float32(0.5) * np.cos(angle)).astype(np.float32).reshape(R1, R2)


def row_tables():
    angle = 2.0 * np.pi * np.outer(np.arange(R1), np.arange(R2)) / L
    return np.concatenate([window_table(), np.cos(angle), -np.sin(angle)], axis=0).astype(np.float32)


def short_dft():
    angle = 2.0 * np.pi * (np.outer(np.arange(HALF), np.arange(R2)) % R2) / R2
    cosine, sine = np.cos(angle), np.sin(angle)
    top = np.concatenate([cosine, sine], axis=1)
    low = np.concatenate([-sine, cosine], axis=1)
    both = np.stack([top.reshape(-1, BINS, 2 * R2), low.reshape(-1, BINS, 2 * R2)], axis=1)
    return both.reshape(R2, 2 * R2).astype(np.float32)


def lag_table():
    core, g, x, y_hi, y_lo, z_hi, z_lo, i = np.ix_(*[np.arange(n) for n in (2, 2, 4, 2, 2, 2, 2, 8)])
    bins = 8 * x + 4 * y_hi + 2 * core + g + R1 * (32 * y_lo + 8 * (2 * z_hi + z_lo) + i)
    lags = (np.arange(LAGS) - LAGS // 2).reshape((1, LAGS) + (1,) * 7)
    angle = 2.0 * np.pi * (lags * bins[:, None] % L) / L
    table = np.stack([np.cos(angle), -np.sin(angle)], axis=7)
    return table.reshape(2, LAGS, NF).astype(np.float32)


def real_dft(x):
    n = len(x)
    if n == 2:
        return [(x[0] + x[1], None), (x[0] - x[1], None)]
    even, odd = real_dft(x[0::2]), real_dft(x[1::2])
    out = [None] * (n // 2 + 1)
    for k in range(n // 4 + 1):
        er, ei = even[k]
        orr, oi = odd[k]
        if k == 0:
            out[0] = (er + orr, None)
            out[n // 2] = (er - orr, None)
            continue
        if 4 * k == n:
            out[k] = (er, -orr)
            continue
        c, s = math.cos(2 * math.pi * k / n), -math.sin(2 * math.pi * k / n)
        if oi is None:
            tr, ti = orr * c, orr * s
        else:
            tr, ti = orr * c - oi * s, orr * s + oi * c
        zi = ti if ei is None else ei + ti
        yi = -ti if ei is None else ei - ti
        out[k] = (er + tr, zi)
        out[n // 2 - k] = (er - tr, -yi)
    return out


SIDE = 4
SLOTS = SIDE ** 3
PIECE = 2 * 2 * BINS * W
PARTS = (((0, 96, (0, 1, 2)), (96, 80, (1, 2, 0)), (176, 80, (2, 0, 1))),
         ((0, 80, (0, 1, 2)), (80, 96, (1, 2, 0)), (176, 80, (2, 0, 1))))
LINES = (0, -1, 1, 2)
ROUNDS = 2
MESH = pl.DeviceIdType.MESH


def position():
    chan, band = lax.axis_index("chan"), lax.axis_index("band")
    return (chan // 4, chan // 2 % 2 * 2 + band // 4, band % 4), chan % 2


def device_at(at, core):
    x, y, z = at
    return (x * 4 + y // 2 * 2 + core, y % 2 * 4 + z)


def neighbour(axis, step):
    at, core = position()
    moved = list(at)
    moved[axis] = lax.rem(at[axis] + step + SIDE, SIDE)
    return device_at(moved, core)


def slots(ref, at, full, first, count):
    whole = slice(None)
    x = whole if 0 in full else at[0]
    y_hi, y_lo = (whole, whole) if 1 in full else (at[1] // 2, at[1] % 2)
    z = whole if 2 in full else at[2]
    return ref.at[x, y_hi, y_lo, z, pl.ds(first, count), :]


def partners(at, core):
    x, y, z = at
    side = lambda step: lax.rem(z + step, SIDE)
    along = [((lax.rem(x + dx, SIDE), y ^ (2 * dy), z), core) for dx in (2, 1, 3, 0) for dy in (1, 0)][:-1]
    across = [((x, y ^ dy, side(dz)), core) for dz in (2, 1, 3, 0) for dy in (1, 0)][:-1]
    return along, across, [((x, y ^ 3, z), core), (at, 1 - core)]


def kernel(strain_hbm, rows_hbm, dft_hbm, tables, block, offset, valid, out,
           strain, rows, dft, table, held, mixed, parts, share, bands, spectra, left, cross, total,
           outgoing, incoming, turned, shipped, landed,
           local_sem, send_sem, recv_sem, side_send, side_recv, chan_send, chan_recv, band_send, band_recv,
           ship_send, ship_recv):
    at, core = position()
    chan, band = lax.axis_index("chan"), lax.axis_index("band")
    sibling = device_at(at, 1 - core)
    lanes = held.shape[-1]
    channels = lanes // W
    columns = channels * SRC_BLOCK
    along, across, rest = partners(at, core)

    def fetch(src, dst, index):
        copy = pltpu.make_async_copy(src, dst, local_sem.at[index])
        copy.start()
        return copy

    fetched = [fetch(strain_hbm, strain, 0), fetch(rows_hbm, rows, 1), fetch(dft_hbm, dft, 2)]
    own_table = fetch(tables.at[core], table, 3)
    barrier = pltpu.get_barrier_semaphore()
    for place, which in along + across + rest:
        pl.semaphore_signal(barrier, inc=1, device_id=device_at(place, which), device_id_type=MESH)
    for copy in fetched:
        copy.wait()

    folded = left.at[0]

    def fold(c, _):
        first = c // BINS * (BINS * (W + 1) * W) + c % BINS
        x = [strain[pl.ds(first + BINS * k, W, stride=BINS * W), :] for k in range(R1)]
        whole = x[0]
        for k in range(1, R1):
            whole = whole + x[k]
        mean = jnp.sum(whole, axis=1, keepdims=True) * (1.0 / L)
        x = [((x[k] - mean) * rows[k:k + 1, :]).astype(jnp.bfloat16).astype(jnp.float32) for k in range(R1)]
        bins = real_dft(x)
        to = pl.ds(pl.multiple_of(c * W, W), W)
        for f in range(R1):
            re, im = bins[f] if f <= R1 // 2 else bins[R1 - f]
            cosine, sine = rows[R1 + f:R1 + f + 1, :], rows[2 * R1 + f:2 * R1 + f + 1, :]
            if im is None:
                gr, gi = re * cosine, re * sine
            else:
                im = im if f <= R1 // 2 else -im
                gr, gi = re * cosine - im * sine, re * sine + im * cosine
            folded[f, to, :R2] = gr.astype(jnp.bfloat16)
            folded[f, to, R2:] = gi.astype(jnp.bfloat16)
        return 0

    lax.fori_loop(0, channels, fold, 0, unroll=2)
    dft_table = dft[...]

    def transform(f, power):
        y = lax.dot_general(dft_table, folded[f], (((1,), (1,)), ((), ())), preferred_element_type=jnp.float32)
        total[f, :R2, :] = y[:, :R2]
        total[f, R2:, :] = y[:, R2:]
        square = (y * y).reshape(HALF // BINS, 2, BINS, lanes)
        return power + (square[:, 0] + square[:, 1]).reshape(HALF, lanes)

    power = lax.fori_loop(0, R1, transform, jnp.zeros((HALF, lanes), jnp.float32), unroll=8)
    scales = []
    for b in range(HALF // BINS):
        mean = jnp.sum(power[b * BINS:(b + 1) * BINS], axis=0, keepdims=True) * (1.0 / 256.0)
        scales.append(jnp.broadcast_to(lax.rsqrt(mean + 1e-06), (2 * BINS, lanes)))
    scale = jnp.concatenate(scales, axis=0)

    def finish_white(to, which, g):
        def step(index, _):
            f = index * 4 + which * 2 + g
            y = jnp.concatenate([total[f, :R2, :], total[f, R2:, :]], axis=1)
            held[to, g, index] = (y * scale).astype(jnp.bfloat16)
            return 0

        lax.fori_loop(0, SIDE * 2, step, 0, unroll=4)

    for g in range(2):
        finish_white(2, 1 - core, g)
    pl.semaphore_wait(barrier, len(along) + len(across) + len(rest))
    swaps = []
    for g in range(2):
        swap = pltpu.make_async_remote_copy(
            src_ref=held.at[2, g], dst_ref=held.at[1, g], send_sem=side_send.at[g], recv_sem=side_recv.at[g],
            device_id=sibling, device_id_type=MESH)
        swap.start()
        swaps.append(swap)
    for g in range(2):
        finish_white(0, core, g)

    row = lax.broadcasted_iota(jnp.int32, (2 * BINS, R2), 0) % BINS
    lane = lax.broadcasted_iota(jnp.int32, (2 * BINS, R2), 1)
    own = lane // W == row

    def spread(core_index):
        def step(index, _):
            x, y_hi, y_lo, z = index // 16, index // 8 % 2, index // 4 % 2, index % 4
            picked = pl.ds(pl.multiple_of((y_lo * SIDE + z) * 16, 16), 16)
            for g in range(2):
                for k in range(channels // 8):
                    value = held[core_index, g, x * 2 + y_hi, picked, k * R2:(k + 1) * R2].astype(jnp.float32)
                    for ri in range(2):
                        even = pltpu.roll(value[ri * BINS:(ri + 1) * BINS], 0, 1, stride=W, stride_axis=0)
                        both = jnp.concatenate([even, pltpu.roll(even, R2 - W, 1)], axis=0)
                        for t in range(4):
                            moved = pltpu.roll(both, R2 - 2 * W * t, 1) if t else both
                            first = ((core_index * channels // 8 + k) * 4 + t) * 2 * BINS
                            left[g, index, first:first + 2 * BINS, ri * R2:(ri + 1) * R2] = jnp.where(
                                own, moved, 0.0).astype(jnp.bfloat16)
            return 0

        return step

    lax.fori_loop(0, 8, spread(0), 0)

    spot = lax.broadcasted_iota(jnp.int32, (1, lanes), 1)
    source = band * channels + spot // W
    stacked = jnp.zeros((1, lanes), jnp.float32)
    for w in range(W):
        stacked = jnp.where(spot % W == w, jnp.where(valid[w] != 0, 1.0, 0.0), stacked)
    chans = R1 // 2

    def chosen(which):
        first = jnp.where(which == block[0], 1, 0)
        second = jnp.where(which == lax.rem(block[0] + 1, chans), 1, 0)
        taken = jnp.where(source >= offset[0], first, second)
        return jnp.where(taken == 1, stacked, 0.0)

    mine, theirs = chosen(chan), chosen(chan ^ 1)
    slot = chan // 2

    def mix(g):
        def step(index, _):
            a, b = held[0, g, index], held[1, g, index]
            value = a.astype(jnp.float32) * mine + b.astype(jnp.float32) * theirs
            mixed[g, index] = value.astype(jnp.bfloat16)
            return 0

        return step

    sums, moves = {}, {}
    for g in range(2):
        swaps[g].wait_recv()
        lax.fori_loop(0, SIDE * 2, mix(g), 0, unroll=4)
        sums[g] = []
        for r, (place, which) in enumerate(along):
            target = place[0] * 2 + place[1] // 2
            sums[g].append(pltpu.make_async_remote_copy(
                src_ref=mixed.at[g, target], dst_ref=parts.at[g, slot],
                send_sem=chan_send.at[g * 7 + r], recv_sem=chan_recv.at[g * 7 + r],
                device_id=device_at(place, which), device_id_type=MESH))
        for copy in sums[g]:
            copy.start()

    def to_bands(g):
        for copy in sums[g]:
            copy.wait_recv()
        parts[g, slot] = mixed[g, slot]
        value = parts[g, 0].astype(jnp.float32)
        for k in range(1, SIDE * 2):
            value = value + parts[g, k].astype(jnp.float32)
        share[g] = value.astype(jnp.bfloat16).reshape(2 * SIDE, 2 * BINS, lanes)
        moves[g] = []
        for r, (place, which) in enumerate(across):
            moves[g].append(pltpu.make_async_remote_copy(
                src_ref=share.at[g, place[1] % 2 * SIDE + place[2]], dst_ref=bands.at[g, band],
                send_sem=band_send.at[g * 7 + r], recv_sem=band_recv.at[g * 7 + r],
                device_id=device_at(place, which), device_id_type=MESH))
        for copy in moves[g]:
            copy.start()
        bands[g, band] = share[g, band]

    def arrange(g):
        for copy in moves[g]:
            copy.wait_recv()
        wide = (2 * BINS * W, lanes)
        same = lax.broadcasted_iota(jnp.int32, wide, 1) % W == lax.broadcasted_iota(jnp.int32, wide, 0) % W
        tall = (lanes, SRC_BLOCK)
        channel = lax.broadcasted_iota(jnp.int32, tall, 0) // W
        column = lax.broadcasted_iota(jnp.int32, tall, 1)
        value = None
        for b in range(2 * SIDE):
            goal = (channel + (b * channels + SRC_BLOCK) - offset[0]) % SRC_BLOCK
            pick = jnp.where(goal == column, 1.0, 0.0).astype(jnp.bfloat16)
            part = bands[g, b].astype(jnp.float32)
            part = jnp.broadcast_to(part[:, None, :], (2 * BINS, W, lanes)).reshape(wide)
            part = jnp.where(same, part, 0.0).astype(jnp.bfloat16)
            term = jnp.dot(part, pick, preferred_element_type=jnp.float32)
            value = term if value is None else value + term
        spectra[at[0], at[1] // 2, at[1] % 2, at[2], g * wide[0]:(g + 1) * wide[0], :] = value.astype(jnp.bfloat16)

    copies = {}

    def send(key, ref, axis, step):
        index = len(copies)
        copies[key] = pltpu.make_async_remote_copy(
            src_ref=ref, dst_ref=ref, send_sem=send_sem.at[index], recv_sem=recv_sem.at[index],
            device_id=neighbour(axis, step), device_id_type=MESH)
        copies[key].start()

    def shifted(order, line, step):
        moved = list(at)
        for axis, by in ((order[1], LINES[line]), (order[2], step)):
            moved[axis] = lax.rem(at[axis] + by + SIDE, SIDE)
        return moved

    def begin(turn, stage):
        for part, (first, count, order) in enumerate(PARTS[turn]):
            ref = slots(spectra, at, order[:stage], turn * 256 + first, count)
            for kind, step in enumerate((1, -1, 2)):
                send((turn, stage, part, kind), ref, order[stage], step)

    def finish(turn, stage):
        for part in range(3):
            for kind in range(3):
                copies[turn, stage, part, kind].wait_recv()

    def send_line(turn, line):
        for part, (first, count, order) in enumerate(PARTS[turn]):
            if line:
                copies[turn, 1, part, line - 1].wait_recv()
            ref = slots(spectra, shifted(order, line, 0), order[:1], turn * 256 + first, count)
            for kind, step in enumerate((1, -1)):
                send((turn, 2, part, kind, line), ref, order[2], step)

    def forward(turn, line):
        for part, (first, count, order) in enumerate(PARTS[turn]):
            low = (count // 32 + (count // 16) % 2 * (line % 2)) * 16
            shares = ((1, -1, 0, low), (-1, 1, low, count - low))
            for kind, (step, origin, skip, rows_sent) in enumerate(shares):
                copies[turn, 2, part, kind, line].wait_recv()
                ref = slots(spectra, shifted(order, line, origin), order[:1], turn * 256 + first + skip, rows_sent)
                send((turn, 2, part, kind + 2, line), ref, order[2], step)

    def finish_lines(turn):
        for line in range(len(LINES)):
            for part in range(3):
                for kind in (2, 3):
                    copies[turn, 2, part, kind, line].wait_recv()

    def multiply(turn):
        def step(index, _):
            results = []
            for h in range(2):
                k = index * 2 + h
                s = spectra[k // 16, k // 8 % 2, k // 4 % 2, k % 4, turn * 256:(turn + 1) * 256, :]
                right = jnp.concatenate([s, jnp.concatenate([-s[R2:], s[:R2]], axis=0)], axis=1)
                results.append(jnp.dot(left[turn, k], right, preferred_element_type=jnp.float32))
            base = pl.multiple_of(index * 32, 32)
            for c in range(2 * channels):
                both = jnp.concatenate([r[c * BINS:(c + 1) * BINS] for r in results], axis=0).astype(jnp.bfloat16)
                cross[pl.ds(base, 16), c * SRC_BLOCK:(c + 1) * SRC_BLOCK] = both[:, :SRC_BLOCK]
                cross[pl.ds(base + 16, 16), c * SRC_BLOCK:(c + 1) * SRC_BLOCK] = both[:, SRC_BLOCK:]
            return 0

        return step

    group = 8
    width = group * SRC_BLOCK

    def sum_lags(turn, core_index, n, store):
        both = slice(core_index * columns + n * width, core_index * columns + (n + 1) * width)
        value = jnp.dot(table[:, turn * 1024:(turn + 1) * 1024], cross[:, both], preferred_element_type=jnp.float32)
        for i in range(group):
            store(n * group + i, core_index * channels + n * group + i, value[:, i * SRC_BLOCK:(i + 1) * SRC_BLOCK])

    def keep(c, held_c, value):
        total[held_c] = value

    def hand_over(c, held_c, value):
        outgoing[c] = ((total[held_c] + value) * FACTOR).astype(jnp.bfloat16)

    def conclude(c, held_c, value):
        total[held_c] = total[held_c] + value

    pairs = SLOTS // 2
    lax.fori_loop(8, SLOTS, spread(0), 0)
    to_bands(0)
    lax.fori_loop(0, 24, spread(1), 0)
    arrange(0)
    begin(0, 0)
    to_bands(1)
    lax.fori_loop(24, 36, spread(1), 0)
    finish(0, 0)
    begin(0, 1)
    send_line(0, 0)
    arrange(1)
    begin(1, 0)
    lax.fori_loop(36, 44, spread(1), 0)
    for line in (1, 2, 3):
        send_line(0, line)
    finish(1, 0)
    begin(1, 1)
    forward(0, 0)
    send_line(1, 0)
    lax.fori_loop(44, SLOTS, spread(1), 0)
    for line in (1, 2, 3):
        forward(0, line)
        send_line(1, line)
    own_table.wait()
    finish_lines(0)
    quarter = pairs // 4
    for line in range(4):
        lax.fori_loop(line * quarter, (line + 1) * quarter, multiply(0), 0, unroll=2)
        forward(1, line)
    for core_index in range(2):
        for n in range(channels // group):
            sum_lags(0, core_index, n, keep)
    finish_lines(1)
    lax.fori_loop(0, pairs, multiply(1), 0, unroll=2)
    for n in range(channels // group):
        sum_lags(1, 1, n, hand_over)
    exchange = pltpu.make_async_remote_copy(
        src_ref=outgoing, dst_ref=incoming, send_sem=side_send.at[2], recv_sem=side_recv.at[2],
        device_id=sibling, device_id_type=MESH)
    exchange.start()
    for n in range(channels // group):
        sum_lags(1, 0, n, conclude)
    exchange.wait_recv()

    diagonal = (lax.broadcasted_iota(jnp.int32, (LAGS, LAGS), 0) == lax.broadcasted_iota(jnp.int32, (LAGS, LAGS), 1))
    unit = jnp.where(diagonal, 1.0, 0.0).astype(jnp.bfloat16)
    last = (((1,), (1,)), ((), ()))
    for c in range(channels):
        value = (total[c] * FACTOR + incoming[c].astype(jnp.float32)).astype(jnp.bfloat16)
        value = lax.dot_general(unit[:SRC_BLOCK, :SRC_BLOCK], value, last, preferred_element_type=jnp.float32)
        for half in range(2):
            turned[half, pl.ds(c, SRC_BLOCK, stride=channels), :] = value[:, half * R2:(half + 1) * R2]

    def pack(index):
        picked = pl.ds(pl.multiple_of(index * 256, 256), 256)
        return jnp.concatenate([turned[0, picked, :], turned[1, picked, :]], axis=1).astype(jnp.bfloat16)

    ships = []
    for r, (place, which) in enumerate(across):
        index = place[1] % 2 * SIDE + place[2]
        shipped[index] = pack(index)
        ship = pltpu.make_async_remote_copy(
            src_ref=shipped.at[index], dst_ref=landed.at[band], send_sem=ship_send.at[r], recv_sem=ship_recv.at[r],
            device_id=device_at(place, which), device_id_type=MESH)
        ship.start()
        ships.append(ship)
    landed[band] = pack(band)
    for ship in ships:
        ship.wait_recv()
    for s in range(SRC_BLOCK // (2 * SIDE)):
        value = landed[:, s * channels:(s + 1) * channels, :].reshape(2 * SIDE * channels, LAGS)
        out[s] = lax.dot_general(unit, value, last, preferred_element_type=jnp.float32).astype(out.dtype)

    for copy in swaps + [exchange] + sums[0] + sums[1] + moves[0] + moves[1] + ships + list(copies.values()):
        copy.wait_send()


def body(strain, source_block, source_offset, window_valid):
    channels = strain.shape[0]
    lanes = channels * W
    columns = channels * SRC_BLOCK
    tiles = strain.reshape(channels // BINS, BINS, -1, R2).transpose(0, 2, 1, 3).reshape(-1, R2)
    copies = ROUNDS * 3 * (3 + 3 + 4 * len(LINES))
    anywhere = pl.BlockSpec(memory_space=pl.ANY)
    scalars = pl.BlockSpec(memory_space=pltpu.SMEM)
    dma = pltpu.SemaphoreType.DMA
    bf16, f32 = jnp.bfloat16, jnp.float32
    return pl.pallas_call(
        kernel,
        in_specs=[anywhere] * 4 + [scalars] * 3,
        out_specs=pl.BlockSpec(memory_space=pltpu.VMEM),
        out_shape=jax.ShapeDtypeStruct((SRC_BLOCK // (2 * SIDE), LAGS, 2 * SIDE * channels), bf16),
        scratch_shapes=[
            pltpu.VMEM(tiles.shape, f32),
            pltpu.VMEM((3 * R1, R2), f32),
            pltpu.VMEM((R2, 2 * R2), bf16),
            pltpu.VMEM((LAGS, NF), bf16),
            pltpu.VMEM((3, 2, SIDE * 2, R2, lanes), bf16),
            pltpu.VMEM((2, SIDE * 2, R2, lanes), bf16),
            pltpu.VMEM((2, SIDE * 2, R2, lanes), bf16),
            pltpu.VMEM((2, SIDE * 2, 2 * BINS, lanes), bf16),
            pltpu.VMEM((2, SIDE * 2, 2 * BINS, lanes), bf16),
            pltpu.VMEM((SIDE, 2, 2, SIDE, PIECE, SRC_BLOCK), bf16),
            pltpu.VMEM((2, SLOTS, 256, 256), bf16),
            pltpu.VMEM((NF // 2, 2 * columns), bf16),
            pltpu.VMEM((2 * channels, LAGS, SRC_BLOCK), f32),
            pltpu.VMEM((channels, LAGS, SRC_BLOCK), bf16),
            pltpu.VMEM((channels, LAGS, SRC_BLOCK), bf16),
            pltpu.VMEM((2, columns, R2), f32),
            pltpu.VMEM((2 * SIDE, 256, LAGS), bf16),
            pltpu.VMEM((2 * SIDE, 256, LAGS), bf16),
            dma((4,)), dma((copies,)), dma((copies,)), dma((3,)), dma((3,)),
            dma((14,)), dma((14,)), dma((14,)), dma((14,)), dma((7,)), dma((7,)),
        ],
        compiler_params=pltpu.CompilerParams(
            vmem_limit_bytes=62 * 2**20, collective_id=1, has_side_effects=True),
        cost_estimate=pl.CostEstimate(flops=4 * 256 * 4096 * 2048, bytes_accessed=20 * 2**20, transcendentals=0),
    )(tiles, jnp.asarray(row_tables()), jnp.asarray(short_dft(), dtype=bf16),
      jnp.asarray(lag_table(), dtype=bf16), source_block, source_offset, window_valid)


def solution(mesh):
    in_specs = (P(("chan", "band"), None), P(), P(), P())
    out_specs = P("band", None, "chan")
    return jax.shard_map(body, mesh=mesh, in_specs=in_specs, out_specs=out_specs, check_vma=False)
```

```python
import functools
import math

import jax
import jax.numpy as jnp
import numpy as np
from jax import lax
from jax.experimental import pallas as pl
from jax.experimental.pallas import tpu as pltpu
from jax.sharding import PartitionSpec as P

L = 4096
HOP = 2048
NF = 2048
W = 16
SRC_BLOCK = 128
LAGS = 256
R1 = 32
R2 = 128
HALF = R2 // 2
BINS = 8
FACTOR = 1.0 / (W * math.sqrt(NF))


def window_table():
    points = np.arange(L, dtype=np.float32)
    angle = (points * np.float32(2.0 * math.pi / L)).astype(np.float32)
    return (np.float32(0.5) - np.float32(0.5) * np.cos(angle)).astype(np.float32).reshape(R1, R2)


def row_tables():
    angle = 2.0 * np.pi * np.outer(np.arange(R1), np.arange(R2)) / L
    return np.concatenate([window_table(), np.cos(angle), -np.sin(angle)], axis=0).astype(np.float32)


def short_dft():
    angle = 2.0 * np.pi * (np.outer(np.arange(HALF), np.arange(R2)) % R2) / R2
    cosine, sine = np.cos(angle), np.sin(angle)
    top = np.concatenate([cosine, sine], axis=1)
    low = np.concatenate([-sine, cosine], axis=1)
    both = np.stack([top.reshape(-1, BINS, 2 * R2), low.reshape(-1, BINS, 2 * R2)], axis=1)
    return both.reshape(R2, 2 * R2).astype(np.float32)


def lag_table():
    core, g, x, y_hi, y_lo, z, i = np.ix_(*[np.arange(n) for n in (2, 2, 4, 2, 2, 4, 8)])
    bins = 8 * x + 4 * y_hi + 2 * core + g + R1 * (32 * y_lo + 8 * z + i)
    lags = (np.arange(LAGS) - LAGS // 2).reshape((1, LAGS) + (1,) * 6)
    angle = 2.0 * np.pi * (lags * bins[:, None] % L) / L
    table = np.stack([np.cos(angle), -np.sin(angle)], axis=7)
    return table.reshape(2, LAGS, NF).astype(np.float32)


def real_dft(x):
    n = len(x)
    if n == 2:
        return [(x[0] + x[1], None), (x[0] - x[1], None)]
    even, odd = real_dft(x[0::2]), real_dft(x[1::2])
    out = [None] * (n // 2 + 1)
    for k in range(n // 4 + 1):
        er, ei = even[k]
        orr, oi = odd[k]
        if k == 0:
            out[0] = (er + orr, None)
            out[n // 2] = (er - orr, None)
            continue
        if 4 * k == n:
            out[k] = (er, -orr)
            continue
        c, s = math.cos(2 * math.pi * k / n), -math.sin(2 * math.pi * k / n)
        if oi is None:
            tr, ti = orr * c, orr * s
        else:
            tr, ti = orr * c - oi * s, orr * s + oi * c
        zi = ti if ei is None else ei + ti
        yi = -ti if ei is None else ei - ti
        out[k] = (er + tr, zi)
        out[n // 2 - k] = (er - tr, -yi)
    return out


SIDE = 4
SLOTS = SIDE ** 3
PIECE = 2 * 2 * BINS * W
PARTS = (((0, 96, (0, 1, 2)), (96, 80, (1, 2, 0)), (176, 80, (2, 0, 1))),
         ((0, 80, (0, 1, 2)), (80, 96, (1, 2, 0)), (176, 80, (2, 0, 1))))
LINES = (0, -1, 1, 2)
ROUNDS = 2
MESH = pl.DeviceIdType.MESH


def position():
    chan, band = lax.axis_index("chan"), lax.axis_index("band")
    return (chan // 4, chan // 2 % 2 * 2 + band // 4, band % 4), chan % 2


def device_at(at, core):
    x, y, z = at
    return (x * 4 + y // 2 * 2 + core, y % 2 * 4 + z)


def neighbour(axis, step):
    at, core = position()
    moved = list(at)
    moved[axis] = lax.rem(at[axis] + step + SIDE, SIDE)
    return device_at(moved, core)


def slots(ref, at, full, first, count):
    whole = slice(None)
    x = whole if 0 in full else at[0]
    y_hi, y_lo = (whole, whole) if 1 in full else (at[1] // 2, at[1] % 2)
    z = whole if 2 in full else at[2]
    return ref.at[x, y_hi, y_lo, z, pl.ds(first, count), :]


def partners(at, core):
    x, y, z = at
    side = lambda step: lax.rem(z + step, SIDE)
    along = [((lax.rem(x + dx, SIDE), y ^ (2 * dy), z), core) for dx in (2, 1, 3, 0) for dy in (1, 0)][:-1]
    across = [((x, y ^ dy, side(dz)), core) for dz in (2, 1, 3, 0) for dy in (1, 0)][:-1]
    return along, across, [((x, y ^ 3, z), core), (at, 1 - core)]


def kernel(strain_hbm, rows_hbm, dft_hbm, tables, block, offset, valid, landed,
           strain, rows, dft, table, held, mixed, parts, share, bands, spectra, left, cross, total,
           outgoing, incoming, turned, shipped,
           local_sem, send_sem, recv_sem, side_send, side_recv, chan_send, chan_recv, band_send, band_recv,
           ship_send, ship_recv):
    at, core = position()
    chan, band = lax.axis_index("chan"), lax.axis_index("band")
    sibling = device_at(at, 1 - core)
    lanes = held.shape[-1]
    channels = lanes // W
    columns = channels * SRC_BLOCK
    along, across, rest = partners(at, core)

    def fetch(src, dst, index):
        copy = pltpu.make_async_copy(src, dst, local_sem.at[index])
        copy.start()
        return copy

    fetched = [fetch(strain_hbm, strain, 0), fetch(rows_hbm, rows, 1), fetch(dft_hbm, dft, 2)]
    own_table = fetch(tables.at[core], table, 3)
    barrier = pltpu.get_barrier_semaphore()
    for place, which in along + across + rest:
        pl.semaphore_signal(barrier, inc=1, device_id=device_at(place, which), device_id_type=MESH)
    for copy in fetched:
        copy.wait()

    folded = left.at[0]

    def fold(c, _):
        first = c // BINS * (BINS * (W + 1) * W) + c % BINS
        x = [strain[pl.ds(first + BINS * k, W, stride=BINS * W), :] for k in range(R1)]
        whole = x[0]
        for k in range(1, R1):
            whole = whole + x[k]
        mean = jnp.sum(whole, axis=1, keepdims=True) * (1.0 / L)
        x = [((x[k] - mean) * rows[k:k + 1, :]).astype(jnp.bfloat16).astype(jnp.float32) for k in range(R1)]
        bins = real_dft(x)
        to = pl.ds(pl.multiple_of(c * W, W), W)
        for f in range(R1):
            re, im = bins[f] if f <= R1 // 2 else bins[R1 - f]
            cosine, sine = rows[R1 + f:R1 + f + 1, :], rows[2 * R1 + f:2 * R1 + f + 1, :]
            if im is None:
                gr, gi = re * cosine, re * sine
            else:
                im = im if f <= R1 // 2 else -im
                gr, gi = re * cosine - im * sine, re * sine + im * cosine
            folded[f, to, :R2] = gr.astype(jnp.bfloat16)
            folded[f, to, R2:] = gi.astype(jnp.bfloat16)
        return 0

    lax.fori_loop(0, channels, fold, 0, unroll=2)
    dft_table = dft[...]

    def transform(f, power):
        y = lax.dot_general(dft_table, folded[f], (((1,), (1,)), ((), ())), preferred_element_type=jnp.float32)
        total[f, :R2, :] = y[:, :R2]
        total[f, R2:, :] = y[:, R2:]
        square = (y * y).reshape(HALF // BINS, 2, BINS, lanes)
        return power + (square[:, 0] + square[:, 1]).reshape(HALF, lanes)

    power = lax.fori_loop(0, R1, transform, jnp.zeros((HALF, lanes), jnp.float32), unroll=8)
    scales = []
    for b in range(HALF // BINS):
        mean = jnp.sum(power[b * BINS:(b + 1) * BINS], axis=0, keepdims=True) * (1.0 / 256.0)
        scales.append(jnp.broadcast_to(lax.rsqrt(mean + 1e-06), (2 * BINS, lanes)))
    scale = jnp.concatenate(scales, axis=0)

    def finish_white(to, which, g):
        def step(index, _):
            f = index * 4 + which * 2 + g
            y = jnp.concatenate([total[f, :R2, :], total[f, R2:, :]], axis=1)
            held[to, g, index] = (y * scale).astype(jnp.bfloat16)
            return 0

        lax.fori_loop(0, SIDE * 2, step, 0, unroll=4)

    for g in range(2):
        finish_white(2, 1 - core, g)
    pl.semaphore_wait(barrier, len(along) + len(across) + len(rest))
    swaps = []
    for g in range(2):
        swap = pltpu.make_async_remote_copy(
            src_ref=held.at[2, g], dst_ref=held.at[1, g], send_sem=side_send.at[g], recv_sem=side_recv.at[g],
            device_id=sibling, device_id_type=MESH)
        swap.start()
        swaps.append(swap)
    for g in range(2):
        finish_white(0, core, g)

    row = lax.broadcasted_iota(jnp.int32, (2 * BINS, R2), 0) % BINS
    lane = lax.broadcasted_iota(jnp.int32, (2 * BINS, R2), 1)
    own = lane // W == row

    def spread(core_index):
        def step(index, _):
            x, y_hi, y_lo, z = index // 16, index // 8 % 2, index // 4 % 2, index % 4
            picked = pl.ds(pl.multiple_of((y_lo * SIDE + z) * 16, 16), 16)
            for g in range(2):
                for k in range(channels // 8):
                    value = held[core_index, g, x * 2 + y_hi, picked, k * R2:(k + 1) * R2].astype(jnp.float32)
                    for ri in range(2):
                        even = pltpu.roll(value[ri * BINS:(ri + 1) * BINS], 0, 1, stride=W, stride_axis=0)
                        both = jnp.concatenate([even, pltpu.roll(even, R2 - W, 1)], axis=0)
                        for t in range(4):
                            moved = pltpu.roll(both, R2 - 2 * W * t, 1) if t else both
                            first = ((core_index * channels // 8 + k) * 4 + t) * 2 * BINS
                            left[g, index, first:first + 2 * BINS, ri * R2:(ri + 1) * R2] = jnp.where(
                                own, moved, 0.0).astype(jnp.bfloat16)
            return 0

        return step

    lax.fori_loop(0, 8, spread(0), 0)

    spot = lax.broadcasted_iota(jnp.int32, (1, lanes), 1)
    source = band * channels + spot // W
    stacked = jnp.zeros((1, lanes), jnp.float32)
    for w in range(W):
        stacked = jnp.where(spot % W == w, jnp.where(valid[w] != 0, 1.0, 0.0), stacked)
    chans = R1 // 2

    def chosen(which):
        first = jnp.where(which == block[0], 1, 0)
        second = jnp.where(which == lax.rem(block[0] + 1, chans), 1, 0)
        taken = jnp.where(source >= offset[0], first, second)
        return jnp.where(taken == 1, stacked, 0.0)

    mine, theirs = chosen(chan), chosen(chan ^ 1)
    slot = chan // 2

    def mix(g):
        def step(index, _):
            a, b = held[0, g, index], held[1, g, index]
            value = a.astype(jnp.float32) * mine + b.astype(jnp.float32) * theirs
            mixed[g, index] = value.astype(jnp.bfloat16)
            return 0

        return step

    sums, moves = {}, {}
    for g in range(2):
        swaps[g].wait_recv()
        lax.fori_loop(0, SIDE * 2, mix(g), 0, unroll=4)
        sums[g] = []
        for r, (place, which) in enumerate(along):
            target = place[0] * 2 + place[1] // 2
            sums[g].append(pltpu.make_async_remote_copy(
                src_ref=mixed.at[g, target], dst_ref=parts.at[g, slot],
                send_sem=chan_send.at[g * 7 + r], recv_sem=chan_recv.at[g * 7 + r],
                device_id=device_at(place, which), device_id_type=MESH))
        for copy in sums[g]:
            copy.start()

    def to_bands(g):
        for copy in sums[g]:
            copy.wait_recv()
        parts[g, slot] = mixed[g, slot]
        value = parts[g, 0].astype(jnp.float32)
        for k in range(1, SIDE * 2):
            value = value + parts[g, k].astype(jnp.float32)
        share[g] = value.astype(jnp.bfloat16).reshape(2 * SIDE, 2 * BINS, lanes)
        moves[g] = []
        for r, (place, which) in enumerate(across):
            moves[g].append(pltpu.make_async_remote_copy(
                src_ref=share.at[g, place[1] % 2 * SIDE + place[2]], dst_ref=bands.at[g, band],
                send_sem=band_send.at[g * 7 + r], recv_sem=band_recv.at[g * 7 + r],
                device_id=device_at(place, which), device_id_type=MESH))
        for copy in moves[g]:
            copy.start()
        bands[g, band] = share[g, band]

    def arrange(g):
        for copy in moves[g]:
            copy.wait_recv()
        wide = (2 * BINS * W, lanes)
        same = lax.broadcasted_iota(jnp.int32, wide, 1) % W == lax.broadcasted_iota(jnp.int32, wide, 0) % W
        tall = (lanes, SRC_BLOCK)
        channel = lax.broadcasted_iota(jnp.int32, tall, 0) // W
        column = lax.broadcasted_iota(jnp.int32, tall, 1)
        value = None
        for b in range(2 * SIDE):
            goal = (channel + (b * channels + SRC_BLOCK) - offset[0]) % SRC_BLOCK
            pick = jnp.where(goal == column, 1.0, 0.0).astype(jnp.bfloat16)
            part = bands[g, b].astype(jnp.float32)
            part = jnp.broadcast_to(part[:, None, :], (2 * BINS, W, lanes)).reshape(wide)
            part = jnp.where(same, part, 0.0).astype(jnp.bfloat16)
            term = jnp.dot(part, pick, preferred_element_type=jnp.float32)
            value = term if value is None else value + term
        spectra[at[0], at[1] // 2, at[1] % 2, at[2], g * wide[0]:(g + 1) * wide[0], :] = value.astype(jnp.bfloat16)

    copies = {}

    def send(key, ref, axis, step):
        index = len(copies)
        copies[key] = pltpu.make_async_remote_copy(
            src_ref=ref, dst_ref=ref, send_sem=send_sem.at[index], recv_sem=recv_sem.at[index],
            device_id=neighbour(axis, step), device_id_type=MESH)
        copies[key].start()

    def shifted(order, line, step):
        moved = list(at)
        for axis, by in ((order[1], LINES[line]), (order[2], step)):
            moved[axis] = lax.rem(at[axis] + by + SIDE, SIDE)
        return moved

    def begin(turn, stage):
        for part, (first, count, order) in enumerate(PARTS[turn]):
            ref = slots(spectra, at, order[:stage], turn * 256 + first, count)
            for kind, step in enumerate((1, -1, 2)):
                send((turn, stage, part, kind), ref, order[stage], step)

    def finish(turn, stage):
        for part in range(3):
            for kind in range(3):
                copies[turn, stage, part, kind].wait_recv()

    def send_line(turn, line):
        for part, (first, count, order) in enumerate(PARTS[turn]):
            if line:
                copies[turn, 1, part, line - 1].wait_recv()
            ref = slots(spectra, shifted(order, line, 0), order[:1], turn * 256 + first, count)
            for kind, step in enumerate((1, -1)):
                send((turn, 2, part, kind, line), ref, order[2], step)

    def forward(turn, line):
        for part, (first, count, order) in enumerate(PARTS[turn]):
            low = (count // 32 + (count // 16) % 2 * (line % 2)) * 16
            shares = ((1, -1, 0, low), (-1, 1, low, count - low))
            for kind, (step, origin, skip, rows_sent) in enumerate(shares):
                copies[turn, 2, part, kind, line].wait_recv()
                ref = slots(spectra, shifted(order, line, origin), order[:1], turn * 256 + first + skip, rows_sent)
                send((turn, 2, part, kind + 2, line), ref, order[2], step)

    def finish_lines(turn):
        for line in range(len(LINES)):
            for part in range(3):
                for kind in (2, 3):
                    copies[turn, 2, part, kind, line].wait_recv()

    def multiply(turn, place=lambda index: index):
        def step(index, _):
            k = place(index)
            s = spectra[k // 16, k // 8 % 2, k // 4 % 2, k % 4, turn * 256:(turn + 1) * 256, :]
            right = jnp.concatenate([s, jnp.concatenate([-s[R2:], s[:R2]], axis=0)], axis=1)
            result = jnp.dot(left[turn, k], right, preferred_element_type=jnp.float32)
            base = pl.multiple_of(k * 16, 16)
            for c in range(2 * channels):
                both = result[c * BINS:(c + 1) * BINS]
                both = jnp.concatenate([both[:, :SRC_BLOCK], both[:, SRC_BLOCK:]], axis=0)
                cross[pl.ds(base, 16), c * SRC_BLOCK:(c + 1) * SRC_BLOCK] = both.astype(jnp.bfloat16)
            return 0

        return step

    def near(digit):
        return digit + digit // 2

    def shift(dx, dy, dz):
        x, y, z = [lax.rem(a + b, SIDE) for a, b in zip(at, (dx, dy, dz))]
        return x * 16 + y * 4 + z

    group = 8
    width = group * SRC_BLOCK

    def sum_lags(turn, core_index, n, store):
        both = slice(core_index * columns + n * width, core_index * columns + (n + 1) * width)
        value = jnp.dot(table[:, turn * 1024:(turn + 1) * 1024], cross[:, both], preferred_element_type=jnp.float32)
        for i in range(group):
            store(n * group + i, core_index * channels + n * group + i, value[:, i * SRC_BLOCK:(i + 1) * SRC_BLOCK])

    def keep(c, held_c, value):
        total[held_c] = value

    def hand_over(c, held_c, value):
        outgoing[c] = ((total[held_c] + value) * FACTOR).astype(jnp.bfloat16)

    def conclude(c, held_c, value):
        total[held_c] = total[held_c] + value

    pairs = SLOTS // 2
    lax.fori_loop(8, SLOTS, spread(0), 0)
    to_bands(0)
    lax.fori_loop(0, 8, spread(1), 0)
    to_bands(1)
    lax.fori_loop(8, 20, spread(1), 0)
    arrange(0)
    begin(0, 0)
    arrange(1)
    begin(1, 0)
    lax.fori_loop(20, 32, spread(1), 0)
    finish(0, 0)
    begin(0, 1)
    send_line(0, 0)
    finish(1, 0)
    begin(1, 1)
    send_line(1, 0)
    lax.fori_loop(32, 44, spread(1), 0)
    for line in (1, 2, 3):
        send_line(0, line)
    forward(0, 0)
    lax.fori_loop(44, SLOTS, spread(1), 0)
    for line in (1, 2, 3):
        forward(0, line)
        send_line(1, line)
    forward(1, 0)
    own_table.wait()
    finish_lines(0)
    quarter = SLOTS // 4
    for line, turns in ((1, 1), (2, 1), (3, 2)):
        first = (line - 1) * quarter
        lax.fori_loop(first, first + turns * quarter, multiply(0), 0, unroll=4)
        forward(1, line)
    for core_index in range(2):
        for n in range(channels // group):
            sum_lags(0, core_index, n, keep)
    lax.fori_loop(0, 27, multiply(1, lambda i: shift(near(i // 9), near(i // 3 % 3), near(i % 3))), 0, unroll=3)
    finish_lines(1)
    lax.fori_loop(0, 16, multiply(1, lambda i: shift(2, i // 4, i % 4)), 0, unroll=4)
    lax.fori_loop(0, 12, multiply(1, lambda i: shift(near(i // 4), 2, i % 4)), 0, unroll=4)
    lax.fori_loop(0, 9, multiply(1, lambda i: shift(near(i // 3), near(i % 3), 2)), 0, unroll=3)
    for n in range(channels // group):
        sum_lags(1, 1, n, hand_over)
    exchange = pltpu.make_async_remote_copy(
        src_ref=outgoing, dst_ref=incoming, send_sem=side_send.at[2], recv_sem=side_recv.at[2],
        device_id=sibling, device_id_type=MESH)
    exchange.start()
    for n in range(channels // group):
        sum_lags(1, 0, n, conclude)
    exchange.wait_recv()

    unit = identity(SRC_BLOCK)
    last = (((1,), (1,)), ((), ()))
    for c in range(channels):
        value = (total[c] * FACTOR + incoming[c].astype(jnp.float32)).astype(jnp.bfloat16)
        value = lax.dot_general(unit, value, last, preferred_element_type=jnp.float32)
        for half in range(2):
            turned[half, pl.ds(c, SRC_BLOCK, stride=channels), :] = value[:, half * R2:(half + 1) * R2]

    def pack(index):
        picked = pl.ds(pl.multiple_of(index * 256, 256), 256)
        return jnp.concatenate([turned[0, picked, :], turned[1, picked, :]], axis=1).astype(jnp.bfloat16)

    ships = []
    for r, (place, which) in enumerate(across):
        index = place[1] % 2 * SIDE + place[2]
        shipped[index] = pack(index)
        ship = pltpu.make_async_remote_copy(
            src_ref=shipped.at[index], dst_ref=landed.at[band], send_sem=ship_send.at[r], recv_sem=ship_recv.at[r],
            device_id=device_at(place, which), device_id_type=MESH)
        ship.start()
        ships.append(ship)
    shipped[band] = pack(band)
    kept = pltpu.make_async_copy(shipped.at[band], landed.at[band], local_sem.at[0])
    kept.start()
    for ship in ships:
        ship.wait_recv()

    kept.wait()
    for copy in swaps + [exchange] + sums[0] + sums[1] + moves[0] + moves[1] + ships + list(copies.values()):
        copy.wait_send()


def identity(n):
    diagonal = lax.broadcasted_iota(jnp.int32, (n, n), 0) == lax.broadcasted_iota(jnp.int32, (n, n), 1)
    return jnp.where(diagonal, 1.0, 0.0).astype(jnp.bfloat16)


def turn_kernel(landed, out):
    unit = identity(LAGS)
    bands, rows, _ = landed.shape
    channels = rows // out.shape[0]
    for s in range(out.shape[0]):
        value = landed[:, s * channels:(s + 1) * channels, :].reshape(bands * channels, LAGS)
        value = lax.dot_general(unit, value, (((1,), (1,)), ((), ())), preferred_element_type=jnp.float32)
        out[s] = value.astype(out.dtype)


def body(strain, source_block, source_offset, window_valid):
    channels = strain.shape[0]
    lanes = channels * W
    columns = channels * SRC_BLOCK
    tiles = strain.reshape(channels // BINS, BINS, -1, R2).transpose(0, 2, 1, 3).reshape(-1, R2)
    copies = ROUNDS * 3 * (3 + 3 + 4 * len(LINES))
    anywhere = pl.BlockSpec(memory_space=pl.ANY)
    scalars = pl.BlockSpec(memory_space=pltpu.SMEM)
    dma = pltpu.SemaphoreType.DMA
    bf16, f32 = jnp.bfloat16, jnp.float32
    landed = pl.pallas_call(
        kernel,
        in_specs=[anywhere] * 4 + [scalars] * 3,
        out_specs=anywhere,
        out_shape=jax.ShapeDtypeStruct((2 * SIDE, 256, LAGS), bf16),
        scratch_shapes=[
            pltpu.VMEM(tiles.shape, f32),
            pltpu.VMEM((3 * R1, R2), f32),
            pltpu.VMEM((R2, 2 * R2), bf16),
            pltpu.VMEM((LAGS, NF), bf16),
            pltpu.VMEM((3, 2, SIDE * 2, R2, lanes), bf16),
            pltpu.VMEM((2, SIDE * 2, R2, lanes), bf16),
            pltpu.VMEM((2, SIDE * 2, R2, lanes), bf16),
            pltpu.VMEM((2, SIDE * 2, 2 * BINS, lanes), bf16),
            pltpu.VMEM((2, SIDE * 2, 2 * BINS, lanes), bf16),
            pltpu.VMEM((SIDE, 2, 2, SIDE, PIECE, SRC_BLOCK), bf16),
            pltpu.VMEM((2, SLOTS, 256, 256), bf16),
            pltpu.VMEM((NF // 2, 2 * columns), bf16),
            pltpu.VMEM((2 * channels, LAGS, SRC_BLOCK), f32),
            pltpu.VMEM((channels, LAGS, SRC_BLOCK), bf16),
            pltpu.VMEM((channels, LAGS, SRC_BLOCK), bf16),
            pltpu.VMEM((2, columns, R2), f32),
            pltpu.VMEM((2 * SIDE, 256, LAGS), bf16),
            dma((4,)), dma((copies,)), dma((copies,)), dma((3,)), dma((3,)),
            dma((14,)), dma((14,)), dma((14,)), dma((14,)), dma((7,)), dma((7,)),
        ],
        compiler_params=pltpu.CompilerParams(
            vmem_limit_bytes=62 * 2**20, collective_id=1, has_side_effects=True),
        cost_estimate=pl.CostEstimate(flops=4 * 256 * 4096 * 2048, bytes_accessed=20 * 2**20, transcendentals=0),
    )(tiles, jnp.asarray(row_tables()), jnp.asarray(short_dft(), dtype=bf16),
      jnp.asarray(lag_table(), dtype=bf16), source_block, source_offset, window_valid)
    sources, steps = SRC_BLOCK // (2 * SIDE), 4
    return pl.pallas_call(
        turn_kernel,
        grid=(steps,),
        in_specs=[pl.BlockSpec((2 * SIDE, 256 // steps, LAGS), lambda i: (0, i, 0))],
        out_specs=pl.BlockSpec((sources // steps, LAGS, 2 * SIDE * channels), lambda i: (i, 0, 0)),
        out_shape=jax.ShapeDtypeStruct((sources, LAGS, 2 * SIDE * channels), bf16),
    )(landed)


def solution(mesh):
    in_specs = (P(("chan", "band"), None), P(), P(), P())
    out_specs = P("band", None, "chan")
    return jax.shard_map(body, mesh=mesh, in_specs=in_specs, out_specs=out_specs, check_vma=False)
```

```python
import functools
import math

import jax
import jax.numpy as jnp
import numpy as np
from jax import lax
from jax.experimental import pallas as pl
from jax.experimental.pallas import tpu as pltpu
from jax.sharding import PartitionSpec as P

L = 4096
HOP = 2048
NF = 2048
W = 16
SRC_BLOCK = 128
LAGS = 256
R1 = 32
R2 = 128
HALF = R2 // 2
BINS = 8
FACTOR = 1.0 / (W * math.sqrt(NF))


def window_table():
    points = np.arange(L, dtype=np.float32)
    angle = (points * np.float32(2.0 * math.pi / L)).astype(np.float32)
    return (np.float32(0.5) - np.float32(0.5) * np.cos(angle)).astype(np.float32).reshape(R1, R2)


def row_tables():
    angle = 2.0 * np.pi * np.outer(np.arange(R1), np.arange(R2)) / L
    return np.concatenate([window_table(), np.cos(angle), -np.sin(angle)], axis=0).astype(np.float32)


def short_dft():
    angle = 2.0 * np.pi * (np.outer(np.arange(HALF), np.arange(R2)) % R2) / R2
    cosine, sine = np.cos(angle), np.sin(angle)
    top = np.concatenate([cosine, sine], axis=1)
    low = np.concatenate([-sine, cosine], axis=1)
    both = np.stack([top.reshape(-1, BINS, 2 * R2), low.reshape(-1, BINS, 2 * R2)], axis=1)
    return both.reshape(R2, 2 * R2).astype(np.float32)


def lag_table():
    core, g, x, y_hi, y_lo, z, i = np.ix_(*[np.arange(n) for n in (2, 2, 4, 2, 2, 4, 8)])
    bins = 8 * x + 4 * y_hi + 2 * core + g + R1 * (32 * y_lo + 8 * z + i)
    lags = (np.arange(LAGS) - LAGS // 2).reshape((1, LAGS) + (1,) * 6)
    angle = 2.0 * np.pi * (lags * bins[:, None] % L) / L
    table = np.stack([np.cos(angle), -np.sin(angle)], axis=7)
    return table.reshape(2, LAGS, NF).astype(np.float32)


def real_dft(x):
    n = len(x)
    if n == 2:
        return [(x[0] + x[1], None), (x[0] - x[1], None)]
    even, odd = real_dft(x[0::2]), real_dft(x[1::2])
    out = [None] * (n // 2 + 1)
    for k in range(n // 4 + 1):
        er, ei = even[k]
        orr, oi = odd[k]
        if k == 0:
            out[0] = (er + orr, None)
            out[n // 2] = (er - orr, None)
            continue
        if 4 * k == n:
            out[k] = (er, -orr)
            continue
        c, s = math.cos(2 * math.pi * k / n), -math.sin(2 * math.pi * k / n)
        if oi is None:
            tr, ti = orr * c, orr * s
        else:
            tr, ti = orr * c - oi * s, orr * s + oi * c
        zi = ti if ei is None else ei + ti
        yi = -ti if ei is None else ei - ti
        out[k] = (er + tr, zi)
        out[n // 2 - k] = (er - tr, -yi)
    return out


SIDE = 4
SLOTS = SIDE ** 3
PIECE = 2 * 2 * BINS * W
PARTS = (((0, 96, (0, 1, 2)), (96, 80, (1, 2, 0)), (176, 80, (2, 0, 1))),
         ((0, 80, (0, 1, 2)), (80, 96, (1, 2, 0)), (176, 80, (2, 0, 1))))
LINES = (0, -1, 1, 2)
ROUNDS = 2
MESH = pl.DeviceIdType.MESH


def position():
    chan, band = lax.axis_index("chan"), lax.axis_index("band")
    return (chan // 4, chan // 2 % 2 * 2 + band // 4, band % 4), chan % 2


def device_at(at, core):
    x, y, z = at
    return (x * 4 + y // 2 * 2 + core, y % 2 * 4 + z)


def neighbour(axis, step):
    at, core = position()
    moved = list(at)
    moved[axis] = lax.rem(at[axis] + step + SIDE, SIDE)
    return device_at(moved, core)


def slots(ref, at, full, first, count):
    whole = slice(None)
    x = whole if 0 in full else at[0]
    y_hi, y_lo = (whole, whole) if 1 in full else (at[1] // 2, at[1] % 2)
    z = whole if 2 in full else at[2]
    return ref.at[x, y_hi, y_lo, z, pl.ds(first, count), :]


def partners(at, core):
    x, y, z = at
    side = lambda step: lax.rem(z + step, SIDE)
    along = [((lax.rem(x + dx, SIDE), y ^ (2 * dy), z), core) for dx in (2, 1, 3, 0) for dy in (1, 0)][:-1]
    across = [((x, y ^ dy, side(dz)), core) for dz in (2, 1, 3, 0) for dy in (1, 0)][:-1]
    return along, across, [((x, y ^ 3, z), core), (at, 1 - core)]


def kernel(strain_hbm, rows_hbm, dft_hbm, tables, block, offset, valid, landed,
           strain, rows, dft, table, held, mixed, parts, share, bands, spectra, left, cross, total,
           outgoing, incoming, turned, shipped,
           local_sem, send_sem, recv_sem, side_send, side_recv, chan_send, chan_recv, band_send, band_recv,
           ship_send, ship_recv):
    at, core = position()
    chan, band = lax.axis_index("chan"), lax.axis_index("band")
    sibling = device_at(at, 1 - core)
    lanes = held.shape[-1]
    channels = lanes // W
    columns = channels * SRC_BLOCK
    along, across, rest = partners(at, core)

    def fetch(src, dst, index):
        copy = pltpu.make_async_copy(src, dst, local_sem.at[index])
        copy.start()
        return copy

    fetched = [fetch(strain_hbm, strain, 0), fetch(rows_hbm, rows, 1), fetch(dft_hbm, dft, 2)]
    own_table = fetch(tables.at[core], table, 3)
    barrier = pltpu.get_barrier_semaphore()
    for place, which in along + across + rest:
        pl.semaphore_signal(barrier, inc=1, device_id=device_at(place, which), device_id_type=MESH)
    for copy in fetched:
        copy.wait()

    folded = left.at[0]

    def fold(c, _):
        first = c // BINS * (BINS * (W + 1) * W) + c % BINS
        x = [strain[pl.ds(first + BINS * k, W, stride=BINS * W), :] for k in range(R1)]
        whole = x[0]
        for k in range(1, R1):
            whole = whole + x[k]
        mean = jnp.sum(whole, axis=1, keepdims=True) * (1.0 / L)
        x = [((x[k] - mean) * rows[k:k + 1, :]).astype(jnp.bfloat16).astype(jnp.float32) for k in range(R1)]
        bins = real_dft(x)
        to = pl.ds(pl.multiple_of(c * W, W), W)
        for f in range(R1):
            re, im = bins[f] if f <= R1 // 2 else bins[R1 - f]
            cosine, sine = rows[R1 + f:R1 + f + 1, :], rows[2 * R1 + f:2 * R1 + f + 1, :]
            if im is None:
                gr, gi = re * cosine, re * sine
            else:
                im = im if f <= R1 // 2 else -im
                gr, gi = re * cosine - im * sine, re * sine + im * cosine
            folded[f, to, :R2] = gr.astype(jnp.bfloat16)
            folded[f, to, R2:] = gi.astype(jnp.bfloat16)
        return 0

    lax.fori_loop(0, channels, fold, 0, unroll=2)
    dft_table = dft[...]

    def transform(f, power):
        y = lax.dot_general(dft_table, folded[f], (((1,), (1,)), ((), ())), preferred_element_type=jnp.float32)
        total[f, :R2, :] = y[:, :R2]
        total[f, R2:, :] = y[:, R2:]
        square = (y * y).reshape(HALF // BINS, 2, BINS, lanes)
        return power + (square[:, 0] + square[:, 1]).reshape(HALF, lanes)

    power = lax.fori_loop(0, R1, transform, jnp.zeros((HALF, lanes), jnp.float32), unroll=8)
    scales = []
    for b in range(HALF // BINS):
        mean = jnp.sum(power[b * BINS:(b + 1) * BINS], axis=0, keepdims=True) * (1.0 / 256.0)
        scales.append(jnp.broadcast_to(lax.rsqrt(mean + 1e-06), (2 * BINS, lanes)))
    scale = jnp.concatenate(scales, axis=0)

    def finish_white(to, which, g):
        def step(index, _):
            f = index * 4 + which * 2 + g
            y = jnp.concatenate([total[f, :R2, :], total[f, R2:, :]], axis=1)
            held[to, g, index] = (y * scale).astype(jnp.bfloat16)
            return 0

        lax.fori_loop(0, SIDE * 2, step, 0, unroll=4)

    for g in range(2):
        finish_white(2, 1 - core, g)
    pl.semaphore_wait(barrier, len(along) + len(across) + len(rest))
    swaps = []
    for g in range(2):
        swap = pltpu.make_async_remote_copy(
            src_ref=held.at[2, g], dst_ref=held.at[1, g], send_sem=side_send.at[g], recv_sem=side_recv.at[g],
            device_id=sibling, device_id_type=MESH)
        swap.start()
        swaps.append(swap)
    for g in range(2):
        finish_white(0, core, g)

    row = lax.broadcasted_iota(jnp.int32, (2 * BINS, R2), 0) % BINS
    lane = lax.broadcasted_iota(jnp.int32, (2 * BINS, R2), 1)
    own = lane // W == row

    def spread(core_index):
        def step(index, _):
            x, y_hi, y_lo, z = index // 16, index // 8 % 2, index // 4 % 2, index % 4
            picked = pl.ds(pl.multiple_of((y_lo * SIDE + z) * 16, 16), 16)
            for g in range(2):
                for k in range(channels // 8):
                    value = held[core_index, g, x * 2 + y_hi, picked, k * R2:(k + 1) * R2].astype(jnp.float32)
                    for ri in range(2):
                        even = pltpu.roll(value[ri * BINS:(ri + 1) * BINS], 0, 1, stride=W, stride_axis=0)
                        both = jnp.concatenate([even, pltpu.roll(even, R2 - W, 1)], axis=0)
                        for t in range(4):
                            moved = pltpu.roll(both, R2 - 2 * W * t, 1) if t else both
                            first = ((core_index * channels // 8 + k) * 4 + t) * 2 * BINS
                            left[g, index, first:first + 2 * BINS, ri * R2:(ri + 1) * R2] = jnp.where(
                                own, moved, 0.0).astype(jnp.bfloat16)
            return 0

        return step

    lax.fori_loop(0, 8, spread(0), 0)

    spot = lax.broadcasted_iota(jnp.int32, (1, lanes), 1)
    source = band * channels + spot // W
    stacked = jnp.zeros((1, lanes), jnp.float32)
    for w in range(W):
        stacked = jnp.where(spot % W == w, jnp.where(valid[w] != 0, 1.0, 0.0), stacked)
    chans = R1 // 2

    def chosen(which):
        first = jnp.where(which == block[0], 1, 0)
        second = jnp.where(which == lax.rem(block[0] + 1, chans), 1, 0)
        taken = jnp.where(source >= offset[0], first, second)
        return jnp.where(taken == 1, stacked, 0.0)

    mine, theirs = chosen(chan), chosen(chan ^ 1)
    slot = chan // 2

    def mix(g):
        def step(index, _):
            a, b = held[0, g, index], held[1, g, index]
            value = a.astype(jnp.float32) * mine + b.astype(jnp.float32) * theirs
            mixed[g, index] = value.astype(jnp.bfloat16)
            return 0

        return step

    sums, moves = {}, {}
    for g in range(2):
        swaps[g].wait_recv()
        lax.fori_loop(0, SIDE * 2, mix(g), 0, unroll=4)
        sums[g] = []
        for r, (place, which) in enumerate(along):
            target = place[0] * 2 + place[1] // 2
            sums[g].append(pltpu.make_async_remote_copy(
                src_ref=mixed.at[g, target], dst_ref=parts.at[g, slot],
                send_sem=chan_send.at[g * 7 + r], recv_sem=chan_recv.at[g * 7 + r],
                device_id=device_at(place, which), device_id_type=MESH))
        for copy in sums[g]:
            copy.start()

    def to_bands(g):
        for copy in sums[g]:
            copy.wait_recv()
        parts[g, slot] = mixed[g, slot]
        value = parts[g, 0].astype(jnp.float32)
        for k in range(1, SIDE * 2):
            value = value + parts[g, k].astype(jnp.float32)
        share[g] = value.astype(jnp.bfloat16).reshape(2 * SIDE, 2 * BINS, lanes)
        moves[g] = []
        for r, (place, which) in enumerate(across):
            moves[g].append(pltpu.make_async_remote_copy(
                src_ref=share.at[g, place[1] % 2 * SIDE + place[2]], dst_ref=bands.at[g, band],
                send_sem=band_send.at[g * 7 + r], recv_sem=band_recv.at[g * 7 + r],
                device_id=device_at(place, which), device_id_type=MESH))
        for copy in moves[g]:
            copy.start()
        bands[g, band] = share[g, band]

    def arrange(g):
        for copy in moves[g]:
            copy.wait_recv()
        wide = (2 * BINS * W, lanes)
        same = lax.broadcasted_iota(jnp.int32, wide, 1) % W == lax.broadcasted_iota(jnp.int32, wide, 0) % W
        tall = (lanes, SRC_BLOCK)
        channel = lax.broadcasted_iota(jnp.int32, tall, 0) // W
        column = lax.broadcasted_iota(jnp.int32, tall, 1)
        value = None
        for b in range(2 * SIDE):
            goal = (channel + (b * channels + SRC_BLOCK) - offset[0]) % SRC_BLOCK
            pick = jnp.where(goal == column, 1.0, 0.0).astype(jnp.bfloat16)
            part = bands[g, b].astype(jnp.float32)
            part = jnp.broadcast_to(part[:, None, :], (2 * BINS, W, lanes)).reshape(wide)
            part = jnp.where(same, part, 0.0).astype(jnp.bfloat16)
            term = jnp.dot(part, pick, preferred_element_type=jnp.float32)
            value = term if value is None else value + term
        spectra[at[0], at[1] // 2, at[1] % 2, at[2], g * wide[0]:(g + 1) * wide[0], :] = value.astype(jnp.bfloat16)

    copies = {}

    def send(key, ref, axis, step):
        index = len(copies)
        copies[key] = pltpu.make_async_remote_copy(
            src_ref=ref, dst_ref=ref, send_sem=send_sem.at[index], recv_sem=recv_sem.at[index],
            device_id=neighbour(axis, step), device_id_type=MESH)
        copies[key].start()

    def shifted(order, line, step):
        moved = list(at)
        for axis, by in ((order[1], LINES[line]), (order[2], step)):
            moved[axis] = lax.rem(at[axis] + by + SIDE, SIDE)
        return moved

    def begin(turn, stage):
        for part, (first, count, order) in enumerate(PARTS[turn]):
            ref = slots(spectra, at, order[:stage], turn * 256 + first, count)
            for kind, step in enumerate((1, -1, 2)):
                send((turn, stage, part, kind), ref, order[stage], step)

    def finish(turn, stage):
        for part in range(3):
            for kind in range(3):
                copies[turn, stage, part, kind].wait_recv()

    def send_line(turn, line):
        for part, (first, count, order) in enumerate(PARTS[turn]):
            if line:
                copies[turn, 1, part, line - 1].wait_recv()
            ref = slots(spectra, shifted(order, line, 0), order[:1], turn * 256 + first, count)
            for kind, step in enumerate((1, -1)):
                send((turn, 2, part, kind, line), ref, order[2], step)

    def forward(turn, line):
        for part, (first, count, order) in enumerate(PARTS[turn]):
            low = (count // 32 + (count // 16) % 2 * (line % 2)) * 16
            shares = ((1, -1, 0, low), (-1, 1, low, count - low))
            for kind, (step, origin, skip, rows_sent) in enumerate(shares):
                copies[turn, 2, part, kind, line].wait_recv()
                ref = slots(spectra, shifted(order, line, origin), order[:1], turn * 256 + first + skip, rows_sent)
                send((turn, 2, part, kind + 2, line), ref, order[2], step)

    def finish_lines(turn):
        for line in range(len(LINES)):
            for part in range(3):
                for kind in (2, 3):
                    copies[turn, 2, part, kind, line].wait_recv()

    def multiply(turn, place=lambda index: index):
        def step(index, _):
            k = place(index)
            s = spectra[k // 16, k // 8 % 2, k // 4 % 2, k % 4, turn * 256:(turn + 1) * 256, :]
            right = jnp.concatenate([s, jnp.concatenate([-s[R2:], s[:R2]], axis=0)], axis=1)
            result = jnp.dot(left[turn, k], right, preferred_element_type=jnp.float32)
            base = pl.multiple_of(k * 16, 16)
            for c in range(2 * channels):
                both = result[c * BINS:(c + 1) * BINS]
                both = jnp.concatenate([both[:, :SRC_BLOCK], both[:, SRC_BLOCK:]], axis=0)
                cross[pl.ds(base, 16), c * SRC_BLOCK:(c + 1) * SRC_BLOCK] = both.astype(jnp.bfloat16)
            return 0

        return step

    def near(digit):
        return digit + digit // 2

    def shift(dx, dy, dz):
        x, y, z = [lax.rem(a + b, SIDE) for a, b in zip(at, (dx, dy, dz))]
        return x * 16 + y * 4 + z

    group = 8
    width = group * SRC_BLOCK

    def sum_lags(turn, core_index, n, store):
        both = slice(core_index * columns + n * width, core_index * columns + (n + 1) * width)
        value = jnp.dot(table[:, turn * 1024:(turn + 1) * 1024], cross[:, both], preferred_element_type=jnp.float32)
        for i in range(group):
            store(n * group + i, core_index * channels + n * group + i, value[:, i * SRC_BLOCK:(i + 1) * SRC_BLOCK])

    def keep(c, held_c, value):
        total[held_c] = value

    def hand_over(c, held_c, value):
        outgoing[c] = ((total[held_c] + value) * FACTOR).astype(jnp.bfloat16)

    def conclude(c, held_c, value):
        total[held_c] = total[held_c] + value

    pairs = SLOTS // 2
    lax.fori_loop(8, SLOTS, spread(0), 0)
    to_bands(0)
    lax.fori_loop(0, 8, spread(1), 0)
    to_bands(1)
    lax.fori_loop(8, 20, spread(1), 0)
    arrange(0)
    begin(0, 0)
    arrange(1)
    begin(1, 0)
    lax.fori_loop(20, 32, spread(1), 0)
    finish(0, 0)
    begin(0, 1)
    send_line(0, 0)
    finish(1, 0)
    begin(1, 1)
    lax.fori_loop(32, 44, spread(1), 0)
    for line in (1, 2, 3):
        send_line(0, line)
    forward(0, 0)
    lax.fori_loop(44, 56, spread(1), 0)
    forward(0, 1)
    send_line(1, 0)
    lax.fori_loop(56, SLOTS, spread(1), 0)
    forward(0, 2)
    forward(0, 3)
    for line in (1, 2, 3):
        send_line(1, line)
    own_table.wait()
    finish_lines(0)
    quarter = SLOTS // 4
    for line in range(4):
        lax.fori_loop(line * quarter, (line + 1) * quarter, multiply(0), 0, unroll=4)
        forward(1, line)
    for core_index in range(2):
        for n in range(channels // group):
            sum_lags(0, core_index, n, keep)
    lax.fori_loop(0, 27, multiply(1, lambda i: shift(near(i // 9), near(i // 3 % 3), near(i % 3))), 0, unroll=3)
    finish_lines(1)
    lax.fori_loop(0, 16, multiply(1, lambda i: shift(2, i // 4, i % 4)), 0, unroll=4)
    lax.fori_loop(0, 12, multiply(1, lambda i: shift(near(i // 4), 2, i % 4)), 0, unroll=4)
    lax.fori_loop(0, 9, multiply(1, lambda i: shift(near(i // 3), near(i % 3), 2)), 0, unroll=3)
    for n in range(channels // group):
        sum_lags(1, 1, n, hand_over)
    exchange = pltpu.make_async_remote_copy(
        src_ref=outgoing, dst_ref=incoming, send_sem=side_send.at[2], recv_sem=side_recv.at[2],
        device_id=sibling, device_id_type=MESH)
    exchange.start()
    for n in range(channels // group):
        sum_lags(1, 0, n, conclude)
    exchange.wait_recv()

    unit = identity(SRC_BLOCK)
    last = (((1,), (1,)), ((), ()))
    for c in range(channels):
        value = (total[c] * FACTOR + incoming[c].astype(jnp.float32)).astype(jnp.bfloat16)
        value = lax.dot_general(unit, value, last, preferred_element_type=jnp.float32)
        for half in range(2):
            turned[half, pl.ds(c, SRC_BLOCK, stride=channels), :] = value[:, half * R2:(half + 1) * R2]

    def pack(index):
        picked = pl.ds(pl.multiple_of(index * 256, 256), 256)
        return jnp.concatenate([turned[0, picked, :], turned[1, picked, :]], axis=1).astype(jnp.bfloat16)

    ships = []
    for r, (place, which) in enumerate(across):
        index = place[1] % 2 * SIDE + place[2]
        shipped[index] = pack(index)
        ship = pltpu.make_async_remote_copy(
            src_ref=shipped.at[index], dst_ref=landed.at[band], send_sem=ship_send.at[r], recv_sem=ship_recv.at[r],
            device_id=device_at(place, which), device_id_type=MESH)
        ship.start()
        ships.append(ship)
    shipped[band] = pack(band)
    kept = pltpu.make_async_copy(shipped.at[band], landed.at[band], local_sem.at[0])
    kept.start()
    for ship in ships:
        ship.wait_recv()

    kept.wait()
    for copy in swaps + [exchange] + sums[0] + sums[1] + moves[0] + moves[1] + ships + list(copies.values()):
        copy.wait_send()


def identity(n):
    diagonal = lax.broadcasted_iota(jnp.int32, (n, n), 0) == lax.broadcasted_iota(jnp.int32, (n, n), 1)
    return jnp.where(diagonal, 1.0, 0.0).astype(jnp.bfloat16)


def turn_kernel(landed, out):
    unit = identity(LAGS)
    bands, rows, _ = landed.shape
    channels = rows // out.shape[0]
    for s in range(out.shape[0]):
        value = landed[:, s * channels:(s + 1) * channels, :].reshape(bands * channels, LAGS)
        value = lax.dot_general(unit, value, (((1,), (1,)), ((), ())), preferred_element_type=jnp.float32)
        out[s] = value.astype(out.dtype)


def body(strain, source_block, source_offset, window_valid):
    channels = strain.shape[0]
    lanes = channels * W
    columns = channels * SRC_BLOCK
    tiles = strain.reshape(channels // BINS, BINS, -1, R2).transpose(0, 2, 1, 3).reshape(-1, R2)
    copies = ROUNDS * 3 * (3 + 3 + 4 * len(LINES))
    anywhere = pl.BlockSpec(memory_space=pl.ANY)
    scalars = pl.BlockSpec(memory_space=pltpu.SMEM)
    dma = pltpu.SemaphoreType.DMA
    bf16, f32 = jnp.bfloat16, jnp.float32
    landed = pl.pallas_call(
        kernel,
        in_specs=[anywhere] * 4 + [scalars] * 3,
        out_specs=anywhere,
        out_shape=jax.ShapeDtypeStruct((2 * SIDE, 256, LAGS), bf16),
        scratch_shapes=[
            pltpu.VMEM(tiles.shape, f32),
            pltpu.VMEM((3 * R1, R2), f32),
            pltpu.VMEM((R2, 2 * R2), bf16),
            pltpu.VMEM((LAGS, NF), bf16),
            pltpu.VMEM((3, 2, SIDE * 2, R2, lanes), bf16),
            pltpu.VMEM((2, SIDE * 2, R2, lanes), bf16),
            pltpu.VMEM((2, SIDE * 2, R2, lanes), bf16),
            pltpu.VMEM((2, SIDE * 2, 2 * BINS, lanes), bf16),
            pltpu.VMEM((2, SIDE * 2, 2 * BINS, lanes), bf16),
            pltpu.VMEM((SIDE, 2, 2, SIDE, PIECE, SRC_BLOCK), bf16),
            pltpu.VMEM((2, SLOTS, 256, 256), bf16),
            pltpu.VMEM((NF // 2, 2 * columns), bf16),
            pltpu.VMEM((2 * channels, LAGS, SRC_BLOCK), f32),
            pltpu.VMEM((channels, LAGS, SRC_BLOCK), bf16),
            pltpu.VMEM((channels, LAGS, SRC_BLOCK), bf16),
            pltpu.VMEM((2, columns, R2), f32),
            pltpu.VMEM((2 * SIDE, 256, LAGS), bf16),
            dma((4,)), dma((copies,)), dma((copies,)), dma((3,)), dma((3,)),
            dma((14,)), dma((14,)), dma((14,)), dma((14,)), dma((7,)), dma((7,)),
        ],
        compiler_params=pltpu.CompilerParams(
            vmem_limit_bytes=62 * 2**20, collective_id=1, has_side_effects=True),
        cost_estimate=pl.CostEstimate(flops=4 * 256 * 4096 * 2048, bytes_accessed=20 * 2**20, transcendentals=0),
    )(tiles, jnp.asarray(row_tables()), jnp.asarray(short_dft(), dtype=bf16),
      jnp.asarray(lag_table(), dtype=bf16), source_block, source_offset, window_valid)
    sources, steps = SRC_BLOCK // (2 * SIDE), 4
    return pl.pallas_call(
        turn_kernel,
        grid=(steps,),
        in_specs=[pl.BlockSpec((2 * SIDE, 256 // steps, LAGS), lambda i: (0, i, 0))],
        out_specs=pl.BlockSpec((sources // steps, LAGS, 2 * SIDE * channels), lambda i: (i, 0, 0)),
        out_shape=jax.ShapeDtypeStruct((sources, LAGS, 2 * SIDE * channels), bf16),
    )(landed)


def solution(mesh):
    in_specs = (P(("chan", "band"), None), P(), P(), P())
    out_specs = P("band", None, "chan")
    return jax.shard_map(body, mesh=mesh, in_specs=in_specs, out_specs=out_specs, check_vma=False)
```

```python
import functools
import math

import jax
import jax.numpy as jnp
import numpy as np
from jax import lax
from jax.experimental import pallas as pl
from jax.experimental.pallas import tpu as pltpu
from jax.sharding import PartitionSpec as P

L = 4096
HOP = 2048
NF = 2048
W = 16
SRC_BLOCK = 128
LAGS = 256
R1 = 32
R2 = 128
HALF = R2 // 2
BINS = 8
FACTOR = 1.0 / (W * math.sqrt(NF))


def window_table():
    points = np.arange(L, dtype=np.float32)
    angle = (points * np.float32(2.0 * math.pi / L)).astype(np.float32)
    return (np.float32(0.5) - np.float32(0.5) * np.cos(angle)).astype(np.float32).reshape(R1, R2)


def row_tables():
    angle = 2.0 * np.pi * np.outer(np.arange(R1), np.arange(R2)) / L
    return np.concatenate([window_table(), np.cos(angle), -np.sin(angle)], axis=0).astype(np.float32)


def short_dft():
    angle = 2.0 * np.pi * (np.outer(np.arange(HALF), np.arange(R2)) % R2) / R2
    cosine, sine = np.cos(angle), np.sin(angle)
    top = np.concatenate([cosine, sine], axis=1)
    low = np.concatenate([-sine, cosine], axis=1)
    both = np.stack([top.reshape(-1, BINS, 2 * R2), low.reshape(-1, BINS, 2 * R2)], axis=1)
    return both.reshape(R2, 2 * R2).astype(np.float32)


def lag_table():
    core, g, x, y_hi, y_lo, z, i = np.ix_(*[np.arange(n) for n in (2, 2, 4, 2, 2, 4, 8)])
    bins = 8 * x + 4 * y_hi + 2 * core + g + R1 * (32 * y_lo + 8 * z + i)
    lags = (np.arange(LAGS) - LAGS // 2).reshape((1, LAGS) + (1,) * 6)
    angle = 2.0 * np.pi * (lags * bins[:, None] % L) / L
    table = np.stack([np.cos(angle), -np.sin(angle)], axis=7)
    return table.reshape(2, LAGS, NF).astype(np.float32)


def real_dft(x):
    n = len(x)
    if n == 2:
        return [(x[0] + x[1], None), (x[0] - x[1], None)]
    even, odd = real_dft(x[0::2]), real_dft(x[1::2])
    out = [None] * (n // 2 + 1)
    for k in range(n // 4 + 1):
        er, ei = even[k]
        orr, oi = odd[k]
        if k == 0:
            out[0] = (er + orr, None)
            out[n // 2] = (er - orr, None)
            continue
        if 4 * k == n:
            out[k] = (er, -orr)
            continue
        c, s = math.cos(2 * math.pi * k / n), -math.sin(2 * math.pi * k / n)
        if oi is None:
            tr, ti = orr * c, orr * s
        else:
            tr, ti = orr * c - oi * s, orr * s + oi * c
        zi = ti if ei is None else ei + ti
        yi = -ti if ei is None else ei - ti
        out[k] = (er + tr, zi)
        out[n // 2 - k] = (er - tr, -yi)
    return out


SIDE = 4
SLOTS = SIDE ** 3
PIECE = 2 * 2 * BINS * W
PARTS = (((0, 96, (0, 1, 2)), (96, 80, (1, 2, 0)), (176, 80, (2, 0, 1))),
         ((0, 80, (0, 1, 2)), (80, 96, (1, 2, 0)), (176, 80, (2, 0, 1))))
LINES = (0, -1, 1, 2)
ROUNDS = 2
MESH = pl.DeviceIdType.MESH


def position():
    chan, band = lax.axis_index("chan"), lax.axis_index("band")
    return (chan // 4, chan // 2 % 2 * 2 + band // 4, band % 4), chan % 2


def device_at(at, core):
    x, y, z = at
    return (x * 4 + y // 2 * 2 + core, y % 2 * 4 + z)


def neighbour(axis, step):
    at, core = position()
    moved = list(at)
    moved[axis] = lax.rem(at[axis] + step + SIDE, SIDE)
    return device_at(moved, core)


def slots(ref, at, full, first, count):
    whole = slice(None)
    x = whole if 0 in full else at[0]
    y_hi, y_lo = (whole, whole) if 1 in full else (at[1] // 2, at[1] % 2)
    z = whole if 2 in full else at[2]
    return ref.at[x, y_hi, y_lo, z, pl.ds(first, count), :]


def partners(at, core):
    x, y, z = at
    side = lambda step: lax.rem(z + step, SIDE)
    along = [((lax.rem(x + dx, SIDE), y ^ (2 * dy), z), core) for dx in (2, 1, 3, 0) for dy in (1, 0)][:-1]
    across = [((x, y ^ dy, side(dz)), core) for dz in (2, 1, 3, 0) for dy in (1, 0)][:-1]
    return along, across, [((x, y ^ 3, z), core), (at, 1 - core)]


def kernel(strain_hbm, rows_hbm, dft_hbm, tables, block, offset, valid, landed,
           strain, rows, dft, table, held, mixed, parts, share, bands, spectra, left, cross, total,
           outgoing, incoming, turned, shipped,
           local_sem, send_sem, recv_sem, side_send, side_recv, chan_send, chan_recv, band_send, band_recv,
           ship_send, ship_recv):
    at, core = position()
    chan, band = lax.axis_index("chan"), lax.axis_index("band")
    sibling = device_at(at, 1 - core)
    lanes = 2 * held.shape[-1]
    channels = lanes // W
    columns = channels * SRC_BLOCK
    along, across, rest = partners(at, core)

    def fetch(src, dst, index):
        copy = pltpu.make_async_copy(src, dst, local_sem.at[index])
        copy.start()
        return copy

    fetched = [fetch(strain_hbm, strain, 0), fetch(rows_hbm, rows, 1), fetch(dft_hbm, dft, 2)]
    own_table = fetch(tables.at[core], table, 3)
    barrier = pltpu.get_barrier_semaphore()
    for place, which in along + across + rest:
        pl.semaphore_signal(barrier, inc=1, device_id=device_at(place, which), device_id_type=MESH)
    for copy in fetched:
        copy.wait()

    folded = left.at[0]

    def fold(c, _):
        first = c // BINS * (BINS * (W + 1) * W) + c % BINS
        x = [strain[pl.ds(first + BINS * k, W, stride=BINS * W), :] for k in range(R1)]
        whole = x[0]
        for k in range(1, R1):
            whole = whole + x[k]
        mean = jnp.sum(whole, axis=1, keepdims=True) * (1.0 / L)
        x = [((x[k] - mean) * rows[k:k + 1, :]).astype(jnp.bfloat16).astype(jnp.float32) for k in range(R1)]
        bins = real_dft(x)
        to = pl.ds(pl.multiple_of(c * W, W), W)
        for f in range(R1):
            re, im = bins[f] if f <= R1 // 2 else bins[R1 - f]
            cosine, sine = rows[R1 + f:R1 + f + 1, :], rows[2 * R1 + f:2 * R1 + f + 1, :]
            if im is None:
                gr, gi = re * cosine, re * sine
            else:
                im = im if f <= R1 // 2 else -im
                gr, gi = re * cosine - im * sine, re * sine + im * cosine
            folded[f, to, :R2] = gr.astype(jnp.bfloat16)
            folded[f, to, R2:] = gi.astype(jnp.bfloat16)
        return 0

    dft_table = dft[...]

    def transform(half):
        picked = slice(half * R2, (half + 1) * R2)

        def step(f, power):
            y = lax.dot_general(
                dft_table, folded[f, picked, :], (((1,), (1,)), ((), ())), preferred_element_type=jnp.float32)
            total[f, picked, :] = y
            square = (y * y).reshape(HALF // BINS, 2, BINS, R2)
            return power + (square[:, 0] + square[:, 1]).reshape(HALF, R2)

        power = lax.fori_loop(0, R1, step, jnp.zeros((HALF, R2), jnp.float32), unroll=8)
        scales = []
        for b in range(HALF // BINS):
            mean = jnp.sum(power[b * BINS:(b + 1) * BINS], axis=0, keepdims=True) * (1.0 / 256.0)
            scales.append(jnp.broadcast_to(lax.rsqrt(mean + 1e-06), (2 * BINS, R2)))
        return jnp.concatenate(scales, axis=0)

    def finish_white(to, which, half, scale):
        def step(index, _):
            j, g = index // 2, index % 2
            y = total[j * 4 + which * 2 + g, half * R2:(half + 1) * R2, :]
            held[to, half, g, j] = (y * scale).astype(jnp.bfloat16)
            return 0

        lax.fori_loop(0, SIDE * 4, step, 0, unroll=4)

    swaps, sums, moves = {}, {}, {}

    def swap(half):
        swaps[half] = pltpu.make_async_remote_copy(
            src_ref=held.at[2, half], dst_ref=held.at[1, half], send_sem=side_send.at[half],
            recv_sem=side_recv.at[half], device_id=sibling, device_id_type=MESH)
        swaps[half].start()

    chans = R1 // 2
    spot = lax.broadcasted_iota(jnp.int32, (1, R2), 1)
    stacked = jnp.zeros((1, R2), jnp.float32)
    for w in range(W):
        stacked = jnp.where(spot % W == w, jnp.where(valid[w] != 0, 1.0, 0.0), stacked)

    def chosen(which, half):
        source = band * channels + half * BINS + spot // W
        first = jnp.where(which == block[0], 1, 0)
        second = jnp.where(which == lax.rem(block[0] + 1, chans), 1, 0)
        taken = jnp.where(source >= offset[0], first, second)
        return jnp.where(taken == 1, stacked, 0.0)

    slot = chan // 2

    def add_up(half):
        mine, theirs = chosen(chan, half), chosen(chan ^ 1, half)
        swaps[half].wait_recv()

        def mix(index, _):
            j, g = index // 2, index % 2
            value = held[0, half, g, j].astype(jnp.float32) * mine + held[1, half, g, j].astype(jnp.float32) * theirs
            mixed[half, j, g] = value.astype(jnp.bfloat16)
            return 0

        lax.fori_loop(0, SIDE * 4, mix, 0, unroll=4)
        sums[half] = []
        for r, (place, which) in enumerate(along):
            target = place[0] * 2 + place[1] // 2
            sums[half].append(pltpu.make_async_remote_copy(
                src_ref=mixed.at[half, target], dst_ref=parts.at[half, slot],
                send_sem=chan_send.at[half * 7 + r], recv_sem=chan_recv.at[half * 7 + r],
                device_id=device_at(place, which), device_id_type=MESH))
        for copy in sums[half]:
            copy.start()

    def to_bands(half):
        for copy in sums[half]:
            copy.wait_recv()
        parts[half, slot] = mixed[half, slot]
        for g in range(2):
            value = parts[half, 0, g].astype(jnp.float32)
            for k in range(1, SIDE * 2):
                value = value + parts[half, k, g].astype(jnp.float32)
            share[half, :, g] = value.astype(jnp.bfloat16).reshape(2 * SIDE, 2 * BINS, R2)
        moves[half] = []
        for r, (place, which) in enumerate(across):
            moves[half].append(pltpu.make_async_remote_copy(
                src_ref=share.at[half, place[1] % 2 * SIDE + place[2]], dst_ref=bands.at[half, band],
                send_sem=band_send.at[half * 7 + r], recv_sem=band_recv.at[half * 7 + r],
                device_id=device_at(place, which), device_id_type=MESH))
        for copy in moves[half]:
            copy.start()
        bands[half, band] = share[half, band]

    lax.fori_loop(0, BINS, fold, 0, unroll=2)
    scale = transform(0)
    finish_white(2, 1 - core, 0, scale)
    pl.semaphore_wait(barrier, len(along) + len(across) + len(rest))
    swap(0)
    finish_white(0, core, 0, scale)
    lax.fori_loop(BINS, BINS + 2, fold, 0, unroll=2)
    add_up(0)
    lax.fori_loop(BINS + 2, channels, fold, 0, unroll=2)
    scale = transform(1)
    finish_white(2, 1 - core, 1, scale)
    swap(1)
    finish_white(0, core, 1, scale)

    row = lax.broadcasted_iota(jnp.int32, (2 * BINS, R2), 0) % BINS
    lane = lax.broadcasted_iota(jnp.int32, (2 * BINS, R2), 1)
    own = lane // W == row

    def spread(core_index):
        def step(index, _):
            x, y_hi, y_lo, z = index // 16, index // 8 % 2, index // 4 % 2, index % 4
            picked = pl.ds(pl.multiple_of((y_lo * SIDE + z) * 16, 16), 16)
            for g in range(2):
                for k in range(channels // 8):
                    value = held[core_index, k, g, x * 2 + y_hi, picked, :].astype(jnp.float32)
                    for ri in range(2):
                        even = pltpu.roll(value[ri * BINS:(ri + 1) * BINS], 0, 1, stride=W, stride_axis=0)
                        both = jnp.concatenate([even, pltpu.roll(even, R2 - W, 1)], axis=0)
                        for t in range(4):
                            moved = pltpu.roll(both, R2 - 2 * W * t, 1) if t else both
                            first = ((core_index * channels // 8 + k) * 4 + t) * 2 * BINS
                            left[g, index, first:first + 2 * BINS, ri * R2:(ri + 1) * R2] = jnp.where(
                                own, moved, 0.0).astype(jnp.bfloat16)
            return 0

        return step

    lax.fori_loop(0, 8, spread(0), 0)

    add_up(1)

    def arrange(g):
        wide = (2 * BINS * W, lanes)
        same = lax.broadcasted_iota(jnp.int32, wide, 1) % W == lax.broadcasted_iota(jnp.int32, wide, 0) % W
        tall = (lanes, SRC_BLOCK)
        channel = lax.broadcasted_iota(jnp.int32, tall, 0) // W
        column = lax.broadcasted_iota(jnp.int32, tall, 1)
        value = None
        for b in range(2 * SIDE):
            goal = (channel + (b * channels + SRC_BLOCK) - offset[0]) % SRC_BLOCK
            pick = jnp.where(goal == column, 1.0, 0.0).astype(jnp.bfloat16)
            part = jnp.concatenate([bands[half, b, g] for half in range(2)], axis=1).astype(jnp.float32)
            part = jnp.broadcast_to(part[:, None, :], (2 * BINS, W, lanes)).reshape(wide)
            part = jnp.where(same, part, 0.0).astype(jnp.bfloat16)
            term = jnp.dot(part, pick, preferred_element_type=jnp.float32)
            value = term if value is None else value + term
        spectra[at[0], at[1] // 2, at[1] % 2, at[2], g * wide[0]:(g + 1) * wide[0], :] = value.astype(jnp.bfloat16)

    copies = {}

    def send(key, ref, axis, step):
        index = len(copies)
        copies[key] = pltpu.make_async_remote_copy(
            src_ref=ref, dst_ref=ref, send_sem=send_sem.at[index], recv_sem=recv_sem.at[index],
            device_id=neighbour(axis, step), device_id_type=MESH)
        copies[key].start()

    def shifted(order, line, step):
        moved = list(at)
        for axis, by in ((order[1], LINES[line]), (order[2], step)):
            moved[axis] = lax.rem(at[axis] + by + SIDE, SIDE)
        return moved

    def begin(turn, stage):
        for part, (first, count, order) in enumerate(PARTS[turn]):
            ref = slots(spectra, at, order[:stage], turn * 256 + first, count)
            for kind, step in enumerate((1, -1, 2)):
                send((turn, stage, part, kind), ref, order[stage], step)

    def finish(turn, stage):
        for part in range(3):
            for kind in range(3):
                copies[turn, stage, part, kind].wait_recv()

    def send_line(turn, line):
        for part, (first, count, order) in enumerate(PARTS[turn]):
            if line:
                copies[turn, 1, part, line - 1].wait_recv()
            ref = slots(spectra, shifted(order, line, 0), order[:1], turn * 256 + first, count)
            for kind, step in enumerate((1, -1)):
                send((turn, 2, part, kind, line), ref, order[2], step)

    def forward(turn, line):
        for part, (first, count, order) in enumerate(PARTS[turn]):
            low = (count // 32 + (count // 16) % 2 * (line % 2)) * 16
            shares = ((1, -1, 0, low), (-1, 1, low, count - low))
            for kind, (step, origin, skip, rows_sent) in enumerate(shares):
                copies[turn, 2, part, kind, line].wait_recv()
                ref = slots(spectra, shifted(order, line, origin), order[:1], turn * 256 + first + skip, rows_sent)
                send((turn, 2, part, kind + 2, line), ref, order[2], step)

    def finish_lines(turn):
        for line in range(len(LINES)):
            for part in range(3):
                for kind in (2, 3):
                    copies[turn, 2, part, kind, line].wait_recv()

    def multiply(turn, place=lambda index: index):
        def step(index, _):
            k = place(index)
            s = spectra[k // 16, k // 8 % 2, k // 4 % 2, k % 4, turn * 256:(turn + 1) * 256, :]
            right = jnp.concatenate([s, jnp.concatenate([-s[R2:], s[:R2]], axis=0)], axis=1)
            result = jnp.dot(left[turn, k], right, preferred_element_type=jnp.float32)
            base = pl.multiple_of(k * 16, 16)
            for c in range(2 * channels):
                both = result[c * BINS:(c + 1) * BINS]
                both = jnp.concatenate([both[:, :SRC_BLOCK], both[:, SRC_BLOCK:]], axis=0)
                cross[pl.ds(base, 16), c * SRC_BLOCK:(c + 1) * SRC_BLOCK] = both.astype(jnp.bfloat16)
            return 0

        return step

    def near(digit):
        return digit + digit // 2

    def shift(dx, dy, dz):
        x, y, z = [lax.rem(a + b, SIDE) for a, b in zip(at, (dx, dy, dz))]
        return x * 16 + y * 4 + z

    group = 8
    width = group * SRC_BLOCK

    def sum_lags(turn, core_index, n, store):
        both = slice(core_index * columns + n * width, core_index * columns + (n + 1) * width)
        value = jnp.dot(table[:, turn * 1024:(turn + 1) * 1024], cross[:, both], preferred_element_type=jnp.float32)
        for i in range(group):
            store(n * group + i, core_index * channels + n * group + i, value[:, i * SRC_BLOCK:(i + 1) * SRC_BLOCK])

    def keep(c, held_c, value):
        total[held_c] = value

    def hand_over(c, held_c, value):
        outgoing[c] = ((total[held_c] + value) * FACTOR).astype(jnp.bfloat16)

    def conclude(c, held_c, value):
        total[held_c] = total[held_c] + value

    pairs = SLOTS // 2
    lax.fori_loop(8, 16, spread(0), 0)
    to_bands(0)
    lax.fori_loop(16, SLOTS, spread(0), 0)
    to_bands(1)
    lax.fori_loop(0, 24, spread(1), 0)
    for half in range(2):
        for copy in moves[half]:
            copy.wait_recv()
    arrange(0)
    begin(0, 0)
    arrange(1)
    begin(1, 0)
    lax.fori_loop(24, 32, spread(1), 0)
    finish(0, 0)
    begin(0, 1)
    send_line(0, 0)
    finish(1, 0)
    begin(1, 1)
    lax.fori_loop(32, 44, spread(1), 0)
    for line in (1, 2, 3):
        send_line(0, line)
    forward(0, 0)
    lax.fori_loop(44, 56, spread(1), 0)
    forward(0, 1)
    send_line(1, 0)
    lax.fori_loop(56, SLOTS, spread(1), 0)
    forward(0, 2)
    forward(0, 3)
    for line in (1, 2, 3):
        send_line(1, line)
    own_table.wait()
    finish_lines(0)
    quarter = SLOTS // 4
    for line in range(4):
        lax.fori_loop(line * quarter, (line + 1) * quarter, multiply(0), 0, unroll=4)
        forward(1, line)
    for core_index in range(2):
        for n in range(channels // group):
            sum_lags(0, core_index, n, keep)
    lax.fori_loop(0, 27, multiply(1, lambda i: shift(near(i // 9), near(i // 3 % 3), near(i % 3))), 0, unroll=3)
    finish_lines(1)
    lax.fori_loop(0, 16, multiply(1, lambda i: shift(2, i // 4, i % 4)), 0, unroll=4)
    lax.fori_loop(0, 12, multiply(1, lambda i: shift(near(i // 4), 2, i % 4)), 0, unroll=4)
    lax.fori_loop(0, 9, multiply(1, lambda i: shift(near(i // 3), near(i % 3), 2)), 0, unroll=3)
    exchanges = []
    for n in range(channels // group):
        sum_lags(1, 1, n, hand_over)
        some = pl.ds(n * group, group)
        exchange = pltpu.make_async_remote_copy(
            src_ref=outgoing.at[some], dst_ref=incoming.at[some], send_sem=side_send.at[2 + n],
            recv_sem=side_recv.at[2 + n], device_id=sibling, device_id_type=MESH)
        exchange.start()
        exchanges.append(exchange)
    for n in range(channels // group):
        sum_lags(1, 0, n, conclude)

    unit = identity(SRC_BLOCK)
    last = (((1,), (1,)), ((), ()))
    for c in range(channels):
        if c % group == 0:
            exchanges[c // group].wait_recv()
        value = (total[c] * FACTOR + incoming[c].astype(jnp.float32)).astype(jnp.bfloat16)
        value = lax.dot_general(unit, value, last, preferred_element_type=jnp.float32)
        for half in range(2):
            turned[half, pl.ds(c, SRC_BLOCK, stride=channels), :] = value[:, half * R2:(half + 1) * R2]

    def pack(index):
        picked = pl.ds(pl.multiple_of(index * 256, 256), 256)
        return jnp.concatenate([turned[0, picked, :], turned[1, picked, :]], axis=1).astype(jnp.bfloat16)

    ships = []
    for r, (place, which) in enumerate(across):
        index = place[1] % 2 * SIDE + place[2]
        shipped[index] = pack(index)
        ship = pltpu.make_async_remote_copy(
            src_ref=shipped.at[index], dst_ref=landed.at[band], send_sem=ship_send.at[r], recv_sem=ship_recv.at[r],
            device_id=device_at(place, which), device_id_type=MESH)
        ship.start()
        ships.append(ship)
    shipped[band] = pack(band)
    kept = pltpu.make_async_copy(shipped.at[band], landed.at[band], local_sem.at[0])
    kept.start()
    for ship in ships:
        ship.wait_recv()

    kept.wait()
    for copy in [swaps[0], swaps[1]] + exchanges + sums[0] + sums[1] + moves[0] + moves[1] + ships + list(copies.values()):
        copy.wait_send()


def identity(n):
    diagonal = lax.broadcasted_iota(jnp.int32, (n, n), 0) == lax.broadcasted_iota(jnp.int32, (n, n), 1)
    return jnp.where(diagonal, 1.0, 0.0).astype(jnp.bfloat16)


def body(strain, source_block, source_offset, window_valid):
    channels = strain.shape[0]
    lanes = channels * W
    columns = channels * SRC_BLOCK
    tiles = strain.reshape(channels // BINS, BINS, -1, R2).transpose(0, 2, 1, 3).reshape(-1, R2)
    copies = ROUNDS * 3 * (3 + 3 + 4 * len(LINES))
    anywhere = pl.BlockSpec(memory_space=pl.ANY)
    scalars = pl.BlockSpec(memory_space=pltpu.SMEM)
    dma = pltpu.SemaphoreType.DMA
    bf16, f32 = jnp.bfloat16, jnp.float32
    landed = pl.pallas_call(
        kernel,
        in_specs=[anywhere] * 4 + [scalars] * 3,
        out_specs=anywhere,
        out_shape=jax.ShapeDtypeStruct((2 * SIDE, 256, LAGS), bf16),
        scratch_shapes=[
            pltpu.VMEM(tiles.shape, f32),
            pltpu.VMEM((3 * R1, R2), f32),
            pltpu.VMEM((R2, 2 * R2), bf16),
            pltpu.VMEM((LAGS, NF), bf16),
            pltpu.VMEM((3, 2, 2, SIDE * 2, R2, lanes // 2), bf16),
            pltpu.VMEM((2, SIDE * 2, 2, R2, lanes // 2), bf16),
            pltpu.VMEM((2, SIDE * 2, 2, R2, lanes // 2), bf16),
            pltpu.VMEM((2, SIDE * 2, 2, 2 * BINS, lanes // 2), bf16),
            pltpu.VMEM((2, SIDE * 2, 2, 2 * BINS, lanes // 2), bf16),
            pltpu.VMEM((SIDE, 2, 2, SIDE, PIECE, SRC_BLOCK), bf16),
            pltpu.VMEM((2, SLOTS, 256, 256), bf16),
            pltpu.VMEM((NF // 2, 2 * columns), bf16),
            pltpu.VMEM((2 * channels, LAGS, SRC_BLOCK), f32),
            pltpu.VMEM((channels, LAGS, SRC_BLOCK), bf16),
            pltpu.VMEM((channels, LAGS, SRC_BLOCK), bf16),
            pltpu.VMEM((2, columns, R2), f32),
            pltpu.VMEM((2 * SIDE, 256, LAGS), bf16),
            dma((4,)), dma((copies,)), dma((copies,)), dma((4,)), dma((4,)),
            dma((14,)), dma((14,)), dma((14,)), dma((14,)), dma((7,)), dma((7,)),
        ],
        compiler_params=pltpu.CompilerParams(
            vmem_limit_bytes=62 * 2**20, collective_id=1, has_side_effects=True),
        cost_estimate=pl.CostEstimate(flops=4 * 256 * 4096 * 2048, bytes_accessed=20 * 2**20, transcendentals=0),
    )(tiles, jnp.asarray(row_tables()), jnp.asarray(short_dft(), dtype=bf16),
      jnp.asarray(lag_table(), dtype=bf16), source_block, source_offset, window_valid)
    rows = landed.reshape(2 * SIDE, -1, channels, LAGS)
    turned = jnp.einsum("tu,bscu->stbc", jnp.eye(LAGS, dtype=bf16), rows, preferred_element_type=f32)
    return turned.astype(bf16).reshape(-1, LAGS, 2 * SIDE * channels)


def solution(mesh):
    in_specs = (P(("chan", "band"), None), P(), P(), P())
    out_specs = P("band", None, "chan")
    return jax.shard_map(body, mesh=mesh, in_specs=in_specs, out_specs=out_specs, check_vma=False)
```

```python
import functools
import math

import jax
import jax.numpy as jnp
import numpy as np
from jax import lax
from jax.experimental import pallas as pl
from jax.experimental.pallas import tpu as pltpu
from jax.sharding import PartitionSpec as P

L = 4096
HOP = 2048
NF = 2048
W = 16
SRC_BLOCK = 128
LAGS = 256
R1 = 32
R2 = 128
HALF = R2 // 2
BINS = 8
FACTOR = 1.0 / (W * math.sqrt(NF))


def window_table():
    points = np.arange(L, dtype=np.float32)
    angle = (points * np.float32(2.0 * math.pi / L)).astype(np.float32)
    return (np.float32(0.5) - np.float32(0.5) * np.cos(angle)).astype(np.float32).reshape(R1, R2)


def row_tables():
    angle = 2.0 * np.pi * np.outer(np.arange(R1), np.arange(R2)) / L
    return np.concatenate([window_table(), np.cos(angle), -np.sin(angle)], axis=0).astype(np.float32)


def short_dft():
    angle = 2.0 * np.pi * (np.outer(np.arange(HALF), np.arange(R2)) % R2) / R2
    cosine, sine = np.cos(angle), np.sin(angle)
    top = np.concatenate([cosine, sine], axis=1)
    low = np.concatenate([-sine, cosine], axis=1)
    both = np.stack([top.reshape(-1, BINS, 2 * R2), low.reshape(-1, BINS, 2 * R2)], axis=1)
    return both.reshape(R2, 2 * R2).astype(np.float32)


def lag_table():
    core, g, x, y_hi, y_lo, z, i = np.ix_(*[np.arange(n) for n in (2, 2, 4, 2, 2, 4, 8)])
    bins = 8 * x + 4 * y_hi + 2 * core + g + R1 * (32 * y_lo + 8 * z + i)
    lags = (np.arange(LAGS) - LAGS // 2).reshape((1, LAGS) + (1,) * 6)
    angle = 2.0 * np.pi * (lags * bins[:, None] % L) / L
    table = np.stack([np.cos(angle), -np.sin(angle)], axis=7)
    return table.reshape(2, LAGS, NF).astype(np.float32)


def real_dft(x):
    n = len(x)
    if n == 2:
        return [(x[0] + x[1], None), (x[0] - x[1], None)]
    even, odd = real_dft(x[0::2]), real_dft(x[1::2])
    out = [None] * (n // 2 + 1)
    for k in range(n // 4 + 1):
        er, ei = even[k]
        orr, oi = odd[k]
        if k == 0:
            out[0] = (er + orr, None)
            out[n // 2] = (er - orr, None)
            continue
        if 4 * k == n:
            out[k] = (er, -orr)
            continue
        c, s = math.cos(2 * math.pi * k / n), -math.sin(2 * math.pi * k / n)
        if oi is None:
            tr, ti = orr * c, orr * s
        else:
            tr, ti = orr * c - oi * s, orr * s + oi * c
        zi = ti if ei is None else ei + ti
        yi = -ti if ei is None else ei - ti
        out[k] = (er + tr, zi)
        out[n // 2 - k] = (er - tr, -yi)
    return out


SIDE = 4
SLOTS = SIDE ** 3
PIECE = 2 * 2 * BINS * W
PARTS = (((0, 96, (0, 1, 2)), (96, 80, (1, 2, 0)), (176, 80, (2, 0, 1))),
         ((0, 80, (0, 1, 2)), (80, 96, (1, 2, 0)), (176, 80, (2, 0, 1))))
LINES = (0, -1, 1, 2)
ROUNDS = 2
MESH = pl.DeviceIdType.MESH


def position():
    chan, band = lax.axis_index("chan"), lax.axis_index("band")
    return (chan // 4, chan // 2 % 2 * 2 + band // 4, band % 4), chan % 2


def device_at(at, core):
    x, y, z = at
    return (x * 4 + y // 2 * 2 + core, y % 2 * 4 + z)


def neighbour(axis, step):
    at, core = position()
    moved = list(at)
    moved[axis] = lax.rem(at[axis] + step + SIDE, SIDE)
    return device_at(moved, core)


def slots(ref, at, full, first, count):
    whole = slice(None)
    x = whole if 0 in full else at[0]
    y_hi, y_lo = (whole, whole) if 1 in full else (at[1] // 2, at[1] % 2)
    z = whole if 2 in full else at[2]
    return ref.at[x, y_hi, y_lo, z, pl.ds(first, count), :]


def partners(at, core):
    x, y, z = at
    side = lambda step: lax.rem(z + step, SIDE)
    along = [((lax.rem(x + dx, SIDE), y ^ (2 * dy), z), core) for dx in (2, 1, 3, 0) for dy in (1, 0)][:-1]
    across = [((x, y ^ dy, side(dz)), core) for dz in (2, 1, 3, 0) for dy in (1, 0)][:-1]
    return along, across, [((x, y ^ 3, z), core), (at, 1 - core)]


def kernel(strain_hbm, rows_hbm, dft_hbm, tables, block, offset, valid, landed,
           strain, rows, dft, table, held, mixed, parts, share, bands, spectra, left, cross, total,
           outgoing, incoming, turned, shipped,
           local_sem, send_sem, recv_sem, side_send, side_recv, chan_send, chan_recv, band_send, band_recv,
           ship_send, ship_recv):
    at, core = position()
    chan, band = lax.axis_index("chan"), lax.axis_index("band")
    sibling = device_at(at, 1 - core)
    lanes = held.shape[-1]
    channels = lanes // W
    columns = channels * SRC_BLOCK
    along, across, rest = partners(at, core)

    def fetch(src, dst, index):
        copy = pltpu.make_async_copy(src, dst, local_sem.at[index])
        copy.start()
        return copy

    fetched = [fetch(strain_hbm, strain, 0), fetch(rows_hbm, rows, 1), fetch(dft_hbm, dft, 2)]
    own_table = fetch(tables.at[core], table, 3)
    barrier = pltpu.get_barrier_semaphore()
    for place, which in along + across + rest:
        pl.semaphore_signal(barrier, inc=1, device_id=device_at(place, which), device_id_type=MESH)
    for copy in fetched:
        copy.wait()

    folded = left.at[0]

    def fold(c, _):
        first = c // BINS * (BINS * (W + 1) * W) + c % BINS
        x = [strain[pl.ds(first + BINS * k, W, stride=BINS * W), :] for k in range(R1)]
        whole = x[0]
        for k in range(1, R1):
            whole = whole + x[k]
        mean = jnp.sum(whole, axis=1, keepdims=True) * (1.0 / L)
        x = [((x[k] - mean) * rows[k:k + 1, :]).astype(jnp.bfloat16).astype(jnp.float32) for k in range(R1)]
        bins = real_dft(x)
        to = pl.ds(pl.multiple_of(c * W, W), W)
        for f in range(R1):
            re, im = bins[f] if f <= R1 // 2 else bins[R1 - f]
            cosine, sine = rows[R1 + f:R1 + f + 1, :], rows[2 * R1 + f:2 * R1 + f + 1, :]
            if im is None:
                gr, gi = re * cosine, re * sine
            else:
                im = im if f <= R1 // 2 else -im
                gr, gi = re * cosine - im * sine, re * sine + im * cosine
            folded[f, to, :R2] = gr.astype(jnp.bfloat16)
            folded[f, to, R2:] = gi.astype(jnp.bfloat16)
        return 0

    lax.fori_loop(0, channels, fold, 0, unroll=2)
    dft_table = dft[...]

    def transform(f, power):
        y = lax.dot_general(dft_table, folded[f], (((1,), (1,)), ((), ())), preferred_element_type=jnp.float32)
        total[f, :R2, :] = y[:, :R2]
        total[f, R2:, :] = y[:, R2:]
        square = (y * y).reshape(HALF // BINS, 2, BINS, lanes)
        return power + (square[:, 0] + square[:, 1]).reshape(HALF, lanes)

    power = lax.fori_loop(0, R1, transform, jnp.zeros((HALF, lanes), jnp.float32), unroll=8)
    scales = []
    for b in range(HALF // BINS):
        mean = jnp.sum(power[b * BINS:(b + 1) * BINS], axis=0, keepdims=True) * (1.0 / 256.0)
        scales.append(jnp.broadcast_to(lax.rsqrt(mean + 1e-06), (2 * BINS, lanes)))
    scale = jnp.concatenate(scales, axis=0)

    def finish_white(to, which, g):
        def step(index, _):
            f = index * 4 + which * 2 + g
            y = jnp.concatenate([total[f, :R2, :], total[f, R2:, :]], axis=1)
            held[to, g, index] = (y * scale).astype(jnp.bfloat16)
            return 0

        lax.fori_loop(0, SIDE * 2, step, 0, unroll=4)

    for g in range(2):
        finish_white(2, 1 - core, g)
    pl.semaphore_wait(barrier, len(along) + len(across) + len(rest))
    swaps = []
    for g in range(2):
        swap = pltpu.make_async_remote_copy(
            src_ref=held.at[2, g], dst_ref=held.at[1, g], send_sem=side_send.at[g], recv_sem=side_recv.at[g],
            device_id=sibling, device_id_type=MESH)
        swap.start()
        swaps.append(swap)
    for g in range(2):
        finish_white(0, core, g)

    row = lax.broadcasted_iota(jnp.int32, (2 * BINS, R2), 0) % BINS
    lane = lax.broadcasted_iota(jnp.int32, (2 * BINS, R2), 1)
    own = lane // W == row

    def spread(core_index):
        def step(index, _):
            x, y_hi, y_lo, z = index // 16, index // 8 % 2, index // 4 % 2, index % 4
            picked = pl.ds(pl.multiple_of((y_lo * SIDE + z) * 16, 16), 16)
            for g in range(2):
                for k in range(channels // 8):
                    value = held[core_index, g, x * 2 + y_hi, picked, k * R2:(k + 1) * R2].astype(jnp.float32)
                    for ri in range(2):
                        even = pltpu.roll(value[ri * BINS:(ri + 1) * BINS], 0, 1, stride=W, stride_axis=0)
                        both = jnp.concatenate([even, pltpu.roll(even, R2 - W, 1)], axis=0)
                        for t in range(4):
                            moved = pltpu.roll(both, R2 - 2 * W * t, 1) if t else both
                            first = ((core_index * channels // 8 + k) * 4 + t) * 2 * BINS
                            left[g, index, first:first + 2 * BINS, ri * R2:(ri + 1) * R2] = jnp.where(
                                own, moved, 0.0).astype(jnp.bfloat16)
            return 0

        return step

    lax.fori_loop(0, 8, spread(0), 0)

    spot = lax.broadcasted_iota(jnp.int32, (1, lanes), 1)
    source = band * channels + spot // W
    stacked = jnp.zeros((1, lanes), jnp.float32)
    for w in range(W):
        stacked = jnp.where(spot % W == w, jnp.where(valid[w] != 0, 1.0, 0.0), stacked)
    chans = R1 // 2

    def chosen(which):
        first = jnp.where(which == block[0], 1, 0)
        second = jnp.where(which == lax.rem(block[0] + 1, chans), 1, 0)
        taken = jnp.where(source >= offset[0], first, second)
        return jnp.where(taken == 1, stacked, 0.0)

    mine, theirs = chosen(chan), chosen(chan ^ 1)
    slot = chan // 2

    def mix(g):
        def step(index, _):
            a, b = held[0, g, index], held[1, g, index]
            value = a.astype(jnp.float32) * mine + b.astype(jnp.float32) * theirs
            mixed[g, index] = value.astype(jnp.bfloat16)
            return 0

        return step

    sums, moves = {}, {}
    for g in range(2):
        swaps[g].wait_recv()
        lax.fori_loop(0, SIDE * 2, mix(g), 0, unroll=4)
        sums[g] = []
        for r, (place, which) in enumerate(along):
            target = place[0] * 2 + place[1] // 2
            sums[g].append(pltpu.make_async_remote_copy(
                src_ref=mixed.at[g, target], dst_ref=parts.at[g, slot],
                send_sem=chan_send.at[g * 7 + r], recv_sem=chan_recv.at[g * 7 + r],
                device_id=device_at(place, which), device_id_type=MESH))
        for copy in sums[g]:
            copy.start()

    def to_bands(g):
        for copy in sums[g]:
            copy.wait_recv()
        parts[g, slot] = mixed[g, slot]
        value = parts[g, 0].astype(jnp.float32)
        for k in range(1, SIDE * 2):
            value = value + parts[g, k].astype(jnp.float32)
        share[g] = value.astype(jnp.bfloat16).reshape(2 * SIDE, 2 * BINS, lanes)
        moves[g] = []
        for r, (place, which) in enumerate(across):
            moves[g].append(pltpu.make_async_remote_copy(
                src_ref=share.at[g, place[1] % 2 * SIDE + place[2]], dst_ref=bands.at[g, band],
                send_sem=band_send.at[g * 7 + r], recv_sem=band_recv.at[g * 7 + r],
                device_id=device_at(place, which), device_id_type=MESH))
        for copy in moves[g]:
            copy.start()
        bands[g, band] = share[g, band]

    def arrange(g):
        for copy in moves[g]:
            copy.wait_recv()
        wide = (2 * BINS * W, lanes)
        same = lax.broadcasted_iota(jnp.int32, wide, 1) % W == lax.broadcasted_iota(jnp.int32, wide, 0) % W
        tall = (lanes, SRC_BLOCK)
        channel = lax.broadcasted_iota(jnp.int32, tall, 0) // W
        column = lax.broadcasted_iota(jnp.int32, tall, 1)
        value = None
        for b in range(2 * SIDE):
            goal = (channel + (b * channels + SRC_BLOCK) - offset[0]) % SRC_BLOCK
            pick = jnp.where(goal == column, 1.0, 0.0).astype(jnp.bfloat16)
            part = bands[g, b].astype(jnp.float32)
            part = jnp.broadcast_to(part[:, None, :], (2 * BINS, W, lanes)).reshape(wide)
            part = jnp.where(same, part, 0.0).astype(jnp.bfloat16)
            term = jnp.dot(part, pick, preferred_element_type=jnp.float32)
            value = term if value is None else value + term
        spectra[at[0], at[1] // 2, at[1] % 2, at[2], g * wide[0]:(g + 1) * wide[0], :] = value.astype(jnp.bfloat16)

    copies = {}

    def send(key, ref, axis, step):
        index = len(copies)
        copies[key] = pltpu.make_async_remote_copy(
            src_ref=ref, dst_ref=ref, send_sem=send_sem.at[index], recv_sem=recv_sem.at[index],
            device_id=neighbour(axis, step), device_id_type=MESH)
        copies[key].start()

    def shifted(order, line, step):
        moved = list(at)
        for axis, by in ((order[1], LINES[line]), (order[2], step)):
            moved[axis] = lax.rem(at[axis] + by + SIDE, SIDE)
        return moved

    def begin(turn, stage):
        for part, (first, count, order) in enumerate(PARTS[turn]):
            ref = slots(spectra, at, order[:stage], turn * 256 + first, count)
            for kind, step in enumerate((1, -1, 2)):
                send((turn, stage, part, kind), ref, order[stage], step)

    def finish(turn, stage):
        for part in range(3):
            for kind in range(3):
                copies[turn, stage, part, kind].wait_recv()

    def send_line(turn, line):
        for part, (first, count, order) in enumerate(PARTS[turn]):
            if line:
                copies[turn, 1, part, line - 1].wait_recv()
            ref = slots(spectra, shifted(order, line, 0), order[:1], turn * 256 + first, count)
            for kind, step in enumerate((1, -1)):
                send((turn, 2, part, kind, line), ref, order[2], step)

    def forward(turn, line):
        for part, (first, count, order) in enumerate(PARTS[turn]):
            low = (count // 32 + (count // 16) % 2 * (line % 2)) * 16
            shares = ((1, -1, 0, low), (-1, 1, low, count - low))
            for kind, (step, origin, skip, rows_sent) in enumerate(shares):
                copies[turn, 2, part, kind, line].wait_recv()
                ref = slots(spectra, shifted(order, line, origin), order[:1], turn * 256 + first + skip, rows_sent)
                send((turn, 2, part, kind + 2, line), ref, order[2], step)

    def finish_lines(turn):
        for line in range(len(LINES)):
            for part in range(3):
                for kind in (2, 3):
                    copies[turn, 2, part, kind, line].wait_recv()

    def multiply(turn, place=lambda index: index):
        def step(index, _):
            k = place(index)
            s = spectra[k // 16, k // 8 % 2, k // 4 % 2, k % 4, turn * 256:(turn + 1) * 256, :]
            right = jnp.concatenate([s, jnp.concatenate([-s[R2:], s[:R2]], axis=0)], axis=1)
            result = jnp.dot(left[turn, k], right, preferred_element_type=jnp.float32)
            base = pl.multiple_of(k * 16, 16)
            for c in range(2 * channels):
                both = result[c * BINS:(c + 1) * BINS]
                both = jnp.concatenate([both[:, :SRC_BLOCK], both[:, SRC_BLOCK:]], axis=0)
                cross[pl.ds(base, 16), c * SRC_BLOCK:(c + 1) * SRC_BLOCK] = both.astype(jnp.bfloat16)
            return 0

        return step

    def near(digit):
        return digit + digit // 2

    def shift(dx, dy, dz):
        x, y, z = [lax.rem(a + b, SIDE) for a, b in zip(at, (dx, dy, dz))]
        return x * 16 + y * 4 + z

    group = 8
    width = group * SRC_BLOCK

    def sum_lags(turn, core_index, n, store):
        both = slice(core_index * columns + n * width, core_index * columns + (n + 1) * width)
        value = jnp.dot(table[:, turn * 1024:(turn + 1) * 1024], cross[:, both], preferred_element_type=jnp.float32)
        for i in range(group):
            store(n * group + i, core_index * channels + n * group + i, value[:, i * SRC_BLOCK:(i + 1) * SRC_BLOCK])

    def keep(c, held_c, value):
        total[held_c] = value

    def hand_over(c, held_c, value):
        outgoing[c] = ((total[held_c] + value) * FACTOR).astype(jnp.bfloat16)

    def conclude(c, held_c, value):
        total[held_c] = total[held_c] + value

    pairs = SLOTS // 2
    lax.fori_loop(8, SLOTS, spread(0), 0)
    to_bands(0)
    lax.fori_loop(0, 8, spread(1), 0)
    to_bands(1)
    lax.fori_loop(8, 28, spread(1), 0)
    arrange(0)
    begin(0, 0)
    arrange(1)
    begin(1, 0)
    lax.fori_loop(28, 36, spread(1), 0)
    finish(0, 0)
    begin(0, 1)
    send_line(0, 0)
    finish(1, 0)
    begin(1, 1)
    lax.fori_loop(36, 46, spread(1), 0)
    for line in (1, 2, 3):
        send_line(0, line)
    forward(0, 0)
    lax.fori_loop(46, 56, spread(1), 0)
    forward(0, 1)
    send_line(1, 0)
    lax.fori_loop(56, SLOTS, spread(1), 0)
    forward(0, 2)
    forward(0, 3)
    for line in (1, 2, 3):
        send_line(1, line)
    own_table.wait()
    finish_lines(0)
    quarter = SLOTS // 4
    for line in range(4):
        lax.fori_loop(line * quarter, (line + 1) * quarter, multiply(0), 0, unroll=4)
        forward(1, line)
    for core_index in range(2):
        for n in range(channels // group):
            sum_lags(0, core_index, n, keep)
    lax.fori_loop(0, 27, multiply(1, lambda i: shift(near(i // 9), near(i // 3 % 3), near(i % 3))), 0, unroll=3)
    finish_lines(1)
    lax.fori_loop(0, 16, multiply(1, lambda i: shift(2, i // 4, i % 4)), 0, unroll=4)
    lax.fori_loop(0, 12, multiply(1, lambda i: shift(near(i // 4), 2, i % 4)), 0, unroll=4)
    lax.fori_loop(0, 9, multiply(1, lambda i: shift(near(i // 3), near(i % 3), 2)), 0, unroll=3)
    exchanges = []
    for n in range(channels // group):
        sum_lags(1, 1, n, hand_over)
        some = pl.ds(n * group, group)
        exchange = pltpu.make_async_remote_copy(
            src_ref=outgoing.at[some], dst_ref=incoming.at[some], send_sem=side_send.at[2 + n],
            recv_sem=side_recv.at[2 + n], device_id=sibling, device_id_type=MESH)
        exchange.start()
        exchanges.append(exchange)
    for n in range(channels // group):
        sum_lags(1, 0, n, conclude)

    unit = identity(SRC_BLOCK)
    last = (((1,), (1,)), ((), ()))
    for c in range(channels):
        if c % group == 0:
            exchanges[c // group].wait_recv()
        value = (total[c] * FACTOR + incoming[c].astype(jnp.float32)).astype(jnp.bfloat16)
        value = lax.dot_general(unit, value, last, preferred_element_type=jnp.float32)
        for half in range(2):
            turned[half, pl.ds(c, SRC_BLOCK, stride=channels), :] = value[:, half * R2:(half + 1) * R2]

    def pack(index):
        picked = pl.ds(pl.multiple_of(index * 256, 256), 256)
        both = jnp.concatenate([turned[0, picked, :], turned[1, picked, :]], axis=1).astype(jnp.bfloat16)
        return both.reshape(-1, channels, LAGS)

    ships = []
    for r, (place, which) in enumerate(across):
        index = place[1] % 2 * SIDE + place[2]
        shipped[index] = pack(index)
        ship = pltpu.make_async_remote_copy(
            src_ref=shipped.at[index], dst_ref=landed.at[:, band], send_sem=ship_send.at[r], recv_sem=ship_recv.at[r],
            device_id=device_at(place, which), device_id_type=MESH)
        ship.start()
        ships.append(ship)
    shipped[band] = pack(band)
    kept = pltpu.make_async_copy(shipped.at[band], landed.at[:, band], local_sem.at[0])
    kept.start()
    for ship in ships:
        ship.wait_recv()

    kept.wait()
    for copy in swaps + exchanges + sums[0] + sums[1] + moves[0] + moves[1] + ships + list(copies.values()):
        copy.wait_send()


def identity(n):
    diagonal = lax.broadcasted_iota(jnp.int32, (n, n), 0) == lax.broadcasted_iota(jnp.int32, (n, n), 1)
    return jnp.where(diagonal, 1.0, 0.0).astype(jnp.bfloat16)


def body(strain, source_block, source_offset, window_valid):
    channels = strain.shape[0]
    lanes = channels * W
    columns = channels * SRC_BLOCK
    tiles = strain.reshape(channels // BINS, BINS, -1, R2).transpose(0, 2, 1, 3).reshape(-1, R2)
    copies = ROUNDS * 3 * (3 + 3 + 4 * len(LINES))
    anywhere = pl.BlockSpec(memory_space=pl.ANY)
    scalars = pl.BlockSpec(memory_space=pltpu.SMEM)
    dma = pltpu.SemaphoreType.DMA
    bf16, f32 = jnp.bfloat16, jnp.float32
    landed = pl.pallas_call(
        kernel,
        in_specs=[anywhere] * 4 + [scalars] * 3,
        out_specs=anywhere,
        out_shape=jax.ShapeDtypeStruct((SRC_BLOCK // (2 * SIDE), 2 * SIDE, channels, LAGS), bf16),
        scratch_shapes=[
            pltpu.VMEM(tiles.shape, f32),
            pltpu.VMEM((3 * R1, R2), f32),
            pltpu.VMEM((R2, 2 * R2), bf16),
            pltpu.VMEM((LAGS, NF), bf16),
            pltpu.VMEM((3, 2, SIDE * 2, R2, lanes), bf16),
            pltpu.VMEM((2, SIDE * 2, R2, lanes), bf16),
            pltpu.VMEM((2, SIDE * 2, R2, lanes), bf16),
            pltpu.VMEM((2, SIDE * 2, 2 * BINS, lanes), bf16),
            pltpu.VMEM((2, SIDE * 2, 2 * BINS, lanes), bf16),
            pltpu.VMEM((SIDE, 2, 2, SIDE, PIECE, SRC_BLOCK), bf16),
            pltpu.VMEM((2, SLOTS, 256, 256), bf16),
            pltpu.VMEM((NF // 2, 2 * columns), bf16),
            pltpu.VMEM((2 * channels, LAGS, SRC_BLOCK), f32),
            pltpu.VMEM((channels, LAGS, SRC_BLOCK), bf16),
            pltpu.VMEM((channels, LAGS, SRC_BLOCK), bf16),
            pltpu.VMEM((2, columns, R2), f32),
            pltpu.VMEM((2 * SIDE, SRC_BLOCK // (2 * SIDE), channels, LAGS), bf16),
            dma((4,)), dma((copies,)), dma((copies,)), dma((4,)), dma((4,)),
            dma((14,)), dma((14,)), dma((14,)), dma((14,)), dma((7,)), dma((7,)),
        ],
        compiler_params=pltpu.CompilerParams(
            vmem_limit_bytes=62 * 2**20, collective_id=1, has_side_effects=True),
        cost_estimate=pl.CostEstimate(flops=4 * 256 * 4096 * 2048, bytes_accessed=20 * 2**20, transcendentals=0),
    )(tiles, jnp.asarray(row_tables()), jnp.asarray(short_dft(), dtype=bf16),
      jnp.asarray(lag_table(), dtype=bf16), source_block, source_offset, window_valid)
    rows = landed.reshape(-1, 2 * SIDE * channels, LAGS)
    return jnp.einsum("tu,scu->stc", jnp.eye(LAGS, dtype=bf16), rows, preferred_element_type=f32).astype(bf16)


def solution(mesh):
    in_specs = (P(("chan", "band"), None), P(), P(), P())
    out_specs = P("band", None, "chan")
    return jax.shard_map(body, mesh=mesh, in_specs=in_specs, out_specs=out_specs, check_vma=False)
```

```python
import functools
import math

import jax
import jax.numpy as jnp
import numpy as np
from jax import lax
from jax.experimental import pallas as pl
from jax.experimental.pallas import tpu as pltpu
from jax.sharding import PartitionSpec as P

L = 4096
HOP = 2048
NF = 2048
W = 16
SRC_BLOCK = 128
LAGS = 256
R1 = 32
R2 = 128
HALF = R2 // 2
BINS = 8
FACTOR = 1.0 / (W * math.sqrt(NF))


def window_table():
    points = np.arange(L, dtype=np.float32)
    angle = (points * np.float32(2.0 * math.pi / L)).astype(np.float32)
    return (np.float32(0.5) - np.float32(0.5) * np.cos(angle)).astype(np.float32).reshape(R1, R2)


def row_tables():
    angle = 2.0 * np.pi * np.outer(np.arange(R1), np.arange(R2)) / L
    return np.concatenate([window_table(), np.cos(angle), -np.sin(angle)], axis=0).astype(np.float32)


def short_dft():
    angle = 2.0 * np.pi * (np.outer(np.arange(HALF), np.arange(R2)) % R2) / R2
    cosine, sine = np.cos(angle), np.sin(angle)
    top = np.concatenate([cosine, sine], axis=1)
    low = np.concatenate([-sine, cosine], axis=1)
    both = np.stack([top.reshape(-1, BINS, 2 * R2), low.reshape(-1, BINS, 2 * R2)], axis=1)
    return both.reshape(R2, 2 * R2).astype(np.float32)


def lag_table():
    core, g, x, y_hi, y_lo, z, i = np.ix_(*[np.arange(n) for n in (2, 2, 4, 2, 2, 4, 8)])
    bins = 8 * x + 4 * y_hi + 2 * core + g + R1 * (32 * y_lo + 8 * z + i)
    lags = (np.arange(LAGS) - LAGS // 2).reshape((1, LAGS) + (1,) * 6)
    angle = 2.0 * np.pi * (lags * bins[:, None] % L) / L
    table = np.stack([np.cos(angle), -np.sin(angle)], axis=7)
    return table.reshape(2, LAGS, NF).astype(np.float32)


def real_dft(x):
    n = len(x)
    if n == 2:
        return [(x[0] + x[1], None), (x[0] - x[1], None)]
    even, odd = real_dft(x[0::2]), real_dft(x[1::2])
    out = [None] * (n // 2 + 1)
    for k in range(n // 4 + 1):
        er, ei = even[k]
        orr, oi = odd[k]
        if k == 0:
            out[0] = (er + orr, None)
            out[n // 2] = (er - orr, None)
            continue
        if 4 * k == n:
            out[k] = (er, -orr)
            continue
        c, s = math.cos(2 * math.pi * k / n), -math.sin(2 * math.pi * k / n)
        if oi is None:
            tr, ti = orr * c, orr * s
        else:
            tr, ti = orr * c - oi * s, orr * s + oi * c
        zi = ti if ei is None else ei + ti
        yi = -ti if ei is None else ei - ti
        out[k] = (er + tr, zi)
        out[n // 2 - k] = (er - tr, -yi)
    return out


SIDE = 4
SLOTS = SIDE ** 3
PIECE = 2 * 2 * BINS * W
PARTS = (((0, 96, (0, 1, 2)), (96, 80, (1, 2, 0)), (176, 80, (2, 0, 1))),
         ((0, 80, (0, 1, 2)), (80, 96, (1, 2, 0)), (176, 80, (2, 0, 1))))
LINES = (0, -1, 1, 2)
ROUNDS = 2
MESH = pl.DeviceIdType.MESH


def position():
    chan, band = lax.axis_index("chan"), lax.axis_index("band")
    return (chan // 4, chan // 2 % 2 * 2 + band // 4, band % 4), chan % 2


def device_at(at, core):
    x, y, z = at
    return (x * 4 + y // 2 * 2 + core, y % 2 * 4 + z)


def neighbour(axis, step):
    at, core = position()
    moved = list(at)
    moved[axis] = lax.rem(at[axis] + step + SIDE, SIDE)
    return device_at(moved, core)


def slots(ref, at, full, first, count):
    whole = slice(None)
    x = whole if 0 in full else at[0]
    y_hi, y_lo = (whole, whole) if 1 in full else (at[1] // 2, at[1] % 2)
    z = whole if 2 in full else at[2]
    return ref.at[x, y_hi, y_lo, z, pl.ds(first, count), :]


def partners(at, core):
    x, y, z = at
    side = lambda step: lax.rem(z + step, SIDE)
    along = [((lax.rem(x + dx, SIDE), y ^ (2 * dy), z), core) for dx in (2, 1, 3, 0) for dy in (1, 0)][:-1]
    across = [((x, y ^ dy, side(dz)), core) for dz in (2, 1, 3, 0) for dy in (1, 0)][:-1]
    return along, across, [((x, y ^ 3, z), core), (at, 1 - core)]


def kernel(strain_hbm, rows_hbm, dft_hbm, tables, block, offset, valid, landed,
           strain, rows, dft, table, held, mixed, parts, share, bands, spectra, left, cross, total,
           outgoing, incoming, turned, shipped,
           local_sem, send_sem, recv_sem, side_send, side_recv, chan_send, chan_recv, band_send, band_recv,
           ship_send, ship_recv):
    at, core = position()
    chan, band = lax.axis_index("chan"), lax.axis_index("band")
    sibling = device_at(at, 1 - core)
    lanes = held.shape[-1]
    channels = lanes // W
    columns = channels * SRC_BLOCK
    along, across, rest = partners(at, core)

    def fetch(src, dst, index):
        copy = pltpu.make_async_copy(src, dst, local_sem.at[index])
        copy.start()
        return copy

    fetched = [fetch(strain_hbm, strain, 0), fetch(rows_hbm, rows, 1), fetch(dft_hbm, dft, 2)]
    own_table = fetch(tables.at[core], table, 3)
    barrier = pltpu.get_barrier_semaphore()
    for place, which in along + across + rest:
        pl.semaphore_signal(barrier, inc=1, device_id=device_at(place, which), device_id_type=MESH)
    for copy in fetched:
        copy.wait()

    folded = left.at[0]

    def fold(c, _):
        first = c // BINS * (BINS * (W + 1) * W) + c % BINS
        x = [strain[pl.ds(first + BINS * k, W, stride=BINS * W), :] for k in range(R1)]
        whole = x[0]
        for k in range(1, R1):
            whole = whole + x[k]
        mean = jnp.sum(whole, axis=1, keepdims=True) * (1.0 / L)
        x = [((x[k] - mean) * rows[k:k + 1, :]).astype(jnp.bfloat16).astype(jnp.float32) for k in range(R1)]
        bins = real_dft(x)
        to = pl.ds(pl.multiple_of(c * W, W), W)
        for f in range(R1):
            re, im = bins[f] if f <= R1 // 2 else bins[R1 - f]
            cosine, sine = rows[R1 + f:R1 + f + 1, :], rows[2 * R1 + f:2 * R1 + f + 1, :]
            if im is None:
                gr, gi = re * cosine, re * sine
            else:
                im = im if f <= R1 // 2 else -im
                gr, gi = re * cosine - im * sine, re * sine + im * cosine
            folded[f, to, :R2] = gr.astype(jnp.bfloat16)
            folded[f, to, R2:] = gi.astype(jnp.bfloat16)
        return 0

    lax.fori_loop(0, channels, fold, 0, unroll=2)
    dft_table = dft[...]

    def transform(f, power):
        y = lax.dot_general(dft_table, folded[f], (((1,), (1,)), ((), ())), preferred_element_type=jnp.float32)
        total[f, :R2, :] = y[:, :R2]
        total[f, R2:, :] = y[:, R2:]
        square = (y * y).reshape(HALF // BINS, 2, BINS, lanes)
        return power + (square[:, 0] + square[:, 1]).reshape(HALF, lanes)

    power = lax.fori_loop(0, R1, transform, jnp.zeros((HALF, lanes), jnp.float32), unroll=8)
    scales = []
    for b in range(HALF // BINS):
        mean = jnp.sum(power[b * BINS:(b + 1) * BINS], axis=0, keepdims=True) * (1.0 / 256.0)
        scales.append(jnp.broadcast_to(lax.rsqrt(mean + 1e-06), (2 * BINS, lanes)))
    scale = jnp.concatenate(scales, axis=0)

    def finish_white(to, which, g):
        def step(index, _):
            f = index * 4 + which * 2 + g
            y = jnp.concatenate([total[f, :R2, :], total[f, R2:, :]], axis=1)
            held[to, g, index] = (y * scale).astype(jnp.bfloat16)
            return 0

        lax.fori_loop(0, SIDE * 2, step, 0, unroll=4)

    for g in range(2):
        finish_white(2, 1 - core, g)
    pl.semaphore_wait(barrier, len(along) + len(across) + len(rest))
    swaps = []
    for g in range(2):
        swap = pltpu.make_async_remote_copy(
            src_ref=held.at[2, g], dst_ref=held.at[1, g], send_sem=side_send.at[g], recv_sem=side_recv.at[g],
            device_id=sibling, device_id_type=MESH)
        swap.start()
        swaps.append(swap)
    for g in range(2):
        finish_white(0, core, g)

    row = lax.broadcasted_iota(jnp.int32, (2 * BINS, R2), 0) % BINS
    lane = lax.broadcasted_iota(jnp.int32, (2 * BINS, R2), 1)
    own = lane // W == row

    def spread(core_index):
        def step(index, _):
            x, y_hi, y_lo, z = index // 16, index // 8 % 2, index // 4 % 2, index % 4
            picked = pl.ds(pl.multiple_of((y_lo * SIDE + z) * 16, 16), 16)
            for g in range(2):
                for k in range(channels // 8):
                    value = held[core_index, g, x * 2 + y_hi, picked, k * R2:(k + 1) * R2].astype(jnp.float32)
                    for ri in range(2):
                        even = pltpu.roll(value[ri * BINS:(ri + 1) * BINS], 0, 1, stride=W, stride_axis=0)
                        both = jnp.concatenate([even, pltpu.roll(even, R2 - W, 1)], axis=0).astype(jnp.bfloat16)
                        for t in range(4):
                            moved = pltpu.roll(both, R2 - 2 * W * t, 1) if t else both
                            first = ((core_index * channels // 8 + k) * 4 + t) * 2 * BINS
                            left[g, index, first:first + 2 * BINS, ri * R2:(ri + 1) * R2] = jnp.where(
                                own, moved, jnp.zeros_like(moved))
            return 0

        return step

    lax.fori_loop(0, 8, spread(0), 0, unroll=4)

    spot = lax.broadcasted_iota(jnp.int32, (1, lanes), 1)
    source = band * channels + spot // W
    stacked = jnp.zeros((1, lanes), jnp.float32)
    for w in range(W):
        stacked = jnp.where(spot % W == w, jnp.where(valid[w] != 0, 1.0, 0.0), stacked)
    chans = R1 // 2

    def chosen(which):
        first = jnp.where(which == block[0], 1, 0)
        second = jnp.where(which == lax.rem(block[0] + 1, chans), 1, 0)
        taken = jnp.where(source >= offset[0], first, second)
        return jnp.where(taken == 1, stacked, 0.0)

    mine, theirs = chosen(chan), chosen(chan ^ 1)
    slot = chan // 2

    def mix(g):
        def step(index, _):
            a, b = held[0, g, index], held[1, g, index]
            value = a.astype(jnp.float32) * mine + b.astype(jnp.float32) * theirs
            mixed[g, index] = value.astype(jnp.bfloat16)
            return 0

        return step

    sums, moves = {}, {}
    for g in range(2):
        swaps[g].wait_recv()
        lax.fori_loop(0, SIDE * 2, mix(g), 0, unroll=4)
        sums[g] = []
        for r, (place, which) in enumerate(along):
            target = place[0] * 2 + place[1] // 2
            sums[g].append(pltpu.make_async_remote_copy(
                src_ref=mixed.at[g, target], dst_ref=parts.at[g, slot],
                send_sem=chan_send.at[g * 7 + r], recv_sem=chan_recv.at[g * 7 + r],
                device_id=device_at(place, which), device_id_type=MESH))
        for copy in sums[g]:
            copy.start()

    def to_bands(g):
        for copy in sums[g]:
            copy.wait_recv()
        parts[g, slot] = mixed[g, slot]
        value = parts[g, 0].astype(jnp.float32)
        for k in range(1, SIDE * 2):
            value = value + parts[g, k].astype(jnp.float32)
        share[g] = value.astype(jnp.bfloat16).reshape(2 * SIDE, 2 * BINS, lanes)
        moves[g] = []
        for r, (place, which) in enumerate(across):
            moves[g].append(pltpu.make_async_remote_copy(
                src_ref=share.at[g, place[1] % 2 * SIDE + place[2]], dst_ref=bands.at[g, band],
                send_sem=band_send.at[g * 7 + r], recv_sem=band_recv.at[g * 7 + r],
                device_id=device_at(place, which), device_id_type=MESH))
        for copy in moves[g]:
            copy.start()
        bands[g, band] = share[g, band]

    def arrange(g):
        for copy in moves[g]:
            copy.wait_recv()
        wide = (2 * BINS * W, lanes)
        same = lax.broadcasted_iota(jnp.int32, wide, 1) % W == lax.broadcasted_iota(jnp.int32, wide, 0) % W
        tall = (lanes, SRC_BLOCK)
        channel = lax.broadcasted_iota(jnp.int32, tall, 0) // W
        column = lax.broadcasted_iota(jnp.int32, tall, 1)
        value = None
        for b in range(2 * SIDE):
            goal = (channel + (b * channels + SRC_BLOCK) - offset[0]) % SRC_BLOCK
            pick = jnp.where(goal == column, 1.0, 0.0).astype(jnp.bfloat16)
            part = bands[g, b].astype(jnp.float32)
            part = jnp.broadcast_to(part[:, None, :], (2 * BINS, W, lanes)).reshape(wide)
            part = jnp.where(same, part, 0.0).astype(jnp.bfloat16)
            term = jnp.dot(part, pick, preferred_element_type=jnp.float32)
            value = term if value is None else value + term
        spectra[at[0], at[1] // 2, at[1] % 2, at[2], g * wide[0]:(g + 1) * wide[0], :] = value.astype(jnp.bfloat16)

    copies = {}

    def send(key, ref, axis, step):
        index = len(copies)
        copies[key] = pltpu.make_async_remote_copy(
            src_ref=ref, dst_ref=ref, send_sem=send_sem.at[index], recv_sem=recv_sem.at[index],
            device_id=neighbour(axis, step), device_id_type=MESH)
        copies[key].start()

    def shifted(order, line, step):
        moved = list(at)
        for axis, by in ((order[1], LINES[line]), (order[2], step)):
            moved[axis] = lax.rem(at[axis] + by + SIDE, SIDE)
        return moved

    def begin(turn, stage):
        for part, (first, count, order) in enumerate(PARTS[turn]):
            ref = slots(spectra, at, order[:stage], turn * 256 + first, count)
            for kind, step in enumerate((1, -1, 2)):
                send((turn, stage, part, kind), ref, order[stage], step)

    def finish(turn, stage):
        for part in range(3):
            for kind in range(3):
                copies[turn, stage, part, kind].wait_recv()

    def send_line(turn, line):
        for part, (first, count, order) in enumerate(PARTS[turn]):
            if line:
                copies[turn, 1, part, line - 1].wait_recv()
            ref = slots(spectra, shifted(order, line, 0), order[:1], turn * 256 + first, count)
            for kind, step in enumerate((1, -1)):
                send((turn, 2, part, kind, line), ref, order[2], step)

    def forward(turn, line):
        for part, (first, count, order) in enumerate(PARTS[turn]):
            low = (count // 32 + (count // 16) % 2 * (line % 2)) * 16
            shares = ((1, -1, 0, low), (-1, 1, low, count - low))
            for kind, (step, origin, skip, rows_sent) in enumerate(shares):
                copies[turn, 2, part, kind, line].wait_recv()
                ref = slots(spectra, shifted(order, line, origin), order[:1], turn * 256 + first + skip, rows_sent)
                send((turn, 2, part, kind + 2, line), ref, order[2], step)

    def finish_lines(turn):
        for line in range(len(LINES)):
            for part in range(3):
                for kind in (2, 3):
                    copies[turn, 2, part, kind, line].wait_recv()

    def multiply(turn, place=lambda index: index):
        def step(index, _):
            k = place(index)
            s = spectra[k // 16, k // 8 % 2, k // 4 % 2, k % 4, turn * 256:(turn + 1) * 256, :]
            right = jnp.concatenate([s, jnp.concatenate([-s[R2:], s[:R2]], axis=0)], axis=1)
            result = jnp.dot(left[turn, k], right, preferred_element_type=jnp.float32)
            base = pl.multiple_of(k * 16, 16)
            for c in range(2 * channels):
                both = result[c * BINS:(c + 1) * BINS]
                both = jnp.concatenate([both[:, :SRC_BLOCK], both[:, SRC_BLOCK:]], axis=0)
                cross[pl.ds(base, 16), c * SRC_BLOCK:(c + 1) * SRC_BLOCK] = both.astype(jnp.bfloat16)
            return 0

        return step

    def near(digit):
        return digit + digit // 2

    def shift(dx, dy, dz):
        x, y, z = [lax.rem(a + b, SIDE) for a, b in zip(at, (dx, dy, dz))]
        return x * 16 + y * 4 + z

    group = 8
    width = group * SRC_BLOCK

    def sum_lags(turn, core_index, n, store):
        both = slice(core_index * columns + n * width, core_index * columns + (n + 1) * width)
        value = jnp.dot(table[:, turn * 1024:(turn + 1) * 1024], cross[:, both], preferred_element_type=jnp.float32)
        for i in range(group):
            store(n * group + i, core_index * channels + n * group + i, value[:, i * SRC_BLOCK:(i + 1) * SRC_BLOCK])

    def keep(c, held_c, value):
        total[held_c] = value

    def hand_over(c, held_c, value):
        outgoing[c] = ((total[held_c] + value) * FACTOR).astype(jnp.bfloat16)

    def conclude(c, held_c, value):
        total[held_c] = total[held_c] + value

    pairs = SLOTS // 2
    lax.fori_loop(8, SLOTS, spread(0), 0, unroll=4)
    to_bands(0)
    lax.fori_loop(0, 16, spread(1), 0, unroll=4)
    to_bands(1)
    lax.fori_loop(16, 32, spread(1), 0, unroll=4)
    arrange(0)
    begin(0, 0)
    arrange(1)
    begin(1, 0)
    lax.fori_loop(32, 40, spread(1), 0, unroll=4)
    finish(0, 0)
    begin(0, 1)
    send_line(0, 0)
    finish(1, 0)
    begin(1, 1)
    lax.fori_loop(40, 48, spread(1), 0, unroll=4)
    for line in (1, 2, 3):
        send_line(0, line)
    forward(0, 0)
    lax.fori_loop(48, 56, spread(1), 0, unroll=4)
    forward(0, 1)
    send_line(1, 0)
    lax.fori_loop(56, SLOTS, spread(1), 0, unroll=4)
    forward(0, 2)
    forward(0, 3)
    for line in (1, 2, 3):
        send_line(1, line)
    own_table.wait()
    finish_lines(0)
    quarter = SLOTS // 4
    for line in range(4):
        lax.fori_loop(line * quarter, (line + 1) * quarter, multiply(0), 0, unroll=4)
        forward(1, line)
    for core_index in range(2):
        for n in range(channels // group):
            sum_lags(0, core_index, n, keep)
    lax.fori_loop(0, 27, multiply(1, lambda i: shift(near(i // 9), near(i // 3 % 3), near(i % 3))), 0, unroll=3)
    finish_lines(1)
    lax.fori_loop(0, 16, multiply(1, lambda i: shift(2, i // 4, i % 4)), 0, unroll=4)
    lax.fori_loop(0, 12, multiply(1, lambda i: shift(near(i // 4), 2, i % 4)), 0, unroll=4)
    lax.fori_loop(0, 9, multiply(1, lambda i: shift(near(i // 3), near(i % 3), 2)), 0, unroll=3)
    exchanges = []
    for n in range(channels // group):
        sum_lags(1, 1, n, hand_over)
        some = pl.ds(n * group, group)
        exchange = pltpu.make_async_remote_copy(
            src_ref=outgoing.at[some], dst_ref=incoming.at[some], send_sem=side_send.at[2 + n],
            recv_sem=side_recv.at[2 + n], device_id=sibling, device_id_type=MESH)
        exchange.start()
        exchanges.append(exchange)
    for n in range(channels // group):
        sum_lags(1, 0, n, conclude)

    unit = identity(SRC_BLOCK)
    last = (((1,), (1,)), ((), ()))
    for c in range(channels):
        if c % group == 0:
            exchanges[c // group].wait_recv()
        value = (total[c] * FACTOR + incoming[c].astype(jnp.float32)).astype(jnp.bfloat16)
        value = lax.dot_general(unit, value, last, preferred_element_type=jnp.float32)
        for half in range(2):
            turned[half, pl.ds(c, SRC_BLOCK, stride=channels), :] = value[:, half * R2:(half + 1) * R2]

    def pack(index):
        picked = pl.ds(pl.multiple_of(index * 256, 256), 256)
        both = jnp.concatenate([turned[0, picked, :], turned[1, picked, :]], axis=1).astype(jnp.bfloat16)
        return both.reshape(-1, channels, LAGS)

    ships = []
    for r, (place, which) in enumerate(across):
        index = place[1] % 2 * SIDE + place[2]
        shipped[index] = pack(index)
        ship = pltpu.make_async_remote_copy(
            src_ref=shipped.at[index], dst_ref=landed.at[:, band], send_sem=ship_send.at[r], recv_sem=ship_recv.at[r],
            device_id=device_at(place, which), device_id_type=MESH)
        ship.start()
        ships.append(ship)
    shipped[band] = pack(band)
    kept = pltpu.make_async_copy(shipped.at[band], landed.at[:, band], local_sem.at[0])
    kept.start()
    for ship in ships:
        ship.wait_recv()

    kept.wait()
    for copy in swaps + exchanges + sums[0] + sums[1] + moves[0] + moves[1] + ships + list(copies.values()):
        copy.wait_send()


def identity(n):
    diagonal = lax.broadcasted_iota(jnp.int32, (n, n), 0) == lax.broadcasted_iota(jnp.int32, (n, n), 1)
    return jnp.where(diagonal, 1.0, 0.0).astype(jnp.bfloat16)


def body(strain, source_block, source_offset, window_valid):
    channels = strain.shape[0]
    lanes = channels * W
    columns = channels * SRC_BLOCK
    tiles = strain.reshape(channels // BINS, BINS, -1, R2).transpose(0, 2, 1, 3).reshape(-1, R2)
    copies = ROUNDS * 3 * (3 + 3 + 4 * len(LINES))
    anywhere = pl.BlockSpec(memory_space=pl.ANY)
    scalars = pl.BlockSpec(memory_space=pltpu.SMEM)
    dma = pltpu.SemaphoreType.DMA
    bf16, f32 = jnp.bfloat16, jnp.float32
    landed = pl.pallas_call(
        kernel,
        in_specs=[anywhere] * 4 + [scalars] * 3,
        out_specs=anywhere,
        out_shape=jax.ShapeDtypeStruct((SRC_BLOCK // (2 * SIDE), 2 * SIDE, channels, LAGS), bf16),
        scratch_shapes=[
            pltpu.VMEM(tiles.shape, f32),
            pltpu.VMEM((3 * R1, R2), f32),
            pltpu.VMEM((R2, 2 * R2), bf16),
            pltpu.VMEM((LAGS, NF), bf16),
            pltpu.VMEM((3, 2, SIDE * 2, R2, lanes), bf16),
            pltpu.VMEM((2, SIDE * 2, R2, lanes), bf16),
            pltpu.VMEM((2, SIDE * 2, R2, lanes), bf16),
            pltpu.VMEM((2, SIDE * 2, 2 * BINS, lanes), bf16),
            pltpu.VMEM((2, SIDE * 2, 2 * BINS, lanes), bf16),
            pltpu.VMEM((SIDE, 2, 2, SIDE, PIECE, SRC_BLOCK), bf16),
            pltpu.VMEM((2, SLOTS, 256, 256), bf16),
            pltpu.VMEM((NF // 2, 2 * columns), bf16),
            pltpu.VMEM((2 * channels, LAGS, SRC_BLOCK), f32),
            pltpu.VMEM((channels, LAGS, SRC_BLOCK), bf16),
            pltpu.VMEM((channels, LAGS, SRC_BLOCK), bf16),
            pltpu.VMEM((2, columns, R2), f32),
            pltpu.VMEM((2 * SIDE, SRC_BLOCK // (2 * SIDE), channels, LAGS), bf16),
            dma((4,)), dma((copies,)), dma((copies,)), dma((4,)), dma((4,)),
            dma((14,)), dma((14,)), dma((14,)), dma((14,)), dma((7,)), dma((7,)),
        ],
        compiler_params=pltpu.CompilerParams(
            vmem_limit_bytes=62 * 2**20, collective_id=1, has_side_effects=True),
        cost_estimate=pl.CostEstimate(flops=4 * 256 * 4096 * 2048, bytes_accessed=20 * 2**20, transcendentals=0),
    )(tiles, jnp.asarray(row_tables()), jnp.asarray(short_dft(), dtype=bf16),
      jnp.asarray(lag_table(), dtype=bf16), source_block, source_offset, window_valid)
    rows = landed.reshape(-1, 2 * SIDE * channels, LAGS)
    return jnp.einsum("tu,scu->stc", jnp.eye(LAGS, dtype=bf16), rows, preferred_element_type=f32).astype(bf16)


def solution(mesh):
    in_specs = (P(("chan", "band"), None), P(), P(), P())
    out_specs = P("band", None, "chan")
    return jax.shard_map(body, mesh=mesh, in_specs=in_specs, out_specs=out_specs, check_vma=False)
```

```python
import functools
import math

import jax
import jax.numpy as jnp
import numpy as np
from jax import lax
from jax.experimental import pallas as pl
from jax.experimental.pallas import tpu as pltpu
from jax.sharding import PartitionSpec as P

L = 4096
HOP = 2048
NF = 2048
W = 16
SRC_BLOCK = 128
LAGS = 256
R1 = 32
R2 = 128
HALF = R2 // 2
BINS = 8
FACTOR = 1.0 / (W * math.sqrt(NF))


def window_table():
    points = np.arange(L, dtype=np.float32)
    angle = (points * np.float32(2.0 * math.pi / L)).astype(np.float32)
    return (np.float32(0.5) - np.float32(0.5) * np.cos(angle)).astype(np.float32).reshape(R1, R2)


def row_tables():
    angle = 2.0 * np.pi * np.outer(np.arange(R1), np.arange(R2)) / L
    return np.concatenate([window_table(), np.cos(angle), -np.sin(angle)], axis=0).astype(np.float32)


def short_dft():
    angle = 2.0 * np.pi * (np.outer(np.arange(HALF), np.arange(R2)) % R2) / R2
    cosine, sine = np.cos(angle), np.sin(angle)
    top = np.concatenate([cosine, sine], axis=1)
    low = np.concatenate([-sine, cosine], axis=1)
    both = np.stack([top.reshape(-1, BINS, 2 * R2), low.reshape(-1, BINS, 2 * R2)], axis=1)
    return both.reshape(R2, 2 * R2).astype(np.float32)


def lag_table():
    core, g, x, y_hi, y_lo, z, i = np.ix_(*[np.arange(n) for n in (2, 2, 4, 2, 2, 4, 8)])
    bins = 8 * x + 4 * y_hi + 2 * core + g + R1 * (32 * y_lo + 8 * z + i)
    lags = (np.arange(LAGS) - LAGS // 2).reshape((1, LAGS) + (1,) * 6)
    angle = 2.0 * np.pi * (lags * bins[:, None] % L) / L
    table = np.stack([np.cos(angle), -np.sin(angle)], axis=7)
    return table.reshape(2, LAGS, NF).astype(np.float32)


def real_dft(x):
    n = len(x)
    if n == 2:
        return [(x[0] + x[1], None), (x[0] - x[1], None)]
    even, odd = real_dft(x[0::2]), real_dft(x[1::2])
    out = [None] * (n // 2 + 1)
    for k in range(n // 4 + 1):
        er, ei = even[k]
        orr, oi = odd[k]
        if k == 0:
            out[0] = (er + orr, None)
            out[n // 2] = (er - orr, None)
            continue
        if 4 * k == n:
            out[k] = (er, -orr)
            continue
        c, s = math.cos(2 * math.pi * k / n), -math.sin(2 * math.pi * k / n)
        if oi is None:
            tr, ti = orr * c, orr * s
        else:
            tr, ti = orr * c - oi * s, orr * s + oi * c
        zi = ti if ei is None else ei + ti
        yi = -ti if ei is None else ei - ti
        out[k] = (er + tr, zi)
        out[n // 2 - k] = (er - tr, -yi)
    return out


SIDE = 4
SLOTS = SIDE ** 3
PIECE = 2 * 2 * BINS * W
PARTS = (((0, 96, (0, 1, 2)), (96, 80, (1, 2, 0)), (176, 80, (2, 0, 1))),
         ((0, 80, (0, 1, 2)), (80, 96, (1, 2, 0)), (176, 80, (2, 0, 1))))
LINES = (0, -1, 1, 2)
ROUNDS = 2
MESH = pl.DeviceIdType.MESH


def position():
    chan, band = lax.axis_index("chan"), lax.axis_index("band")
    return (chan // 4, chan // 2 % 2 * 2 + band // 4, band % 4), chan % 2


def device_at(at, core):
    x, y, z = at
    return (x * 4 + y // 2 * 2 + core, y % 2 * 4 + z)


def neighbour(axis, step):
    at, core = position()
    moved = list(at)
    moved[axis] = lax.rem(at[axis] + step + SIDE, SIDE)
    return device_at(moved, core)


def slots(ref, at, full, first, count):
    whole = slice(None)
    x = whole if 0 in full else at[0]
    y_hi, y_lo = (whole, whole) if 1 in full else (at[1] // 2, at[1] % 2)
    z = whole if 2 in full else at[2]
    return ref.at[x, y_hi, y_lo, z, pl.ds(first, count), :]


def partners(at, core):
    x, y, z = at
    side = lambda step: lax.rem(z + step, SIDE)
    along = [((lax.rem(x + dx, SIDE), y ^ (2 * dy), z), core) for dx in (2, 1, 3, 0) for dy in (1, 0)][:-1]
    across = [((x, y ^ dy, side(dz)), core) for dz in (2, 1, 3, 0) for dy in (1, 0)][:-1]
    return along, across, [((x, y ^ 3, z), core), (at, 1 - core)]


def kernel(strain_hbm, rows_hbm, dft_hbm, tables, block, offset, valid, landed,
           strain, rows, dft, table, held, mixed, parts, share, bands, spectra, left, cross, total,
           outgoing, incoming, turned, shipped, picks,
           local_sem, send_sem, recv_sem, side_send, side_recv, chan_send, chan_recv, band_send, band_recv,
           ship_send, ship_recv):
    at, core = position()
    chan, band = lax.axis_index("chan"), lax.axis_index("band")
    sibling = device_at(at, 1 - core)
    lanes = held.shape[-1]
    channels = lanes // W
    columns = channels * SRC_BLOCK
    along, across, rest = partners(at, core)

    def fetch(src, dst, index):
        copy = pltpu.make_async_copy(src, dst, local_sem.at[index])
        copy.start()
        return copy

    fetched = [fetch(strain_hbm, strain, 0), fetch(rows_hbm, rows, 1), fetch(dft_hbm, dft, 2)]
    own_table = fetch(tables.at[core], table, 3)
    barrier = pltpu.get_barrier_semaphore()
    for place, which in along + across + rest:
        pl.semaphore_signal(barrier, inc=1, device_id=device_at(place, which), device_id_type=MESH)
    for copy in fetched:
        copy.wait()

    folded = left.at[0]

    def fold(c, _):
        first = c // BINS * (BINS * (W + 1) * W) + c % BINS
        x = [strain[pl.ds(first + BINS * k, W, stride=BINS * W), :] for k in range(R1)]
        whole = x[0]
        for k in range(1, R1):
            whole = whole + x[k]
        mean = jnp.sum(whole, axis=1, keepdims=True) * (1.0 / L)
        x = [((x[k] - mean) * rows[k:k + 1, :]).astype(jnp.bfloat16).astype(jnp.float32) for k in range(R1)]
        bins = real_dft(x)
        to = pl.ds(pl.multiple_of(c * W, W), W)
        for f in range(R1):
            re, im = bins[f] if f <= R1 // 2 else bins[R1 - f]
            cosine, sine = rows[R1 + f:R1 + f + 1, :], rows[2 * R1 + f:2 * R1 + f + 1, :]
            if im is None:
                gr, gi = re * cosine, re * sine
            else:
                im = im if f <= R1 // 2 else -im
                gr, gi = re * cosine - im * sine, re * sine + im * cosine
            folded[f, to, :R2] = gr.astype(jnp.bfloat16)
            folded[f, to, R2:] = gi.astype(jnp.bfloat16)
        return 0

    lax.fori_loop(0, channels, fold, 0, unroll=2)
    dft_table = dft[...]

    def transform(f, power):
        y = lax.dot_general(dft_table, folded[f], (((1,), (1,)), ((), ())), preferred_element_type=jnp.float32)
        total[f, :R2, :] = y[:, :R2]
        total[f, R2:, :] = y[:, R2:]
        square = (y * y).reshape(HALF // BINS, 2, BINS, lanes)
        return power + (square[:, 0] + square[:, 1]).reshape(HALF, lanes)

    power = lax.fori_loop(0, R1, transform, jnp.zeros((HALF, lanes), jnp.float32), unroll=8)
    scales = []
    for b in range(HALF // BINS):
        mean = jnp.sum(power[b * BINS:(b + 1) * BINS], axis=0, keepdims=True) * (1.0 / 256.0)
        scales.append(jnp.broadcast_to(lax.rsqrt(mean + 1e-06), (2 * BINS, lanes)))
    scale = jnp.concatenate(scales, axis=0)

    def finish_white(to, which, g):
        def step(index, _):
            f = index * 4 + which * 2 + g
            y = jnp.concatenate([total[f, :R2, :], total[f, R2:, :]], axis=1)
            held[to, g, index] = (y * scale).astype(jnp.bfloat16)
            return 0

        lax.fori_loop(0, SIDE * 2, step, 0, unroll=4)

    for g in range(2):
        finish_white(2, 1 - core, g)
    pl.semaphore_wait(barrier, len(along) + len(across) + len(rest))
    swaps = []
    for g in range(2):
        swap = pltpu.make_async_remote_copy(
            src_ref=held.at[2, g], dst_ref=held.at[1, g], send_sem=side_send.at[g], recv_sem=side_recv.at[g],
            device_id=sibling, device_id_type=MESH)
        swap.start()
        swaps.append(swap)
    for g in range(2):
        finish_white(0, core, g)

    row = lax.broadcasted_iota(jnp.int32, (2 * BINS, R2), 0) % BINS
    lane = lax.broadcasted_iota(jnp.int32, (2 * BINS, R2), 1)
    own = lane // W == row

    def spread(core_index):
        def step(index, _):
            x, y_hi, y_lo, z = index // 16, index // 8 % 2, index // 4 % 2, index % 4
            picked = pl.ds(pl.multiple_of((y_lo * SIDE + z) * 16, 16), 16)
            for g in range(2):
                for k in range(channels // 8):
                    value = held[core_index, g, x * 2 + y_hi, picked, k * R2:(k + 1) * R2].astype(jnp.float32)
                    for ri in range(2):
                        even = pltpu.roll(value[ri * BINS:(ri + 1) * BINS], 0, 1, stride=W, stride_axis=0)
                        both = jnp.concatenate([even, pltpu.roll(even, R2 - W, 1)], axis=0).astype(jnp.bfloat16)
                        for t in range(4):
                            moved = pltpu.roll(both, R2 - 2 * W * t, 1) if t else both
                            first = ((core_index * channels // 8 + k) * 4 + t) * 2 * BINS
                            left[g, index, first:first + 2 * BINS, ri * R2:(ri + 1) * R2] = jnp.where(
                                own, moved, jnp.zeros_like(moved))
            return 0

        return step

    lax.fori_loop(0, 8, spread(0), 0, unroll=4)

    spot = lax.broadcasted_iota(jnp.int32, (1, lanes), 1)
    source = band * channels + spot // W
    stacked = jnp.zeros((1, lanes), jnp.float32)
    for w in range(W):
        stacked = jnp.where(spot % W == w, jnp.where(valid[w] != 0, 1.0, 0.0), stacked)
    chans = R1 // 2

    def chosen(which):
        first = jnp.where(which == block[0], 1, 0)
        second = jnp.where(which == lax.rem(block[0] + 1, chans), 1, 0)
        taken = jnp.where(source >= offset[0], first, second)
        return jnp.where(taken == 1, stacked, 0.0)

    mine, theirs = chosen(chan), chosen(chan ^ 1)
    slot = chan // 2

    def mix(g):
        def step(index, _):
            a, b = held[0, g, index], held[1, g, index]
            value = a.astype(jnp.float32) * mine + b.astype(jnp.float32) * theirs
            mixed[g, index] = value.astype(jnp.bfloat16)
            return 0

        return step

    sums, moves = {}, {}
    for g in range(2):
        swaps[g].wait_recv()
        lax.fori_loop(0, SIDE * 2, mix(g), 0, unroll=4)
        sums[g] = []
        for r, (place, which) in enumerate(along):
            target = place[0] * 2 + place[1] // 2
            sums[g].append(pltpu.make_async_remote_copy(
                src_ref=mixed.at[g, target], dst_ref=parts.at[g, slot],
                send_sem=chan_send.at[g * 7 + r], recv_sem=chan_recv.at[g * 7 + r],
                device_id=device_at(place, which), device_id_type=MESH))
        for copy in sums[g]:
            copy.start()

    def to_bands(g):
        for copy in sums[g]:
            copy.wait_recv()
        parts[g, slot] = mixed[g, slot]
        value = parts[g, 0].astype(jnp.float32)
        for k in range(1, SIDE * 2):
            value = value + parts[g, k].astype(jnp.float32)
        share[g] = value.astype(jnp.bfloat16).reshape(2 * SIDE, 2 * BINS, lanes)
        moves[g] = []
        for r, (place, which) in enumerate(across):
            moves[g].append(pltpu.make_async_remote_copy(
                src_ref=share.at[g, place[1] % 2 * SIDE + place[2]], dst_ref=bands.at[g, band],
                send_sem=band_send.at[g * 7 + r], recv_sem=band_recv.at[g * 7 + r],
                device_id=device_at(place, which), device_id_type=MESH))
        for copy in moves[g]:
            copy.start()
        bands[g, band] = share[g, band]

    def select():
        tall = (2 * SIDE * lanes, SRC_BLOCK)
        source = lax.broadcasted_iota(jnp.int32, tall, 0) // W
        goal = (source + SRC_BLOCK - offset[0]) % SRC_BLOCK
        picks[...] = jnp.where(goal == lax.broadcasted_iota(jnp.int32, tall, 1), 1.0, 0.0).astype(jnp.bfloat16)

    def arrange(g):
        for copy in moves[g]:
            copy.wait_recv()
        wide = (2 * BINS * W, lanes)
        same = lax.broadcasted_iota(jnp.int32, wide, 1) % W == lax.broadcasted_iota(jnp.int32, wide, 0) % W
        spaced = []
        for b in range(2 * SIDE):
            part = bands[g, b].astype(jnp.float32)
            part = jnp.broadcast_to(part[:, None, :], (2 * BINS, W, lanes)).reshape(wide)
            spaced.append(jnp.where(same, part, 0.0).astype(jnp.bfloat16))
        value = jnp.dot(jnp.concatenate(spaced, axis=1), picks[...], preferred_element_type=jnp.float32)
        spectra[at[0], at[1] // 2, at[1] % 2, at[2], g * wide[0]:(g + 1) * wide[0], :] = value.astype(jnp.bfloat16)

    copies = {}

    def send(key, ref, axis, step):
        index = len(copies)
        copies[key] = pltpu.make_async_remote_copy(
            src_ref=ref, dst_ref=ref, send_sem=send_sem.at[index], recv_sem=recv_sem.at[index],
            device_id=neighbour(axis, step), device_id_type=MESH)
        copies[key].start()

    def shifted(order, line, step):
        moved = list(at)
        for axis, by in ((order[1], LINES[line]), (order[2], step)):
            moved[axis] = lax.rem(at[axis] + by + SIDE, SIDE)
        return moved

    def begin(turn, stage):
        for part, (first, count, order) in enumerate(PARTS[turn]):
            ref = slots(spectra, at, order[:stage], turn * 256 + first, count)
            for kind, step in enumerate((1, -1, 2)):
                send((turn, stage, part, kind), ref, order[stage], step)

    def finish(turn, stage):
        for part in range(3):
            for kind in range(3):
                copies[turn, stage, part, kind].wait_recv()

    def send_line(turn, line):
        for part, (first, count, order) in enumerate(PARTS[turn]):
            if line:
                copies[turn, 1, part, line - 1].wait_recv()
            ref = slots(spectra, shifted(order, line, 0), order[:1], turn * 256 + first, count)
            for kind, step in enumerate((1, -1)):
                send((turn, 2, part, kind, line), ref, order[2], step)

    def forward(turn, line):
        for part, (first, count, order) in enumerate(PARTS[turn]):
            low = (count // 32 + (count // 16) % 2 * (line % 2)) * 16
            shares = ((1, -1, 0, low), (-1, 1, low, count - low))
            for kind, (step, origin, skip, rows_sent) in enumerate(shares):
                copies[turn, 2, part, kind, line].wait_recv()
                ref = slots(spectra, shifted(order, line, origin), order[:1], turn * 256 + first + skip, rows_sent)
                send((turn, 2, part, kind + 2, line), ref, order[2], step)

    def finish_lines(turn):
        for line in range(len(LINES)):
            for part in range(3):
                for kind in (2, 3):
                    copies[turn, 2, part, kind, line].wait_recv()

    def multiply(turn, place=lambda index: index):
        def step(index, _):
            k = place(index)
            s = spectra[k // 16, k // 8 % 2, k // 4 % 2, k % 4, turn * 256:(turn + 1) * 256, :]
            right = jnp.concatenate([s, jnp.concatenate([-s[R2:], s[:R2]], axis=0)], axis=1)
            result = jnp.dot(left[turn, k], right, preferred_element_type=jnp.float32)
            base = pl.multiple_of(k * 16, 16)
            for c in range(2 * channels):
                both = result[c * BINS:(c + 1) * BINS]
                both = jnp.concatenate([both[:, :SRC_BLOCK], both[:, SRC_BLOCK:]], axis=0)
                cross[pl.ds(base, 16), c * SRC_BLOCK:(c + 1) * SRC_BLOCK] = both.astype(jnp.bfloat16)
            return 0

        return step

    def near(digit):
        return digit + digit // 2

    def shift(dx, dy, dz):
        x, y, z = [lax.rem(a + b, SIDE) for a, b in zip(at, (dx, dy, dz))]
        return x * 16 + y * 4 + z

    group = 8
    width = group * SRC_BLOCK

    def sum_lags(turn, core_index, n, store):
        both = slice(core_index * columns + n * width, core_index * columns + (n + 1) * width)
        value = jnp.dot(table[:, turn * 1024:(turn + 1) * 1024], cross[:, both], preferred_element_type=jnp.float32)
        for i in range(group):
            store(n * group + i, core_index * channels + n * group + i, value[:, i * SRC_BLOCK:(i + 1) * SRC_BLOCK])

    def keep(c, held_c, value):
        total[held_c] = value

    def hand_over(c, held_c, value):
        outgoing[c] = ((total[held_c] + value) * FACTOR).astype(jnp.bfloat16)

    def conclude(c, held_c, value):
        total[held_c] = total[held_c] + value

    pairs = SLOTS // 2
    lax.fori_loop(8, SLOTS, spread(0), 0, unroll=4)
    select()
    lax.fori_loop(0, 40, spread(1), 0, unroll=4)
    to_bands(0)
    lax.fori_loop(40, 52, spread(1), 0, unroll=4)
    to_bands(1)
    lax.fori_loop(52, 60, spread(1), 0, unroll=4)
    arrange(0)
    begin(0, 0)
    arrange(1)
    begin(1, 0)
    lax.fori_loop(60, SLOTS, spread(1), 0, unroll=4)
    finish(0, 0)
    begin(0, 1)
    send_line(0, 0)
    finish(1, 0)
    begin(1, 1)
    for line in (1, 2, 3):
        send_line(0, line)
    forward(0, 0)
    forward(0, 1)
    send_line(1, 0)
    forward(0, 2)
    forward(0, 3)
    for line in (1, 2, 3):
        send_line(1, line)
    own_table.wait()
    finish_lines(0)
    quarter = SLOTS // 4
    for line in range(4):
        lax.fori_loop(line * quarter, (line + 1) * quarter, multiply(0), 0, unroll=4)
        forward(1, line)
    for core_index in range(2):
        for n in range(channels // group):
            sum_lags(0, core_index, n, keep)
    lax.fori_loop(0, 27, multiply(1, lambda i: shift(near(i // 9), near(i // 3 % 3), near(i % 3))), 0, unroll=3)
    finish_lines(1)
    lax.fori_loop(0, 16, multiply(1, lambda i: shift(2, i // 4, i % 4)), 0, unroll=4)
    lax.fori_loop(0, 12, multiply(1, lambda i: shift(near(i // 4), 2, i % 4)), 0, unroll=4)
    lax.fori_loop(0, 9, multiply(1, lambda i: shift(near(i // 3), near(i % 3), 2)), 0, unroll=3)
    exchanges = []
    for n in range(channels // group):
        sum_lags(1, 1, n, hand_over)
        some = pl.ds(n * group, group)
        exchange = pltpu.make_async_remote_copy(
            src_ref=outgoing.at[some], dst_ref=incoming.at[some], send_sem=side_send.at[2 + n],
            recv_sem=side_recv.at[2 + n], device_id=sibling, device_id_type=MESH)
        exchange.start()
        exchanges.append(exchange)
    for n in range(channels // group):
        sum_lags(1, 0, n, conclude)

    unit = identity(SRC_BLOCK)
    last = (((1,), (1,)), ((), ()))
    for c in range(channels):
        if c % group == 0:
            exchanges[c // group].wait_recv()
        value = (total[c] * FACTOR + incoming[c].astype(jnp.float32)).astype(jnp.bfloat16)
        value = lax.dot_general(unit, value, last, preferred_element_type=jnp.float32)
        for half in range(2):
            turned[half, pl.ds(c, SRC_BLOCK, stride=channels), :] = value[:, half * R2:(half + 1) * R2]

    def pack(index):
        picked = pl.ds(pl.multiple_of(index * 256, 256), 256)
        both = jnp.concatenate([turned[0, picked, :], turned[1, picked, :]], axis=1).astype(jnp.bfloat16)
        return both.reshape(-1, channels, LAGS)

    ships = []
    for r, (place, which) in enumerate(across):
        index = place[1] % 2 * SIDE + place[2]
        shipped[index] = pack(index)
        ship = pltpu.make_async_remote_copy(
            src_ref=shipped.at[index], dst_ref=landed.at[:, band], send_sem=ship_send.at[r], recv_sem=ship_recv.at[r],
            device_id=device_at(place, which), device_id_type=MESH)
        ship.start()
        ships.append(ship)
    shipped[band] = pack(band)
    kept = pltpu.make_async_copy(shipped.at[band], landed.at[:, band], local_sem.at[0])
    kept.start()
    for ship in ships:
        ship.wait_recv()

    kept.wait()
    for copy in swaps + exchanges + sums[0] + sums[1] + moves[0] + moves[1] + ships + list(copies.values()):
        copy.wait_send()


def identity(n):
    diagonal = lax.broadcasted_iota(jnp.int32, (n, n), 0) == lax.broadcasted_iota(jnp.int32, (n, n), 1)
    return jnp.where(diagonal, 1.0, 0.0).astype(jnp.bfloat16)


def body(strain, source_block, source_offset, window_valid):
    channels = strain.shape[0]
    lanes = channels * W
    columns = channels * SRC_BLOCK
    tiles = strain.reshape(channels // BINS, BINS, -1, R2).transpose(0, 2, 1, 3).reshape(-1, R2)
    copies = ROUNDS * 3 * (3 + 3 + 4 * len(LINES))
    anywhere = pl.BlockSpec(memory_space=pl.ANY)
    scalars = pl.BlockSpec(memory_space=pltpu.SMEM)
    dma = pltpu.SemaphoreType.DMA
    bf16, f32 = jnp.bfloat16, jnp.float32
    landed = pl.pallas_call(
        kernel,
        in_specs=[anywhere] * 4 + [scalars] * 3,
        out_specs=anywhere,
        out_shape=jax.ShapeDtypeStruct((SRC_BLOCK // (2 * SIDE), 2 * SIDE, channels, LAGS), bf16),
        scratch_shapes=[
            pltpu.VMEM(tiles.shape, f32),
            pltpu.VMEM((3 * R1, R2), f32),
            pltpu.VMEM((R2, 2 * R2), bf16),
            pltpu.VMEM((LAGS, NF), bf16),
            pltpu.VMEM((3, 2, SIDE * 2, R2, lanes), bf16),
            pltpu.VMEM((2, SIDE * 2, R2, lanes), bf16),
            pltpu.VMEM((2, SIDE * 2, R2, lanes), bf16),
            pltpu.VMEM((2, SIDE * 2, 2 * BINS, lanes), bf16),
            pltpu.VMEM((2, SIDE * 2, 2 * BINS, lanes), bf16),
            pltpu.VMEM((SIDE, 2, 2, SIDE, PIECE, SRC_BLOCK), bf16),
            pltpu.VMEM((2, SLOTS, 256, 256), bf16),
            pltpu.VMEM((NF // 2, 2 * columns), bf16),
            pltpu.VMEM((2 * channels, LAGS, SRC_BLOCK), f32),
            pltpu.VMEM((channels, LAGS, SRC_BLOCK), bf16),
            pltpu.VMEM((channels, LAGS, SRC_BLOCK), bf16),
            pltpu.VMEM((2, columns, R2), f32),
            pltpu.VMEM((2 * SIDE, SRC_BLOCK // (2 * SIDE), channels, LAGS), bf16),
            pltpu.VMEM((2 * SIDE * lanes, SRC_BLOCK), bf16),
            dma((4,)), dma((copies,)), dma((copies,)), dma((4,)), dma((4,)),
            dma((14,)), dma((14,)), dma((14,)), dma((14,)), dma((7,)), dma((7,)),
        ],
        compiler_params=pltpu.CompilerParams(
            vmem_limit_bytes=62 * 2**20, collective_id=1, has_side_effects=True),
        cost_estimate=pl.CostEstimate(flops=4 * 256 * 4096 * 2048, bytes_accessed=20 * 2**20, transcendentals=0),
    )(tiles, jnp.asarray(row_tables()), jnp.asarray(short_dft(), dtype=bf16),
      jnp.asarray(lag_table(), dtype=bf16), source_block, source_offset, window_valid)
    rows = landed.reshape(-1, 2 * SIDE * channels, LAGS)
    return jnp.einsum("tu,scu->stc", jnp.eye(LAGS, dtype=bf16), rows, preferred_element_type=f32).astype(bf16)


def solution(mesh):
    in_specs = (P(("chan", "band"), None), P(), P(), P())
    out_specs = P("band", None, "chan")
    return jax.shard_map(body, mesh=mesh, in_specs=in_specs, out_specs=out_specs, check_vma=False)
```

```python
import functools
import math

import jax
import jax.numpy as jnp
import numpy as np
from jax import lax
from jax.experimental import pallas as pl
from jax.experimental.pallas import tpu as pltpu
from jax.sharding import PartitionSpec as P

L = 4096
HOP = 2048
NF = 2048
W = 16
SRC_BLOCK = 128
LAGS = 256
R1 = 32
R2 = 128
HALF = R2 // 2
BINS = 8
FACTOR = 1.0 / (W * math.sqrt(NF))


def window_table():
    points = np.arange(L, dtype=np.float32)
    angle = (points * np.float32(2.0 * math.pi / L)).astype(np.float32)
    return (np.float32(0.5) - np.float32(0.5) * np.cos(angle)).astype(np.float32).reshape(R1, R2)


def row_tables():
    angle = 2.0 * np.pi * np.outer(np.arange(R1), np.arange(R2)) / L
    return np.concatenate([window_table(), np.cos(angle), -np.sin(angle)], axis=0).astype(np.float32)


def short_dft():
    angle = 2.0 * np.pi * (np.outer(np.arange(HALF), np.arange(R2)) % R2) / R2
    cosine, sine = np.cos(angle), np.sin(angle)
    top = np.concatenate([cosine, sine], axis=1)
    low = np.concatenate([-sine, cosine], axis=1)
    both = np.stack([top.reshape(-1, BINS, 2 * R2), low.reshape(-1, BINS, 2 * R2)], axis=1)
    return both.reshape(R2, 2 * R2).astype(np.float32)


def lag_table():
    core, g, x, y_hi, y_lo, z, i = np.ix_(*[np.arange(n) for n in (2, 2, 4, 2, 2, 4, 8)])
    bins = 8 * x + 4 * y_hi + 2 * core + g + R1 * (32 * y_lo + 8 * z + i)
    lags = (np.arange(LAGS) - LAGS // 2).reshape((1, LAGS) + (1,) * 6)
    angle = 2.0 * np.pi * (lags * bins[:, None] % L) / L
    table = np.stack([np.cos(angle), -np.sin(angle)], axis=7)
    return table.reshape(2, LAGS, NF).astype(np.float32)


def real_dft(x):
    n = len(x)
    if n == 2:
        return [(x[0] + x[1], None), (x[0] - x[1], None)]
    even, odd = real_dft(x[0::2]), real_dft(x[1::2])
    out = [None] * (n // 2 + 1)
    for k in range(n // 4 + 1):
        er, ei = even[k]
        orr, oi = odd[k]
        if k == 0:
            out[0] = (er + orr, None)
            out[n // 2] = (er - orr, None)
            continue
        if 4 * k == n:
            out[k] = (er, -orr)
            continue
        c, s = math.cos(2 * math.pi * k / n), -math.sin(2 * math.pi * k / n)
        if oi is None:
            tr, ti = orr * c, orr * s
        else:
            tr, ti = orr * c - oi * s, orr * s + oi * c
        zi = ti if ei is None else ei + ti
        yi = -ti if ei is None else ei - ti
        out[k] = (er + tr, zi)
        out[n // 2 - k] = (er - tr, -yi)
    return out


SIDE = 4
SLOTS = SIDE ** 3
PIECE = 2 * 2 * BINS * W
PARTS = (((0, 96, (0, 1, 2)), (96, 80, (1, 2, 0)), (176, 80, (2, 0, 1))),
         ((0, 80, (0, 1, 2)), (80, 96, (1, 2, 0)), (176, 80, (2, 0, 1))))
LINES = (0, -1, 1, 2)
ROUNDS = 2
MESH = pl.DeviceIdType.MESH


def position():
    chan, band = lax.axis_index("chan"), lax.axis_index("band")
    return (chan // 4, chan // 2 % 2 * 2 + band // 4, band % 4), chan % 2


def device_at(at, core):
    x, y, z = at
    return (x * 4 + y // 2 * 2 + core, y % 2 * 4 + z)


def neighbour(axis, step):
    at, core = position()
    moved = list(at)
    moved[axis] = lax.rem(at[axis] + step + SIDE, SIDE)
    return device_at(moved, core)


def slots(ref, at, full, first, count):
    whole = slice(None)
    x = whole if 0 in full else at[0]
    y_hi, y_lo = (whole, whole) if 1 in full else (at[1] // 2, at[1] % 2)
    z = whole if 2 in full else at[2]
    return ref.at[x, y_hi, y_lo, z, pl.ds(first, count), :]


def partners(at, core):
    x, y, z = at
    side = lambda step: lax.rem(z + step, SIDE)
    along = [((lax.rem(x + dx, SIDE), y ^ (2 * dy), z), core) for dx in (2, 1, 3, 0) for dy in (1, 0)][:-1]
    across = [((x, y ^ dy, side(dz)), core) for dz in (2, 1, 3, 0) for dy in (1, 0)][:-1]
    return along, across, [((x, y ^ 3, z), core), (at, 1 - core)]


def kernel(strain_hbm, rows_hbm, dft_hbm, tables, block, offset, valid, landed,
           strain, rows, dft, table, held, mixed, parts, share, bands, spectra, left, cross, total,
           outgoing, incoming, turned, shipped, picks,
           local_sem, send_sem, recv_sem, side_send, side_recv, chan_send, chan_recv, band_send, band_recv,
           ship_send, ship_recv):
    at, core = position()
    chan, band = lax.axis_index("chan"), lax.axis_index("band")
    sibling = device_at(at, 1 - core)
    lanes = held.shape[-1]
    channels = lanes // W
    columns = channels * SRC_BLOCK
    along, across, rest = partners(at, core)

    def fetch(src, dst, index):
        copy = pltpu.make_async_copy(src, dst, local_sem.at[index])
        copy.start()
        return copy

    fetched = [fetch(strain_hbm, strain, 0), fetch(rows_hbm, rows, 1), fetch(dft_hbm, dft, 2)]
    own_table = fetch(tables.at[core], table, 3)
    barrier = pltpu.get_barrier_semaphore()
    for place, which in along + across + rest:
        pl.semaphore_signal(barrier, inc=1, device_id=device_at(place, which), device_id_type=MESH)
    for copy in fetched:
        copy.wait()

    folded = left.at[0]

    def fold(c, _):
        first = c // BINS * (BINS * (W + 1) * W) + c % BINS
        x = [strain[pl.ds(first + BINS * k, W, stride=BINS * W), :] for k in range(R1)]
        whole = x[0]
        for k in range(1, R1):
            whole = whole + x[k]
        mean = jnp.sum(whole, axis=1, keepdims=True) * (1.0 / L)
        x = [((x[k] - mean) * rows[k:k + 1, :]).astype(jnp.bfloat16).astype(jnp.float32) for k in range(R1)]
        bins = real_dft(x)
        to = pl.ds(pl.multiple_of(c * W, W), W)
        for f in range(R1):
            re, im = bins[f] if f <= R1 // 2 else bins[R1 - f]
            cosine, sine = rows[R1 + f:R1 + f + 1, :], rows[2 * R1 + f:2 * R1 + f + 1, :]
            if im is None:
                gr, gi = re * cosine, re * sine
            else:
                im = im if f <= R1 // 2 else -im
                gr, gi = re * cosine - im * sine, re * sine + im * cosine
            folded[f, to, :R2] = gr.astype(jnp.bfloat16)
            folded[f, to, R2:] = gi.astype(jnp.bfloat16)
        return 0

    lax.fori_loop(0, channels, fold, 0, unroll=2)
    dft_table = dft[...]

    def transform(f, power):
        y = lax.dot_general(dft_table, folded[f], (((1,), (1,)), ((), ())), preferred_element_type=jnp.float32)
        total[f, :R2, :] = y[:, :R2]
        total[f, R2:, :] = y[:, R2:]
        square = (y * y).reshape(HALF // BINS, 2, BINS, lanes)
        return power + (square[:, 0] + square[:, 1]).reshape(HALF, lanes)

    power = lax.fori_loop(0, R1, transform, jnp.zeros((HALF, lanes), jnp.float32), unroll=8)
    scales = []
    for b in range(HALF // BINS):
        mean = jnp.sum(power[b * BINS:(b + 1) * BINS], axis=0, keepdims=True) * (1.0 / 256.0)
        scales.append(jnp.broadcast_to(lax.rsqrt(mean + 1e-06), (2 * BINS, lanes)))
    scale = jnp.concatenate(scales, axis=0)

    def finish_white(to, which, g):
        def step(index, _):
            f = index * 4 + which * 2 + g
            y = jnp.concatenate([total[f, :R2, :], total[f, R2:, :]], axis=1)
            held[to, g, index] = (y * scale).astype(jnp.bfloat16)
            return 0

        lax.fori_loop(0, SIDE * 2, step, 0, unroll=4)

    for g in range(2):
        finish_white(2, 1 - core, g)
    pl.semaphore_wait(barrier, len(along) + len(across) + len(rest))
    swaps = []
    for g in range(2):
        swap = pltpu.make_async_remote_copy(
            src_ref=held.at[2, g], dst_ref=held.at[1, g], send_sem=side_send.at[g], recv_sem=side_recv.at[g],
            device_id=sibling, device_id_type=MESH)
        swap.start()
        swaps.append(swap)
    for g in range(2):
        finish_white(0, core, g)

    row = lax.broadcasted_iota(jnp.int32, (2 * BINS, R2), 0) % BINS
    lane = lax.broadcasted_iota(jnp.int32, (2 * BINS, R2), 1)
    own = lane // W == row

    def spread(core_index):
        def step(index, _):
            x, y_hi, y_lo, z = index // 16, index // 8 % 2, index // 4 % 2, index % 4
            picked = pl.ds(pl.multiple_of((y_lo * SIDE + z) * 16, 16), 16)
            for g in range(2):
                for k in range(channels // 8):
                    value = held[core_index, g, x * 2 + y_hi, picked, k * R2:(k + 1) * R2].astype(jnp.float32)
                    for ri in range(2):
                        even = pltpu.roll(value[ri * BINS:(ri + 1) * BINS], 0, 1, stride=W, stride_axis=0)
                        both = jnp.concatenate([even, pltpu.roll(even, R2 - W, 1)], axis=0).astype(jnp.bfloat16)
                        for t in range(4):
                            moved = pltpu.roll(both, R2 - 2 * W * t, 1) if t else both
                            first = ((core_index * channels // 8 + k) * 4 + t) * 2 * BINS
                            left[g, index, first:first + 2 * BINS, ri * R2:(ri + 1) * R2] = jnp.where(
                                own, moved, jnp.zeros_like(moved))
            return 0

        return step

    lax.fori_loop(0, 8, spread(0), 0, unroll=4)

    spot = lax.broadcasted_iota(jnp.int32, (1, lanes), 1)
    source = band * channels + spot // W
    stacked = jnp.zeros((1, lanes), jnp.float32)
    for w in range(W):
        stacked = jnp.where(spot % W == w, jnp.where(valid[w] != 0, 1.0, 0.0), stacked)
    chans = R1 // 2

    def chosen(which):
        first = jnp.where(which == block[0], 1, 0)
        second = jnp.where(which == lax.rem(block[0] + 1, chans), 1, 0)
        taken = jnp.where(source >= offset[0], first, second)
        return jnp.where(taken == 1, stacked, 0.0)

    mine, theirs = chosen(chan), chosen(chan ^ 1)
    slot = chan // 2

    def mix(g):
        def step(index, _):
            a, b = held[0, g, index], held[1, g, index]
            value = a.astype(jnp.float32) * mine + b.astype(jnp.float32) * theirs
            mixed[g, index] = value.astype(jnp.bfloat16)
            return 0

        return step

    sums, moves = {}, {}
    for g in range(2):
        swaps[g].wait_recv()
        lax.fori_loop(0, SIDE * 2, mix(g), 0, unroll=4)
        sums[g] = []
        for r, (place, which) in enumerate(along):
            target = place[0] * 2 + place[1] // 2
            sums[g].append(pltpu.make_async_remote_copy(
                src_ref=mixed.at[g, target], dst_ref=parts.at[g, slot],
                send_sem=chan_send.at[g * 7 + r], recv_sem=chan_recv.at[g * 7 + r],
                device_id=device_at(place, which), device_id_type=MESH))
        for copy in sums[g]:
            copy.start()

    def to_bands(g):
        for copy in sums[g]:
            copy.wait_recv()
        parts[g, slot] = mixed[g, slot]
        value = parts[g, 0].astype(jnp.float32)
        for k in range(1, SIDE * 2):
            value = value + parts[g, k].astype(jnp.float32)
        share[g] = value.astype(jnp.bfloat16).reshape(2 * SIDE, 2 * BINS, lanes)
        moves[g] = []
        for r, (place, which) in enumerate(across):
            moves[g].append(pltpu.make_async_remote_copy(
                src_ref=share.at[g, place[1] % 2 * SIDE + place[2]], dst_ref=bands.at[g, band],
                send_sem=band_send.at[g * 7 + r], recv_sem=band_recv.at[g * 7 + r],
                device_id=device_at(place, which), device_id_type=MESH))
        for copy in moves[g]:
            copy.start()
        bands[g, band] = share[g, band]

    def select():
        tall = (2 * SIDE * lanes, SRC_BLOCK)
        source = lax.broadcasted_iota(jnp.int32, tall, 0) // W
        goal = (source + SRC_BLOCK - offset[0]) % SRC_BLOCK
        picks[...] = jnp.where(goal == lax.broadcasted_iota(jnp.int32, tall, 1), 1.0, 0.0).astype(jnp.bfloat16)

    def arrange(g):
        for copy in moves[g]:
            copy.wait_recv()
        wide = (2 * BINS * W, lanes)
        same = lax.broadcasted_iota(jnp.int32, wide, 1) % W == lax.broadcasted_iota(jnp.int32, wide, 0) % W
        spaced = []
        for b in range(2 * SIDE):
            part = bands[g, b].astype(jnp.float32)
            part = jnp.broadcast_to(part[:, None, :], (2 * BINS, W, lanes)).reshape(wide)
            spaced.append(jnp.where(same, part, 0.0).astype(jnp.bfloat16))
        value = jnp.dot(jnp.concatenate(spaced, axis=1), picks[...], preferred_element_type=jnp.float32)
        spectra[at[0], at[1] // 2, at[1] % 2, at[2], g * wide[0]:(g + 1) * wide[0], :] = value.astype(jnp.bfloat16)

    copies = {}

    def send(key, ref, axis, step):
        index = len(copies)
        copies[key] = pltpu.make_async_remote_copy(
            src_ref=ref, dst_ref=ref, send_sem=send_sem.at[index], recv_sem=recv_sem.at[index],
            device_id=neighbour(axis, step), device_id_type=MESH)
        copies[key].start()

    def shifted(order, line, step):
        moved = list(at)
        for axis, by in ((order[1], LINES[line]), (order[2], step)):
            moved[axis] = lax.rem(at[axis] + by + SIDE, SIDE)
        return moved

    def begin(turn, stage):
        for part, (first, count, order) in enumerate(PARTS[turn]):
            ref = slots(spectra, at, order[:stage], turn * 256 + first, count)
            for kind, step in enumerate((1, -1, 2)):
                send((turn, stage, part, kind), ref, order[stage], step)

    def finish(turn, stage):
        for part in range(3):
            for kind in range(3):
                copies[turn, stage, part, kind].wait_recv()

    def send_line(turn, line):
        for part, (first, count, order) in enumerate(PARTS[turn]):
            if line:
                copies[turn, 1, part, line - 1].wait_recv()
            ref = slots(spectra, shifted(order, line, 0), order[:1], turn * 256 + first, count)
            for kind, step in enumerate((1, -1)):
                send((turn, 2, part, kind, line), ref, order[2], step)

    def forward(turn, line):
        for part, (first, count, order) in enumerate(PARTS[turn]):
            low = (count // 32 + (count // 16) % 2 * (line % 2)) * 16
            shares = ((1, -1, 0, low), (-1, 1, low, count - low))
            for kind, (step, origin, skip, rows_sent) in enumerate(shares):
                copies[turn, 2, part, kind, line].wait_recv()
                ref = slots(spectra, shifted(order, line, origin), order[:1], turn * 256 + first + skip, rows_sent)
                send((turn, 2, part, kind + 2, line), ref, order[2], step)

    def finish_lines(turn):
        for line in range(len(LINES)):
            for part in range(3):
                for kind in (2, 3):
                    copies[turn, 2, part, kind, line].wait_recv()

    def multiply(turn, place=lambda index: index):
        def step(index, _):
            k = place(index)
            s = spectra[k // 16, k // 8 % 2, k // 4 % 2, k % 4, turn * 256:(turn + 1) * 256, :]
            right = jnp.concatenate([s, jnp.concatenate([-s[R2:], s[:R2]], axis=0)], axis=1)
            result = jnp.dot(left[turn, k], right, preferred_element_type=jnp.float32)
            base = pl.multiple_of(k * 16, 16)
            for c in range(2 * channels):
                both = result[c * BINS:(c + 1) * BINS]
                both = jnp.concatenate([both[:, :SRC_BLOCK], both[:, SRC_BLOCK:]], axis=0)
                cross[pl.ds(base, 16), c * SRC_BLOCK:(c + 1) * SRC_BLOCK] = both.astype(jnp.bfloat16)
            return 0

        return step

    def near(digit):
        return digit + digit // 2

    def shift(dx, dy, dz):
        x, y, z = [lax.rem(a + b, SIDE) for a, b in zip(at, (dx, dy, dz))]
        return x * 16 + y * 4 + z

    group = 8
    width = group * SRC_BLOCK

    def sum_lags(turn, core_index, n, store):
        both = slice(core_index * columns + n * width, core_index * columns + (n + 1) * width)
        value = jnp.dot(table[:, turn * 1024:(turn + 1) * 1024], cross[:, both], preferred_element_type=jnp.float32)
        for i in range(group):
            store(n * group + i, core_index * channels + n * group + i, value[:, i * SRC_BLOCK:(i + 1) * SRC_BLOCK])

    def keep(c, held_c, value):
        total[held_c] = value

    def hand_over(c, held_c, value):
        outgoing[c] = ((total[held_c] + value) * FACTOR).astype(jnp.bfloat16)

    def conclude(c, held_c, value):
        total[held_c] = total[held_c] + value

    pairs = SLOTS // 2
    lax.fori_loop(8, SLOTS, spread(0), 0, unroll=4)
    select()
    lax.fori_loop(0, 40, spread(1), 0, unroll=4)
    to_bands(0)
    lax.fori_loop(40, 52, spread(1), 0, unroll=4)
    to_bands(1)
    lax.fori_loop(52, 60, spread(1), 0, unroll=4)
    arrange(0)
    begin(0, 0)
    arrange(1)
    begin(1, 0)
    lax.fori_loop(60, SLOTS, spread(1), 0, unroll=4)
    finish(0, 0)
    begin(0, 1)
    send_line(0, 0)
    finish(1, 0)
    begin(1, 1)
    for line in (1, 2, 3):
        send_line(0, line)
    forward(0, 0)
    forward(0, 1)
    send_line(1, 0)
    forward(0, 2)
    forward(0, 3)
    for line in (1, 2, 3):
        send_line(1, line)
    own_table.wait()
    forward(1, 0)
    finish_lines(0)
    quarter = SLOTS // 4
    for line in range(4):
        lax.fori_loop(line * quarter, (line + 1) * quarter, multiply(0), 0, unroll=4)
        if line < 3:
            forward(1, line + 1)
    for core_index in range(2):
        for n in range(channels // group):
            sum_lags(0, core_index, n, keep)
    lax.fori_loop(0, 27, multiply(1, lambda i: shift(near(i // 9), near(i // 3 % 3), near(i % 3))), 0, unroll=3)
    finish_lines(1)
    lax.fori_loop(0, 16, multiply(1, lambda i: shift(2, i // 4, i % 4)), 0, unroll=4)
    lax.fori_loop(0, 12, multiply(1, lambda i: shift(near(i // 4), 2, i % 4)), 0, unroll=4)
    lax.fori_loop(0, 9, multiply(1, lambda i: shift(near(i // 3), near(i % 3), 2)), 0, unroll=3)
    exchanges = []
    for n in range(channels // group):
        sum_lags(1, 1, n, hand_over)
        some = pl.ds(n * group, group)
        exchange = pltpu.make_async_remote_copy(
            src_ref=outgoing.at[some], dst_ref=incoming.at[some], send_sem=side_send.at[2 + n],
            recv_sem=side_recv.at[2 + n], device_id=sibling, device_id_type=MESH)
        exchange.start()
        exchanges.append(exchange)
    for n in range(channels // group):
        sum_lags(1, 0, n, conclude)

    unit = identity(SRC_BLOCK)
    last = (((1,), (1,)), ((), ()))
    for c in range(channels):
        if c % group == 0:
            exchanges[c // group].wait_recv()
        value = (total[c] * FACTOR + incoming[c].astype(jnp.float32)).astype(jnp.bfloat16)
        value = lax.dot_general(unit, value, last, preferred_element_type=jnp.float32)
        for half in range(2):
            turned[half, pl.ds(c, SRC_BLOCK, stride=channels), :] = value[:, half * R2:(half + 1) * R2]

    def pack(index):
        picked = pl.ds(pl.multiple_of(index * 256, 256), 256)
        both = jnp.concatenate([turned[0, picked, :], turned[1, picked, :]], axis=1).astype(jnp.bfloat16)
        return both.reshape(-1, channels, LAGS)

    ships = []
    for r, (place, which) in enumerate(across):
        index = place[1] % 2 * SIDE + place[2]
        shipped[index] = pack(index)
        ship = pltpu.make_async_remote_copy(
            src_ref=shipped.at[index], dst_ref=landed.at[:, band], send_sem=ship_send.at[r], recv_sem=ship_recv.at[r],
            device_id=device_at(place, which), device_id_type=MESH)
        ship.start()
        ships.append(ship)
    shipped[band] = pack(band)
    kept = pltpu.make_async_copy(shipped.at[band], landed.at[:, band], local_sem.at[0])
    kept.start()
    for ship in ships:
        ship.wait_recv()

    kept.wait()
    for copy in swaps + exchanges + sums[0] + sums[1] + moves[0] + moves[1] + ships + list(copies.values()):
        copy.wait_send()


def identity(n):
    diagonal = lax.broadcasted_iota(jnp.int32, (n, n), 0) == lax.broadcasted_iota(jnp.int32, (n, n), 1)
    return jnp.where(diagonal, 1.0, 0.0).astype(jnp.bfloat16)


def turn_kernel(landed, out):
    for s in range(out.shape[0]):
        out[s] = landed[s].astype(jnp.float32).T.astype(out.dtype)


def body(strain, source_block, source_offset, window_valid):
    channels = strain.shape[0]
    lanes = channels * W
    columns = channels * SRC_BLOCK
    tiles = strain.reshape(channels // BINS, BINS, -1, R2).transpose(0, 2, 1, 3).reshape(-1, R2)
    copies = ROUNDS * 3 * (3 + 3 + 4 * len(LINES))
    anywhere = pl.BlockSpec(memory_space=pl.ANY)
    scalars = pl.BlockSpec(memory_space=pltpu.SMEM)
    dma = pltpu.SemaphoreType.DMA
    bf16, f32 = jnp.bfloat16, jnp.float32
    landed = pl.pallas_call(
        kernel,
        in_specs=[anywhere] * 4 + [scalars] * 3,
        out_specs=anywhere,
        out_shape=jax.ShapeDtypeStruct((SRC_BLOCK // (2 * SIDE), 2 * SIDE, channels, LAGS), bf16),
        scratch_shapes=[
            pltpu.VMEM(tiles.shape, f32),
            pltpu.VMEM((3 * R1, R2), f32),
            pltpu.VMEM((R2, 2 * R2), bf16),
            pltpu.VMEM((LAGS, NF), bf16),
            pltpu.VMEM((3, 2, SIDE * 2, R2, lanes), bf16),
            pltpu.VMEM((2, SIDE * 2, R2, lanes), bf16),
            pltpu.VMEM((2, SIDE * 2, R2, lanes), bf16),
            pltpu.VMEM((2, SIDE * 2, 2 * BINS, lanes), bf16),
            pltpu.VMEM((2, SIDE * 2, 2 * BINS, lanes), bf16),
            pltpu.VMEM((SIDE, 2, 2, SIDE, PIECE, SRC_BLOCK), bf16),
            pltpu.VMEM((2, SLOTS, 256, 256), bf16),
            pltpu.VMEM((NF // 2, 2 * columns), bf16),
            pltpu.VMEM((2 * channels, LAGS, SRC_BLOCK), f32),
            pltpu.VMEM((channels, LAGS, SRC_BLOCK), bf16),
            pltpu.VMEM((channels, LAGS, SRC_BLOCK), bf16),
            pltpu.VMEM((2, columns, R2), f32),
            pltpu.VMEM((2 * SIDE, SRC_BLOCK // (2 * SIDE), channels, LAGS), bf16),
            pltpu.VMEM((2 * SIDE * lanes, SRC_BLOCK), bf16),
            dma((4,)), dma((copies,)), dma((copies,)), dma((4,)), dma((4,)),
            dma((14,)), dma((14,)), dma((14,)), dma((14,)), dma((7,)), dma((7,)),
        ],
        compiler_params=pltpu.CompilerParams(
            vmem_limit_bytes=62 * 2**20, collective_id=1, has_side_effects=True),
        cost_estimate=pl.CostEstimate(flops=4 * 256 * 4096 * 2048, bytes_accessed=20 * 2**20, transcendentals=0),
    )(tiles, jnp.asarray(row_tables()), jnp.asarray(short_dft(), dtype=bf16),
      jnp.asarray(lag_table(), dtype=bf16), source_block, source_offset, window_valid)
    sources, steps = SRC_BLOCK // (2 * SIDE), 2
    rows = 2 * SIDE * channels
    return pl.pallas_call(
        turn_kernel,
        grid=(steps,),
        in_specs=[pl.BlockSpec((sources // steps, rows, LAGS), lambda i: (i, 0, 0))],
        out_specs=pl.BlockSpec((sources // steps, LAGS, rows), lambda i: (i, 0, 0)),
        out_shape=jax.ShapeDtypeStruct((sources, LAGS, rows), bf16),
    )(landed.reshape(sources, rows, LAGS))


def solution(mesh):
    in_specs = (P(("chan", "band"), None), P(), P(), P())
    out_specs = P("band", None, "chan")
    return jax.shard_map(body, mesh=mesh, in_specs=in_specs, out_specs=out_specs, check_vma=False)
```

```python
import functools
import math

import jax
import jax.numpy as jnp
import numpy as np
from jax import lax
from jax.experimental import pallas as pl
from jax.experimental.pallas import tpu as pltpu
from jax.sharding import PartitionSpec as P

L = 4096
HOP = 2048
NF = 2048
W = 16
SRC_BLOCK = 128
LAGS = 256
R1 = 32
R2 = 128
HALF = R2 // 2
BINS = 8
FACTOR = 1.0 / (W * math.sqrt(NF))


def window_table():
    points = np.arange(L, dtype=np.float32)
    angle = (points * np.float32(2.0 * math.pi / L)).astype(np.float32)
    return (np.float32(0.5) - np.float32(0.5) * np.cos(angle)).astype(np.float32).reshape(R1, R2)


def row_tables():
    angle = 2.0 * np.pi * np.outer(np.arange(R1), np.arange(R2)) / L
    return np.concatenate([window_table(), np.cos(angle), -np.sin(angle)], axis=0).astype(np.float32)


def short_dft():
    angle = 2.0 * np.pi * (np.outer(np.arange(HALF), np.arange(R2)) % R2) / R2
    cosine, sine = np.cos(angle), np.sin(angle)
    top = np.concatenate([cosine, sine], axis=1)
    low = np.concatenate([-sine, cosine], axis=1)
    both = np.stack([top.reshape(-1, BINS, 2 * R2), low.reshape(-1, BINS, 2 * R2)], axis=1)
    return both.reshape(R2, 2 * R2).astype(np.float32)


def lag_table():
    core, g, x, y_hi, y_lo, z, i = np.ix_(*[np.arange(n) for n in (2, 2, 4, 2, 2, 4, 8)])
    bins = 8 * x + 4 * y_hi + 2 * core + g + R1 * (32 * y_lo + 8 * z + i)
    lags = (np.arange(LAGS) - LAGS // 2).reshape((1, LAGS) + (1,) * 6)
    angle = 2.0 * np.pi * (lags * bins[:, None] % L) / L
    table = np.stack([np.cos(angle), -np.sin(angle)], axis=7)
    return table.reshape(2, LAGS, NF).astype(np.float32)


def real_dft(x):
    n = len(x)
    if n == 2:
        return [(x[0] + x[1], None), (x[0] - x[1], None)]
    even, odd = real_dft(x[0::2]), real_dft(x[1::2])
    out = [None] * (n // 2 + 1)
    for k in range(n // 4 + 1):
        er, ei = even[k]
        orr, oi = odd[k]
        if k == 0:
            out[0] = (er + orr, None)
            out[n // 2] = (er - orr, None)
            continue
        if 4 * k == n:
            out[k] = (er, -orr)
            continue
        c, s = math.cos(2 * math.pi * k / n), -math.sin(2 * math.pi * k / n)
        if oi is None:
            tr, ti = orr * c, orr * s
        else:
            tr, ti = orr * c - oi * s, orr * s + oi * c
        zi = ti if ei is None else ei + ti
        yi = -ti if ei is None else ei - ti
        out[k] = (er + tr, zi)
        out[n // 2 - k] = (er - tr, -yi)
    return out


SIDE = 4
SLOTS = SIDE ** 3
PIECE = 2 * 2 * BINS * W
PARTS = (((0, 96, (0, 1, 2)), (96, 80, (1, 2, 0)), (176, 80, (2, 0, 1))),
         ((0, 80, (0, 1, 2)), (80, 96, (1, 2, 0)), (176, 80, (2, 0, 1))))
LINES = (0, -1, 1, 2)
ROUNDS = 2
MESH = pl.DeviceIdType.MESH


def position():
    chan, band = lax.axis_index("chan"), lax.axis_index("band")
    return (chan // 4, chan // 2 % 2 * 2 + band // 4, band % 4), chan % 2


def device_at(at, core):
    x, y, z = at
    return (x * 4 + y // 2 * 2 + core, y % 2 * 4 + z)


def neighbour(axis, step):
    at, core = position()
    moved = list(at)
    moved[axis] = lax.rem(at[axis] + step + SIDE, SIDE)
    return device_at(moved, core)


def slots(ref, at, full, first, count):
    whole = slice(None)
    x = whole if 0 in full else at[0]
    y_hi, y_lo = (whole, whole) if 1 in full else (at[1] // 2, at[1] % 2)
    z = whole if 2 in full else at[2]
    return ref.at[x, y_hi, y_lo, z, pl.ds(first, count), :]


def partners(at, core):
    x, y, z = at
    side = lambda step: lax.rem(z + step, SIDE)
    along = [((lax.rem(x + dx, SIDE), y ^ (2 * dy), z), core) for dx in (2, 1, 3, 0) for dy in (1, 0)][:-1]
    across = [((x, y ^ dy, side(dz)), core) for dz in (2, 1, 3, 0) for dy in (1, 0)][:-1]
    return along, across, [((x, y ^ 3, z), core), (at, 1 - core)]


def kernel(strain_hbm, rows_hbm, dft_hbm, tables, block, offset, valid, landed,
           strain, rows, dft, table, held, mixed, parts, share, bands, spectra, left, cross, total,
           outgoing, incoming, turned, shipped, picks,
           local_sem, send_sem, recv_sem, side_send, side_recv, chan_send, chan_recv, band_send, band_recv,
           ship_send, ship_recv):
    at, core = position()
    chan, band = lax.axis_index("chan"), lax.axis_index("band")
    sibling = device_at(at, 1 - core)
    lanes = held.shape[-1]
    channels = lanes // W
    columns = channels * SRC_BLOCK
    along, across, rest = partners(at, core)

    def fetch(src, dst, index):
        copy = pltpu.make_async_copy(src, dst, local_sem.at[index])
        copy.start()
        return copy

    fetched = [fetch(strain_hbm, strain, 0), fetch(rows_hbm, rows, 1), fetch(dft_hbm, dft, 2)]
    own_table = fetch(tables.at[core], table, 3)
    barrier = pltpu.get_barrier_semaphore()
    for place, which in along + across + rest:
        pl.semaphore_signal(barrier, inc=1, device_id=device_at(place, which), device_id_type=MESH)
    for copy in fetched:
        copy.wait()

    folded = left.at[0]

    def fold(c, _):
        first = c // BINS * (BINS * (W + 1) * W) + c % BINS
        x = [strain[pl.ds(first + BINS * k, W, stride=BINS * W), :] for k in range(R1)]
        whole = x[0]
        for k in range(1, R1):
            whole = whole + x[k]
        mean = jnp.sum(whole, axis=1, keepdims=True) * (1.0 / L)
        x = [((x[k] - mean) * rows[k:k + 1, :]).astype(jnp.bfloat16).astype(jnp.float32) for k in range(R1)]
        bins = real_dft(x)
        to = pl.ds(pl.multiple_of(c * W, W), W)
        for f in range(R1):
            re, im = bins[f] if f <= R1 // 2 else bins[R1 - f]
            cosine, sine = rows[R1 + f:R1 + f + 1, :], rows[2 * R1 + f:2 * R1 + f + 1, :]
            if im is None:
                gr, gi = re * cosine, re * sine
            else:
                im = im if f <= R1 // 2 else -im
                gr, gi = re * cosine - im * sine, re * sine + im * cosine
            folded[f, to, :R2] = gr.astype(jnp.bfloat16)
            folded[f, to, R2:] = gi.astype(jnp.bfloat16)
        return 0

    lax.fori_loop(0, channels, fold, 0, unroll=2)
    dft_table = dft[...]

    def transform(f, power):
        y = lax.dot_general(dft_table, folded[f], (((1,), (1,)), ((), ())), preferred_element_type=jnp.float32)
        total[f, :R2, :] = y[:, :R2]
        total[f, R2:, :] = y[:, R2:]
        square = (y * y).reshape(HALF // BINS, 2, BINS, lanes)
        return power + (square[:, 0] + square[:, 1]).reshape(HALF, lanes)

    power = lax.fori_loop(0, R1, transform, jnp.zeros((HALF, lanes), jnp.float32), unroll=8)
    scales = []
    for b in range(HALF // BINS):
        mean = jnp.sum(power[b * BINS:(b + 1) * BINS], axis=0, keepdims=True) * (1.0 / 256.0)
        scales.append(jnp.broadcast_to(lax.rsqrt(mean + 1e-06), (2 * BINS, lanes)))
    scale = jnp.concatenate(scales, axis=0)

    def finish_white(to, which, g):
        def step(index, _):
            f = index * 4 + which * 2 + g
            y = jnp.concatenate([total[f, :R2, :], total[f, R2:, :]], axis=1)
            held[to, g, index] = (y * scale).astype(jnp.bfloat16)
            return 0

        lax.fori_loop(0, SIDE * 2, step, 0, unroll=4)

    for g in range(2):
        finish_white(2, 1 - core, g)
    pl.semaphore_wait(barrier, len(along) + len(across) + len(rest))
    swaps = []
    for g in range(2):
        swap = pltpu.make_async_remote_copy(
            src_ref=held.at[2, g], dst_ref=held.at[1, g], send_sem=side_send.at[g], recv_sem=side_recv.at[g],
            device_id=sibling, device_id_type=MESH)
        swap.start()
        swaps.append(swap)
    for g in range(2):
        finish_white(0, core, g)

    row = lax.broadcasted_iota(jnp.int32, (2 * BINS, R2), 0) % BINS
    lane = lax.broadcasted_iota(jnp.int32, (2 * BINS, R2), 1)
    own = lane // W == row

    def spread(core_index):
        def step(index, _):
            x, y_hi, y_lo, z = index // 16, index // 8 % 2, index // 4 % 2, index % 4
            picked = pl.ds(pl.multiple_of((y_lo * SIDE + z) * 16, 16), 16)
            for g in range(2):
                for k in range(channels // 8):
                    value = held[core_index, g, x * 2 + y_hi, picked, k * R2:(k + 1) * R2].astype(jnp.float32)
                    for ri in range(2):
                        even = pltpu.roll(value[ri * BINS:(ri + 1) * BINS], 0, 1, stride=W, stride_axis=0)
                        both = jnp.concatenate([even, pltpu.roll(even, R2 - W, 1)], axis=0).astype(jnp.bfloat16)
                        for t in range(4):
                            moved = pltpu.roll(both, R2 - 2 * W * t, 1) if t else both
                            first = ((core_index * channels // 8 + k) * 4 + t) * 2 * BINS
                            left[g, index, first:first + 2 * BINS, ri * R2:(ri + 1) * R2] = jnp.where(
                                own, moved, jnp.zeros_like(moved))
            return 0

        return step

    lax.fori_loop(0, 8, spread(0), 0, unroll=4)

    spot = lax.broadcasted_iota(jnp.int32, (1, lanes), 1)
    source = band * channels + spot // W
    stacked = jnp.zeros((1, lanes), jnp.float32)
    for w in range(W):
        stacked = jnp.where(spot % W == w, jnp.where(valid[w] != 0, 1.0, 0.0), stacked)
    chans = R1 // 2

    def chosen(which):
        first = jnp.where(which == block[0], 1, 0)
        second = jnp.where(which == lax.rem(block[0] + 1, chans), 1, 0)
        taken = jnp.where(source >= offset[0], first, second)
        return jnp.where(taken == 1, stacked, 0.0)

    mine, theirs = chosen(chan), chosen(chan ^ 1)
    slot = chan // 2

    def mix(g):
        def step(index, _):
            a, b = held[0, g, index], held[1, g, index]
            value = a.astype(jnp.float32) * mine + b.astype(jnp.float32) * theirs
            mixed[g, index] = value.astype(jnp.bfloat16)
            return 0

        return step

    sums, moves = {}, {}
    for g in range(2):
        swaps[g].wait_recv()
        lax.fori_loop(0, SIDE * 2, mix(g), 0, unroll=4)
        sums[g] = []
        for r, (place, which) in enumerate(along):
            target = place[0] * 2 + place[1] // 2
            sums[g].append(pltpu.make_async_remote_copy(
                src_ref=mixed.at[g, target], dst_ref=parts.at[g, slot],
                send_sem=chan_send.at[g * 7 + r], recv_sem=chan_recv.at[g * 7 + r],
                device_id=device_at(place, which), device_id_type=MESH))
        for copy in sums[g]:
            copy.start()

    def to_bands(g):
        for copy in sums[g]:
            copy.wait_recv()
        parts[g, slot] = mixed[g, slot]
        value = parts[g, 0].astype(jnp.float32)
        for k in range(1, SIDE * 2):
            value = value + parts[g, k].astype(jnp.float32)
        share[g] = value.astype(jnp.bfloat16).reshape(2 * SIDE, 2 * BINS, lanes)
        moves[g] = []
        for r, (place, which) in enumerate(across):
            moves[g].append(pltpu.make_async_remote_copy(
                src_ref=share.at[g, place[1] % 2 * SIDE + place[2]], dst_ref=bands.at[g, band],
                send_sem=band_send.at[g * 7 + r], recv_sem=band_recv.at[g * 7 + r],
                device_id=device_at(place, which), device_id_type=MESH))
        for copy in moves[g]:
            copy.start()
        bands[g, band] = share[g, band]

    def select():
        tall = (2 * SIDE * lanes, SRC_BLOCK)
        source = lax.broadcasted_iota(jnp.int32, tall, 0) // W
        goal = (source + SRC_BLOCK - offset[0]) % SRC_BLOCK
        picks[...] = jnp.where(goal == lax.broadcasted_iota(jnp.int32, tall, 1), 1.0, 0.0).astype(jnp.bfloat16)

    def arrange(g):
        for copy in moves[g]:
            copy.wait_recv()
        wide = (2 * BINS * W, lanes)
        same = lax.broadcasted_iota(jnp.int32, wide, 1) % W == lax.broadcasted_iota(jnp.int32, wide, 0) % W
        spaced = []
        for b in range(2 * SIDE):
            part = bands[g, b].astype(jnp.float32)
            part = jnp.broadcast_to(part[:, None, :], (2 * BINS, W, lanes)).reshape(wide)
            spaced.append(jnp.where(same, part, 0.0).astype(jnp.bfloat16))
        value = jnp.dot(jnp.concatenate(spaced, axis=1), picks[...], preferred_element_type=jnp.float32)
        spectra[at[0], at[1] // 2, at[1] % 2, at[2], g * wide[0]:(g + 1) * wide[0], :] = value.astype(jnp.bfloat16)

    copies = {}

    def send(key, ref, axis, step):
        index = len(copies)
        copies[key] = pltpu.make_async_remote_copy(
            src_ref=ref, dst_ref=ref, send_sem=send_sem.at[index], recv_sem=recv_sem.at[index],
            device_id=neighbour(axis, step), device_id_type=MESH)
        copies[key].start()

    def shifted(order, line, step):
        moved = list(at)
        for axis, by in ((order[1], LINES[line]), (order[2], step)):
            moved[axis] = lax.rem(at[axis] + by + SIDE, SIDE)
        return moved

    def begin(turn, stage):
        for part, (first, count, order) in enumerate(PARTS[turn]):
            ref = slots(spectra, at, order[:stage], turn * 256 + first, count)
            for kind, step in enumerate((1, -1, 2)):
                send((turn, stage, part, kind), ref, order[stage], step)

    def finish(turn, stage):
        for part in range(3):
            for kind in range(3):
                copies[turn, stage, part, kind].wait_recv()

    def send_line(turn, line):
        for part, (first, count, order) in enumerate(PARTS[turn]):
            if line:
                copies[turn, 1, part, line - 1].wait_recv()
            ref = slots(spectra, shifted(order, line, 0), order[:1], turn * 256 + first, count)
            for kind, step in enumerate((1, -1)):
                send((turn, 2, part, kind, line), ref, order[2], step)

    def forward(turn, line):
        for part, (first, count, order) in enumerate(PARTS[turn]):
            low = (count // 32 + (count // 16) % 2 * (line % 2)) * 16
            shares = ((1, -1, 0, low), (-1, 1, low, count - low))
            for kind, (step, origin, skip, rows_sent) in enumerate(shares):
                copies[turn, 2, part, kind, line].wait_recv()
                ref = slots(spectra, shifted(order, line, origin), order[:1], turn * 256 + first + skip, rows_sent)
                send((turn, 2, part, kind + 2, line), ref, order[2], step)

    def finish_lines(turn):
        for line in range(len(LINES)):
            for part in range(3):
                for kind in (2, 3):
                    copies[turn, 2, part, kind, line].wait_recv()

    def multiply(turn, place=lambda index: index):
        def step(index, _):
            k = place(index)
            s = spectra[k // 16, k // 8 % 2, k // 4 % 2, k % 4, turn * 256:(turn + 1) * 256, :]
            right = jnp.concatenate([s, jnp.concatenate([-s[R2:], s[:R2]], axis=0)], axis=1)
            result = jnp.dot(left[turn, k], right, preferred_element_type=jnp.float32)
            base = pl.multiple_of(k * 16, 16)
            for c in range(2 * channels):
                both = result[c * BINS:(c + 1) * BINS]
                both = jnp.concatenate([both[:, :SRC_BLOCK], both[:, SRC_BLOCK:]], axis=0)
                cross[pl.ds(base, 16), c * SRC_BLOCK:(c + 1) * SRC_BLOCK] = both.astype(jnp.bfloat16)
            return 0

        return step

    def near(digit):
        return digit + digit // 2

    def shift(dx, dy, dz):
        x, y, z = [lax.rem(a + b, SIDE) for a, b in zip(at, (dx, dy, dz))]
        return x * 16 + y * 4 + z

    group = 8
    width = group * SRC_BLOCK

    def sum_lags(turn, core_index, n, store):
        both = slice(core_index * columns + n * width, core_index * columns + (n + 1) * width)
        value = jnp.dot(table[:, turn * 1024:(turn + 1) * 1024], cross[:, both], preferred_element_type=jnp.float32)
        for i in range(group):
            store(n * group + i, core_index * channels + n * group + i, value[:, i * SRC_BLOCK:(i + 1) * SRC_BLOCK])

    def keep(c, held_c, value):
        total[held_c] = value

    def hand_over(c, held_c, value):
        outgoing[c] = ((total[held_c] + value) * FACTOR).astype(jnp.bfloat16)

    def conclude(c, held_c, value):
        total[held_c] = total[held_c] + value

    pairs = SLOTS // 2
    lax.fori_loop(8, SLOTS, spread(0), 0, unroll=4)
    select()
    lax.fori_loop(0, 40, spread(1), 0, unroll=4)
    to_bands(0)
    lax.fori_loop(40, 52, spread(1), 0, unroll=4)
    to_bands(1)
    lax.fori_loop(52, 60, spread(1), 0, unroll=4)
    arrange(0)
    begin(0, 0)
    arrange(1)
    begin(1, 0)
    lax.fori_loop(60, SLOTS, spread(1), 0, unroll=4)
    finish(0, 0)
    begin(0, 1)
    send_line(0, 0)
    finish(1, 0)
    begin(1, 1)
    for line in (1, 2, 3):
        send_line(0, line)
    forward(0, 0)
    forward(0, 1)
    send_line(1, 0)
    forward(0, 2)
    forward(0, 3)
    for line in (1, 2, 3):
        send_line(1, line)
    own_table.wait()
    finish_lines(0)
    quarter = SLOTS // 4
    for line in range(4):
        lax.fori_loop(line * quarter, (line + 1) * quarter, multiply(0), 0, unroll=4)
        forward(1, line)
    for core_index in range(2):
        for n in range(channels // group):
            sum_lags(0, core_index, n, keep)
    lax.fori_loop(0, 27, multiply(1, lambda i: shift(near(i // 9), near(i // 3 % 3), near(i % 3))), 0, unroll=3)
    finish_lines(1)
    lax.fori_loop(0, 16, multiply(1, lambda i: shift(2, i // 4, i % 4)), 0, unroll=4)
    lax.fori_loop(0, 12, multiply(1, lambda i: shift(near(i // 4), 2, i % 4)), 0, unroll=4)
    lax.fori_loop(0, 9, multiply(1, lambda i: shift(near(i // 3), near(i % 3), 2)), 0, unroll=3)
    exchanges = []
    for n in range(channels // group):
        sum_lags(1, 1, n, hand_over)
        some = pl.ds(n * group, group)
        exchange = pltpu.make_async_remote_copy(
            src_ref=outgoing.at[some], dst_ref=incoming.at[some], send_sem=side_send.at[2 + n],
            recv_sem=side_recv.at[2 + n], device_id=sibling, device_id_type=MESH)
        exchange.start()
        exchanges.append(exchange)
    for n in range(channels // group):
        sum_lags(1, 0, n, conclude)

    unit = identity(SRC_BLOCK)
    last = (((1,), (1,)), ((), ()))
    for c in range(channels):
        if c % group == 0:
            exchanges[c // group].wait_recv()
        value = (total[c] * FACTOR + incoming[c].astype(jnp.float32)).astype(jnp.bfloat16)
        value = lax.dot_general(unit, value, last, preferred_element_type=jnp.float32)
        for half in range(2):
            turned[half, pl.ds(c, SRC_BLOCK, stride=channels), :] = value[:, half * R2:(half + 1) * R2]

    def pack(index):
        picked = pl.ds(pl.multiple_of(index * 256, 256), 256)
        both = jnp.concatenate([turned[0, picked, :], turned[1, picked, :]], axis=1).astype(jnp.bfloat16)
        return both.reshape(-1, channels, LAGS)

    ships = []
    for r, (place, which) in enumerate(across):
        index = place[1] % 2 * SIDE + place[2]
        shipped[index] = pack(index)
        ship = pltpu.make_async_remote_copy(
            src_ref=shipped.at[index], dst_ref=landed.at[:, band], send_sem=ship_send.at[r], recv_sem=ship_recv.at[r],
            device_id=device_at(place, which), device_id_type=MESH)
        ship.start()
        ships.append(ship)
    shipped[band] = pack(band)
    kept = pltpu.make_async_copy(shipped.at[band], landed.at[:, band], local_sem.at[0])
    kept.start()
    for ship in ships:
        ship.wait_recv()

    kept.wait()
    for copy in swaps + exchanges + sums[0] + sums[1] + moves[0] + moves[1] + ships + list(copies.values()):
        copy.wait_send()


def identity(n):
    diagonal = lax.broadcasted_iota(jnp.int32, (n, n), 0) == lax.broadcasted_iota(jnp.int32, (n, n), 1)
    return jnp.where(diagonal, 1.0, 0.0).astype(jnp.bfloat16)


def turn_kernel(landed, out):
    for s in range(out.shape[0]):
        out[s] = landed[s].astype(jnp.float32).T.astype(out.dtype)


def body(strain, source_block, source_offset, window_valid):
    channels = strain.shape[0]
    lanes = channels * W
    columns = channels * SRC_BLOCK
    tiles = strain.reshape(channels // BINS, BINS, -1, R2).transpose(0, 2, 1, 3).reshape(-1, R2)
    copies = ROUNDS * 3 * (3 + 3 + 4 * len(LINES))
    anywhere = pl.BlockSpec(memory_space=pl.ANY)
    scalars = pl.BlockSpec(memory_space=pltpu.SMEM)
    dma = pltpu.SemaphoreType.DMA
    bf16, f32 = jnp.bfloat16, jnp.float32
    landed = pl.pallas_call(
        kernel,
        in_specs=[anywhere] * 4 + [scalars] * 3,
        out_specs=anywhere,
        out_shape=jax.ShapeDtypeStruct((SRC_BLOCK // (2 * SIDE), 2 * SIDE, channels, LAGS), bf16),
        scratch_shapes=[
            pltpu.VMEM(tiles.shape, f32),
            pltpu.VMEM((3 * R1, R2), f32),
            pltpu.VMEM((R2, 2 * R2), bf16),
            pltpu.VMEM((LAGS, NF), bf16),
            pltpu.VMEM((3, 2, SIDE * 2, R2, lanes), bf16),
            pltpu.VMEM((2, SIDE * 2, R2, lanes), bf16),
            pltpu.VMEM((2, SIDE * 2, R2, lanes), bf16),
            pltpu.VMEM((2, SIDE * 2, 2 * BINS, lanes), bf16),
            pltpu.VMEM((2, SIDE * 2, 2 * BINS, lanes), bf16),
            pltpu.VMEM((SIDE, 2, 2, SIDE, PIECE, SRC_BLOCK), bf16),
            pltpu.VMEM((2, SLOTS, 256, 256), bf16),
            pltpu.VMEM((NF // 2, 2 * columns), bf16),
            pltpu.VMEM((2 * channels, LAGS, SRC_BLOCK), f32),
            pltpu.VMEM((channels, LAGS, SRC_BLOCK), bf16),
            pltpu.VMEM((channels, LAGS, SRC_BLOCK), bf16),
            pltpu.VMEM((2, columns, R2), f32),
            pltpu.VMEM((2 * SIDE, SRC_BLOCK // (2 * SIDE), channels, LAGS), bf16),
            pltpu.VMEM((2 * SIDE * lanes, SRC_BLOCK), bf16),
            dma((4,)), dma((copies,)), dma((copies,)), dma((4,)), dma((4,)),
            dma((14,)), dma((14,)), dma((14,)), dma((14,)), dma((7,)), dma((7,)),
        ],
        compiler_params=pltpu.CompilerParams(
            vmem_limit_bytes=62 * 2**20, collective_id=1, has_side_effects=True),
        cost_estimate=pl.CostEstimate(flops=4 * 256 * 4096 * 2048, bytes_accessed=20 * 2**20, transcendentals=0),
    )(tiles, jnp.asarray(row_tables()), jnp.asarray(short_dft(), dtype=bf16),
      jnp.asarray(lag_table(), dtype=bf16), source_block, source_offset, window_valid)
    sources, steps = SRC_BLOCK // (2 * SIDE), 2
    rows = 2 * SIDE * channels
    return pl.pallas_call(
        turn_kernel,
        grid=(steps,),
        in_specs=[pl.BlockSpec((sources // steps, rows, LAGS), lambda i: (i, 0, 0))],
        out_specs=pl.BlockSpec((sources // steps, LAGS, rows), lambda i: (i, 0, 0)),
        out_shape=jax.ShapeDtypeStruct((sources, LAGS, rows), bf16),
    )(landed.reshape(sources, rows, LAGS))


def solution(mesh):
    in_specs = (P(("chan", "band"), None), P(), P(), P())
    out_specs = P("band", None, "chan")
    return jax.shard_map(body, mesh=mesh, in_specs=in_specs, out_specs=out_specs, check_vma=False)
```
